32 devices in a mesh: dp: 8 (over z, core), ctx: 4 (over y, x).
Axes of the slice: x: 2, y: 2, z: 4, core: 2. Of those that a mesh axis runs over, the one named last changes fastest.
Arguments:
- tokens: bfloat16 [8192, 2048], P(('dp', 'ctx')), may hold values from -6 to 6
- w_query: bfloat16 [2048, 2048], P(('dp', 'ctx')), may hold values from -0.125 to 0.125
- w_key: bfloat16 [2048, 2048], P(('dp', 'ctx')), may hold values from -0.125 to 0.125
- w_value: bfloat16 [2048, 2048], P(('dp', 'ctx')), may hold values from -0.125 to 0.125
- w_out: bfloat16 [2048, 2048], P(('dp', 'ctx')), may hold values from -0.125 to 0.125
- gain_query: bfloat16 [2048], P(('dp', 'ctx')), may hold values from 0.099609375 to 1.8984375
- gain_key: bfloat16 [2048], P(('dp', 'ctx')), may hold values from 0.099609375 to 1.8984375
- gain_attn: bfloat16 [2048], P(('dp', 'ctx')), may hold values from 0.099609375 to 1.8984375
- w_gate: bfloat16 [2048, 8192], P(('dp', 'ctx')), may hold values from -0.125 to 0.125
- w_up: bfloat16 [2048, 8192], P(('dp', 'ctx')), may hold values from -0.125 to 0.125
- w_down: bfloat16 [8192, 2048], P(('dp', 'ctx')), may hold values from -0.0625 to 0.0625
- gain_ffn: bfloat16 [2048], P(('dp', 'ctx')), may hold values from 0.099609375 to 1.8984375
- positions: int32 [8192], replicated, may hold values from 0 to 1023, as said below
- image_starts: int32 [8, 2], replicated, may hold values from 0 to 768, as said below
- cotangent: bfloat16 [8192, 2048], P(('dp', 'ctx')), may hold values from -6 to 6
Outputs:
- output: bfloat16 [8192, 2048], P(('dp', 'ctx'))
- grad_input: float32 [8192, 2048], P(('dp', 'ctx'))
- grad_w_query: float32 [2048, 2048], P(('dp', 'ctx'))
- grad_w_key: float32 [2048, 2048], P(('dp', 'ctx'))
- grad_w_value: float32 [2048, 2048], P(('dp', 'ctx'))
- grad_w_out: float32 [2048, 2048], P(('dp', 'ctx'))
- grad_gain_query: float32 [2048], P(('dp', 'ctx'))
- grad_gain_key: float32 [2048], P(('dp', 'ctx'))
- grad_gain_attn: float32 [2048], P(('dp', 'ctx'))
- grad_w_gate: float32 [2048, 8192], P(('dp', 'ctx'))
- grad_w_up: float32 [2048, 8192], P(('dp', 'ctx'))
- grad_w_down: float32 [8192, 2048], P(('dp', 'ctx'))
- grad_gain_ffn: float32 [2048], P(('dp', 'ctx'))
The draws below stay inside these ranges and needn't reach their ends.
Inputs may be any that keep to these rules, and one draw needn't show every extreme that they name: Each sequence's 1024 rows hold every position once; consecutive groups of 256 rows hold two aligned blocks of 128 positions, block b and block 7 - b, in that order, each block within it in rising order; which b lands where is drawn per sequence. `image_starts`: piece j of a sequence lies inside the j-th of 2 equal parts of the sequence.
All inputs are finite; a program needn't handle non-finite values.
Results may differ from the reference program's by a relative error of at most 0.018.
Values may be sent and summed in bfloat16 or wider, within the bound.
A program may use at most 640 MiB of HBM per device.

```python
import math
import jax
import jax.numpy as jnp
from jax import lax

D = 2048
H = 16
HD = 128
FF = 8192
SEQ = 1024
IMG = 256
NIMG = 2
TOK_DEV = 256
SEQS = 8
TOKENS = 8192


def draw_positions(key, part):
    half_block = TOK_DEV // 2
    block_count = SEQ // half_block
    pair_count = block_count // 2
    seq_keys = jax.random.split(key, SEQS)

    def arrange(seq_key):
        shuffled = jax.random.permutation(seq_key, pair_count).astype(jnp.int32)
        paired = jnp.stack([shuffled, block_count - 1 - shuffled], axis=1).reshape(-1)
        inner = jnp.arange(half_block, dtype=jnp.int32)
        return (paired[:, None] * half_block + inner[None, :]).reshape(-1)
    return jax.vmap(arrange)(seq_keys).reshape(-1).astype(jnp.int32)


def draw_image_starts(key, part):
    region = SEQ // NIMG
    offsets = jax.random.randint(key, (SEQS, NIMG), 0, region - IMG + 1)
    return (jnp.arange(NIMG, dtype=jnp.int32)[None, :] * region + offsets).astype(jnp.int32)


def strengthened(drawn, key, source, target, blocks, factor):
    def block_of(axis_at):
        return (jnp.arange(drawn.shape[axis_at]) // (drawn.shape[axis_at] // blocks)).reshape((-1,) + (1,) * (drawn.ndim - 1 - axis_at))

    near = jax.random.permutation(key, blocks)[block_of(target)]
    other_side = (block_of(target) + blocks // 2) % blocks
    return jnp.where((block_of(source) == near) | (block_of(source) == other_side), factor * drawn, drawn)


def levels(key, dims, cuts, least, top_value):
    level, own = 1.0, jax.random.fold_in(key, 6)
    for axis_at, parts in cuts:
        heights = jnp.exp(jax.random.uniform(jax.random.fold_in(own, axis_at), (parts,), jnp.float32, least / len(cuts), top_value / len(cuts)))
        level = level * jnp.repeat(heights, dims[axis_at] // parts).reshape([-1 if axis == axis_at else 1 for axis in range(len(dims))])
    return level


def noise(rng, dims, scale, limit, cuts=(), kind=jnp.bfloat16):
    gain = levels(rng, dims, cuts, -0.22, 0.18) if cuts else 1.0
    entries = jax.random.normal(rng, dims, jnp.float32) * scale * gain
    return jnp.minimum(jnp.maximum(entries, -limit), limit).astype(kind)


def bell_draw_with(rng, extent, width, most, shards, heavy, kind=jnp.bfloat16):
    values = width * jax.random.normal(rng, extent, jnp.float32)
    if shards:
        values = values * levels(rng, extent, shards, -0.22, 0.18)
    return jnp.clip(strengthened(values, jax.random.fold_in(rng, 3), *heavy), -most, most).astype(kind)


def setup_inputs(seed: int = 0) -> dict:
    keys = jax.random.split(jax.random.key(seed), 16)
    tokens = bell_draw_with(keys[0], (TOKENS, D), 1.0, 6.0, ((0, 32),), (0, 1, 32, 2.75))
    w_query = noise(keys[1], (D, D), D ** -0.5, 0.125, ((0, 32),))
    w_key = noise(keys[2], (D, D), D ** -0.5, 0.125, ((0, 32),))
    w_value = noise(keys[3], (D, D), D ** -0.5, 0.125, ((0, 32),))
    w_out = noise(keys[4], (D, D), D ** -0.5, 0.125, ((0, 32),))
    gain_query = jnp.clip(1.0 + 0.18 * jax.random.normal(keys[5], (D,), jnp.float32), 0.099609375, 1.8984375).astype(jnp.bfloat16)
    gain_key = jnp.clip(1.0 + 0.18 * jax.random.normal(keys[6], (D,), jnp.float32), 0.099609375, 1.8984375).astype(jnp.bfloat16)
    gain_attn = jnp.clip(1.0 + 0.18 * jax.random.normal(keys[7], (D,), jnp.float32), 0.099609375, 1.8984375).astype(jnp.bfloat16)
    w_gate = noise(keys[8], (D, FF), D ** -0.5, 0.125, ((0, 32),))
    w_up = noise(keys[9], (D, FF), D ** -0.5, 0.125, ((0, 32),))
    w_down = noise(keys[10], (FF, D), FF ** -0.5, 0.0625, ((0, 32),))
    gain_ffn = jnp.clip(1.0 + 0.18 * jax.random.normal(keys[11], (D,), jnp.float32), 0.099609375, 1.8984375).astype(jnp.bfloat16)
    positions = draw_positions(jax.random.fold_in(keys[15], 71), 0)
    image_starts = draw_image_starts(jax.random.fold_in(keys[15], 71), 0)
    cotangent = noise(keys[14], (TOKENS, D), 1.0, 6.0, ((0, 32),))
    return dict(tokens=tokens, w_query=w_query, w_key=w_key, w_value=w_value, w_out=w_out, gain_query=gain_query, gain_key=gain_key, gain_attn=gain_attn, w_gate=w_gate, w_up=w_up, w_down=w_down, gain_ffn=gain_ffn, positions=positions, image_starts=image_starts, cotangent=cotangent)


EPS = 1e-06
THETA = 500000.0
NEG = -1e+30

@jax.custom_vjp
def low(v):
    return lax.optimization_barrier(v.astype(jnp.bfloat16)).astype(jnp.float32)

@jax.custom_vjp
def low_back(v):
    return v

def low_keep(v):
    return (low(v), None)

def low_pass(kept, grad):
    return (grad,)

def back_keep(v):
    return (v, None)

def back_low(kept, grad):
    return (low(grad),)
low.defvjp(low_keep, low_pass)
low_back.defvjp(back_keep, back_low)

def product(left, right):
    return jnp.dot(left, right, precision=lax.Precision.HIGHEST, preferred_element_type=jnp.float32)

def rms_norm(tensor, gain_row):
    return tensor * lax.rsqrt(lax.optimization_barrier(jnp.mean(tensor * tensor, axis=-1, keepdims=True)) + EPS) * gain_row

def turning(token_places):
    half_width = HD // 2
    frequency = THETA ** (-(jnp.arange(half_width, dtype=jnp.float32) * 2.0) / HD)
    angles = token_places.astype(jnp.float32)[:, None] * frequency[None, :]
    return (jnp.cos(angles)[:, None, :], jnp.sin(angles)[:, None, :])

def rotate(tensor, cosine_table, sine_table, direction_sign):
    row_count = tensor.shape[0]
    grouped = tensor.reshape(row_count, -1, HD)
    leading = grouped[..., :HD // 2]
    trailing = grouped[..., HD // 2:]
    turned = jnp.concatenate([leading * cosine_table - direction_sign * trailing * sine_table, trailing * cosine_table + direction_sign * leading * sine_table], axis=-1)
    return turned.reshape(row_count, -1)

def piece_label(token_places, starts_row):
    inside = (token_places[:, None] >= starts_row[None, :]) & (token_places[:, None] < starts_row[None, :] + IMG)
    labels = jnp.arange(1, starts_row.shape[0] + 1, dtype=jnp.int32)
    return lax.optimization_barrier(jnp.sum(jnp.where(inside, labels[None, :], 0), axis=1)).astype(jnp.int32) - 1

def visible(query_places, key_places, starts_row):
    query_label = piece_label(query_places, starts_row)
    key_label = piece_label(key_places, starts_row)
    causal = key_places[None, :] <= query_places[:, None]
    same_piece = (query_label[:, None] == key_label[None, :]) & (query_label[:, None] >= 0)
    return causal | same_piece

def layer(tokens, w_query, w_key, w_value, w_out, gain_query, gain_key, gain_attn, w_gate, w_up, w_down, gain_ffn, token_places, starts_row):
    seq_rows = tokens.shape[0]
    factor_scale = 1.0 / math.sqrt(HD)
    query_raw = low_back(product(tokens, w_query))
    key_raw = low_back(product(tokens, w_key))
    value_raw = low_back(product(tokens, w_value))
    cosine_table, sine_table = turning(token_places)
    query_turned = low(rotate(rms_norm(query_raw, gain_query), cosine_table, sine_table, 1.0))
    key_turned = low(rotate(rms_norm(key_raw, gain_key), cosine_table, sine_table, 1.0))
    value_low = low(value_raw)
    allowed = visible(token_places, token_places, starts_row)
    query_heads = query_turned.reshape(seq_rows, H, HD).transpose(1, 0, 2)
    key_heads = key_turned.reshape(seq_rows, H, HD).transpose(1, 0, 2)
    value_heads = value_low.reshape(seq_rows, H, HD).transpose(1, 0, 2)

    def one_head(triple):
        query_head, key_head, value_head = triple
        scores = low_back(product(query_head, key_head.T) * factor_scale)
        scores = jnp.where(allowed, scores, NEG)
        row_peak = lax.optimization_barrier(jnp.max(scores, axis=-1, keepdims=True))
        exponent = jnp.exp(scores - row_peak)
        softmax_weights = exponent / lax.optimization_barrier(jnp.sum(exponent, axis=-1, keepdims=True))
        return product(low(softmax_weights), value_head)
    attended = lax.map(jax.checkpoint(one_head), (query_heads, key_heads, value_heads))
    attended = attended.transpose(1, 0, 2).reshape(seq_rows, H * HD)
    attended = low(low_back(attended))
    attn_proj = low_back(product(attended, w_out))
    hidden = tokens + rms_norm(attn_proj, gain_attn)
    hidden_low = low(hidden)
    gate_pre = low_back(product(hidden_low, w_gate))
    up_pre = low_back(product(hidden_low, w_up))
    mixed_low = low(jax.nn.silu(gate_pre) * up_pre)
    ffn_proj = low_back(product(mixed_low, w_down))
    return hidden + rms_norm(ffn_proj, gain_ffn)

def reference(tokens, w_query, w_key, w_value, w_out, gain_query, gain_key, gain_attn, w_gate, w_up, w_down, gain_ffn, positions, image_starts, cotangent):
    weights = tuple((matrix.astype(jnp.float32) for matrix in (w_query, w_key, w_value, w_out, gain_query, gain_key, gain_attn, w_gate, w_up, w_down, gain_ffn)))
    token_rows = tokens.astype(jnp.float32).reshape(SEQS, SEQ, D)
    cot_rows = cotangent.astype(jnp.float32).reshape(SEQS, SEQ, D)
    place_rows = positions.reshape(SEQS, SEQ)

    def one_sequence(totals, sequence_item):
        seq_tokens, seq_cot, seq_places, seq_starts = sequence_item

        def forward(token_block, *weight_list):
            return layer(token_block, *weight_list, seq_places, seq_starts)
        result, pull = jax.vjp(forward, seq_tokens, *weights)
        grads = pull(seq_cot)
        totals = tuple((running + update for running, update in zip(totals, grads[1:])))
        return (totals, (result, grads[0]))
    start_totals = tuple((jnp.zeros_like(matrix) for matrix in weights))
    totals, (results, input_grads) = lax.scan(one_sequence, start_totals, (token_rows, cot_rows, place_rows, image_starts))
    return (results.reshape(TOKENS, D).astype(jnp.bfloat16), input_grads.reshape(TOKENS, D), totals[0], totals[1], totals[2], totals[3], totals[4], totals[5], totals[6], totals[7], totals[8], totals[9], totals[10])
```

```python
import functools
import math

import jax
import jax.numpy as jnp
from jax import lax
from jax.experimental import pallas as pl
from jax.experimental.pallas import tpu as pltpu
from jax.sharding import PartitionSpec as P

HD = 128
IMG = 256
EPS = 1e-06
THETA = 500000.0
NEG = -1e30
AXES = ("dp", "ctx")
F32 = jnp.float32
BF16 = jnp.bfloat16
SCALE = 1.0 / math.sqrt(HD)
LOG2E = math.log2(math.e)


def dot(left, right, left_dim, right_dim, kind=F32):
    return lax.dot_general(
        left, right, (((left_dim,), (right_dim,)), ((), ())), preferred_element_type=kind
    )


def probs_of(q, k, limit, places):
    scores = dot(q, k, 1, 1)
    scores = jnp.where(places <= limit, scores, NEG)
    peak = jnp.max(scores, axis=-1, keepdims=True)
    weights = jnp.exp2((scores - peak) * (SCALE * LOG2E))
    return weights * (1.0 / jnp.sum(weights, axis=-1, keepdims=True))


def attend_kernel(q_ref, k_ref, v_ref, limit_ref, place_ref, out_ref):
    probs = probs_of(q_ref[...], k_ref[...], limit_ref[...], place_ref[0])
    out_ref[...] = dot(probs.astype(BF16), v_ref[...], 1, 0).astype(BF16)


def attend_back_kernel(
    q_ref, k_ref, v_ref, g_ref, limit_ref, place_ref, dq_ref, dk_ref, dv_ref
):
    step = pl.program_id(2)

    @pl.when(step == 0)
    def _():
        dk_ref[...] = jnp.zeros_like(dk_ref)
        dv_ref[...] = jnp.zeros_like(dv_ref)

    q, k, v, g = q_ref[...], k_ref[...], v_ref[...], g_ref[...]
    probs = probs_of(q, k, limit_ref[...], place_ref[0])
    grad_probs = dot(g, v, 1, 1)
    inner = jnp.sum(probs * grad_probs, axis=-1, keepdims=True)
    grad_scores = (probs * (grad_probs - inner)).astype(BF16)
    dq_ref[...] = dot(grad_scores, k, 1, 0) * SCALE
    dk_ref[...] += dot(grad_scores, q, 0, 0) * SCALE
    dv_ref[...] += dot(probs.astype(BF16), g, 0, 0)


def attention_specs(seq_len, rows):
    steps = seq_len // rows
    query = pl.BlockSpec((rows, HD), lambda s, h, i: (s * steps + i, h))
    keys = pl.BlockSpec((seq_len, HD), lambda s, h, i: (s, h))
    limit = pl.BlockSpec((rows, 1), lambda s, h, i: (s * steps + i, 0))
    places = pl.BlockSpec((1, 1, seq_len), lambda s, h, i: (s, 0, 0))
    return query, keys, limit, places


def attend(q, k, v, limits, places, seq_len):
    rows = min(256, seq_len)
    total, width = q.shape
    query, keys, limit, place = attention_specs(seq_len, rows)
    return pl.pallas_call(
        attend_kernel,
        out_shape=jax.ShapeDtypeStruct((total, width), BF16),
        grid=(total // seq_len, width // HD, seq_len // rows),
        in_specs=[query, keys, keys, limit, place],
        out_specs=query,
        compiler_params=pltpu.CompilerParams(vmem_limit_bytes=48 * 2**20),
        cost_estimate=pl.CostEstimate(
            flops=4 * total * seq_len * width,
            bytes_accessed=8 * total * width,
            transcendentals=total * seq_len * (width // HD),
        ),
        name="attend",
    )(q, k, v, limits, places)


def attend_back(q, k, v, g, limits, places, seq_len):
    rows = min(256, seq_len)
    total, width = q.shape
    query, keys, limit, place = attention_specs(seq_len, rows)
    shape = jax.ShapeDtypeStruct((total, width), F32)
    return pl.pallas_call(
        attend_back_kernel,
        out_shape=(shape, shape, shape),
        grid=(total // seq_len, width // HD, seq_len // rows),
        in_specs=[query, keys, keys, query, limit, place],
        out_specs=(query, keys, keys),
        compiler_params=pltpu.CompilerParams(vmem_limit_bytes=48 * 2**20),
        cost_estimate=pl.CostEstimate(
            flops=10 * total * seq_len * width,
            bytes_accessed=20 * total * width,
            transcendentals=total * seq_len * (width // HD),
        ),
        name="attend_back",
    )(q, k, v, g, limits, places)


def rope_tables(places):
    half = HD // 2
    frequency = THETA ** (-(jnp.arange(half, dtype=F32) * 2.0) / HD)
    angles = places.astype(F32)[:, None] * frequency[None, :]
    return jnp.cos(angles)[:, None, :], jnp.sin(angles)[:, None, :]


def rotate(tensor, cosine, sine, sign):
    rows = tensor.shape[0]
    grouped = tensor.reshape(rows, -1, HD)
    low, high = grouped[..., : HD // 2], grouped[..., HD // 2 :]
    turned = jnp.concatenate(
        [low * cosine - sign * high * sine, high * cosine + sign * low * sine], axis=-1
    )
    return turned.reshape(rows, -1)


def row_norm(tensor):
    factor = lax.rsqrt(jnp.mean(tensor * tensor, axis=-1, keepdims=True) + EPS)
    return tensor * factor, factor


def row_norm_back(unit, factor, gain, incoming):
    weighted = incoming * gain
    inner = jnp.mean(weighted * unit, axis=-1, keepdims=True)
    return factor * (weighted - unit * inner), jnp.sum(incoming * unit, axis=0)


def layer(
    ctx_size,
    dp_size,
    tokens,
    w_query,
    w_key,
    w_value,
    w_out,
    gain_query,
    gain_key,
    gain_attn,
    w_gate,
    w_up,
    w_down,
    gain_ffn,
    positions,
    image_starts,
    cotangent,
):
    C, Z = ctx_size, dp_size // 2
    A = 2 * C
    N = Z * A
    ctx, dp = lax.axis_index("ctx"), lax.axis_index("dp")
    core, z = lax.rem(dp, 2), lax.div(dp, 2)
    plane_at = core * C + ctx
    own_at = dp * C + ctx
    rows, width = tokens.shape
    ffn_width = w_gate.shape[1]
    shard = w_query.shape[0]
    down_shard = w_down.shape[0]
    seq_len = rows * C
    slice_width = width // A
    ffn_slice = ffn_width // A
    bits = [1 << b for b in range(C.bit_length() - 1)]
    planes = [[zz * A + p for p in range(A)] for zz in range(Z)]

    def swap(x, bit):
        return lax.ppermute(x, AXES, [(i, i ^ bit) for i in range(N)])

    def swap_core(x):
        return swap(x, C)

    def ring(x):
        return lax.ppermute(x, AXES, [(i, (i + A) % N) for i in range(N)])

    def rows_of(x, at, count):
        return lax.dynamic_slice_in_dim(x, at, count, 0)

    def put(x, part, at):
        return lax.dynamic_update_slice_in_dim(x, part, at, 0)

    def gather_ctx(x):
        count = x.shape[0]
        half = count // 2
        whole = jnp.zeros((C * count,) + x.shape[1:], x.dtype)
        for number, order in enumerate((bits, bits[::-1])):
            pieces = [(0, x[number * half : (number + 1) * half])]
            for bit in order:
                pieces = pieces + [(mask ^ bit, swap(part, bit)) for mask, part in pieces]
            for mask, part in pieces:
                whole = put(whole, part, (ctx ^ mask) * count + number * half)
        return whole

    def gather_plane(x):
        own = gather_ctx(x)
        return own, swap_core(own)

    def scatter_ctx(x):
        count = x.shape[0] // C
        half = count // 2
        halves = []
        for number, order in enumerate((bits, bits[::-1])):
            held = {
                mask: rows_of(x, (ctx ^ mask) * count + number * half, half) for mask in range(C)
            }
            for bit in order[::-1]:
                arrived = {m ^ bit: swap(held[m].astype(BF16), bit) for m in held if m & bit}
                held = {m: held[m].astype(F32) + arrived[m].astype(F32) for m in arrived}
            halves.append(held[0])
        return jnp.concatenate(halves, axis=0)

    def scatter_plane(own, other):
        arrived = swap_core(other)
        return scatter_ctx((own.astype(F32) + arrived.astype(F32)).astype(BF16))

    def gather_z(x):
        count = x.shape[0]
        whole = jnp.zeros((Z * count,) + x.shape[1:], x.dtype)
        whole = put(whole, x, z * count)
        for step in range(1, Z):
            x = ring(x)
            whole = put(whole, x, lax.rem(z + Z - step, Z) * count)
        return whole

    def scatter_z(x):
        count = x.shape[0] // Z
        moving = rows_of(x, lax.rem(z + Z - 1, Z) * count, count)
        for step in range(1, Z):
            arrived = ring(moving.astype(BF16)).astype(F32)
            moving = arrived + rows_of(x, lax.rem(z + 2 * Z - 1 - step, Z) * count, count).astype(F32)
        return moving

    def exchange(x):
        return lax.all_to_all(x, AXES, 0, 0, tiled=True, axis_index_groups=planes)

    def sum_everywhere(x):
        for power in range(N.bit_length() - 1):
            x = x + swap(x, 1 << power)
        return x

    def sum_plane(own, other):
        stats = jnp.stack([own, other])
        for bit in bits:
            stats = stats + swap(stats, bit)
        stats = stats + swap_core(stats)[::-1]
        return stats[0], stats[1]

    def sorted_cores(own, other):
        return jnp.where(core == 0, jnp.stack([own, other]), jnp.stack([other, own]))

    qkv = jnp.stack(
        [w.reshape(shard, A, slice_width) for w in (w_query, w_key, w_value)], axis=1
    ).transpose(2, 0, 1, 3)
    qkv = exchange(qkv.reshape(A * shard, 3 * slice_width))
    full_qkv = gather_z(qkv)
    part = down_shard
    gate_up = jnp.stack([w.reshape(shard, Z, A, part) for w in (w_gate, w_up)], axis=1)
    gate_up = exchange(gate_up.transpose(3, 0, 1, 2, 4).reshape(A * shard, 2 * ffn_slice))

    gains = jnp.stack([gain_query, gain_key, gain_attn, gain_ffn]).astype(F32)
    all_gains = sum_everywhere(
        lax.dynamic_update_slice(jnp.zeros((4, width), F32), gains, (0, own_at * shard))
    )
    head_gains = lax.dynamic_slice(all_gains, (0, plane_at * slice_width), (2, slice_width))
    gain_q, gain_k = head_gains[0:1], head_gains[1:2]
    gain_a, gain_f = all_gains[2:3], all_gains[3:4]

    out_own, out_other = gather_plane(gather_z(w_out))
    full_out = (
        sorted_cores(out_own, out_other)
        .reshape(2, C, Z, shard, width)
        .transpose(2, 0, 1, 3, 4)
        .reshape(width, width)
    )
    full_gate_up = gather_z(gate_up)
    full_down = gather_z(w_down)

    x_own, x_other = gather_plane(tokens)
    x_all = jnp.concatenate([x_own, x_other], axis=0)
    other_dp = dp + 1 - 2 * core
    places = jnp.concatenate(
        [rows_of(positions, dp * seq_len, seq_len), rows_of(positions, other_dp * seq_len, seq_len)]
    )
    starts = jnp.concatenate([rows_of(image_starts, dp, 1), rows_of(image_starts, other_dp, 1)])
    start_rows = jnp.repeat(starts, seq_len, axis=0)
    inside = (places[:, None] >= start_rows) & (places[:, None] < start_rows + IMG)
    limits = jnp.max(jnp.where(inside, start_rows + (IMG - 1), places[:, None]), axis=1)
    limit_column = limits[:, None]
    place_rows = places.reshape(2, 1, seq_len)
    cosine, sine = rope_tables(places)

    def project(x):
        raw = dot(x, full_qkv, 1, 0)
        return raw, jnp.stack(
            [
                jnp.sum(jnp.square(raw[:, i * slice_width : (i + 1) * slice_width]), axis=1)
                for i in range(2)
            ]
        )

    raw_own, squares_own = project(x_own)
    raw_other, squares_other = project(x_other)
    squares_own, squares_other = sum_plane(squares_own, squares_other)
    raw = jnp.concatenate([raw_own, raw_other], axis=0)
    factors = lax.rsqrt(jnp.concatenate([squares_own, squares_other], axis=1) / width + EPS)
    factor_q, factor_k = factors[0][:, None], factors[1][:, None]
    unit_q = raw[:, :slice_width] * factor_q
    unit_k = raw[:, slice_width : 2 * slice_width] * factor_k
    value = raw[:, 2 * slice_width :].astype(BF16)
    query_turned = rotate(unit_q * gain_q, cosine, sine, 1.0).astype(BF16)
    key_turned = rotate(unit_k * gain_k, cosine, sine, 1.0).astype(BF16)
    attended = attend(query_turned, key_turned, value, limit_column, place_rows, seq_len)
    by_core = sorted_cores(attended[:seq_len], attended[seq_len:])
    attended_own = (
        exchange(by_core.reshape(A * rows, slice_width))
        .reshape(A, rows, slice_width)
        .transpose(1, 0, 2)
        .reshape(rows, width)
    )
    attn_proj = dot(attended_own, full_out, 1, 0)
    attn_unit, attn_factor = row_norm(attn_proj)
    hidden = tokens.astype(F32) + attn_unit * gain_a

    h_own, h_other = gather_plane(hidden.astype(BF16))
    h_all = jnp.concatenate([h_own, h_other], axis=0)

    def mix(h):
        pre = dot(h, full_gate_up, 1, 0)
        gate, up = pre[:, :ffn_slice], pre[:, ffn_slice:]
        return gate, up, (gate * jax.nn.sigmoid(gate) * up).astype(BF16)

    gate_other, up_other, mixed_other = mix(h_other)
    gate_own, up_own, mixed_own = mix(h_own)
    ffn_other = dot(mixed_other, full_down, 1, 0, BF16)
    ffn_own = dot(mixed_own, full_down, 1, 0, BF16)
    ffn_proj = scatter_plane(ffn_own, ffn_other)
    ffn_unit, ffn_factor = row_norm(ffn_proj)
    output = (hidden + ffn_unit * gain_f).astype(BF16)

    grad_out = cotangent.astype(F32)
    grad_ffn, term_gain_ffn = row_norm_back(ffn_unit, ffn_factor, gain_f, grad_out)
    f_own, f_other = gather_plane(grad_ffn.astype(BF16))
    f_all = jnp.concatenate([f_own, f_other], axis=0)
    mixed_all = jnp.concatenate([mixed_own, mixed_other], axis=0)
    grad_w_down = scatter_z(dot(mixed_all, f_all, 0, 0, BF16))

    def mix_back(f, gate, up):
        grad_mixed = dot(f, full_down, 1, 1)
        sig = jax.nn.sigmoid(gate)
        grad_gate = grad_mixed * up * sig * (1.0 + gate * (1.0 - sig))
        return jnp.concatenate([grad_gate.astype(BF16), (grad_mixed * (gate * sig)).astype(BF16)], axis=1)

    b_other = mix_back(f_other, gate_other, up_other)
    b_own = mix_back(f_own, gate_own, up_own)
    back_other = dot(b_other, full_gate_up, 1, 1, BF16)
    back_own = dot(b_own, full_gate_up, 1, 1, BF16)
    b_all = jnp.concatenate([b_own, b_other], axis=0)
    grad_gate_up = scatter_z(dot(h_all, b_all, 0, 0, BF16)).astype(BF16)
    grad_gate_up = (
        exchange(grad_gate_up)
        .reshape(A, shard, 2, Z, part)
        .transpose(2, 1, 3, 0, 4)
        .reshape(2, shard, ffn_width)
        .astype(F32)
    )
    grad_hidden = grad_out + scatter_plane(back_own, back_other)

    grad_attn, term_gain_attn = row_norm_back(attn_unit, attn_factor, gain_a, grad_hidden)
    grad_attn = grad_attn.astype(BF16)
    grad_attended = dot(grad_attn, full_out, 1, 1, BF16)
    grad_attended = exchange(
        grad_attended.reshape(rows, A, slice_width).transpose(1, 0, 2).reshape(A * rows, slice_width)
    ).reshape(2, seq_len, slice_width)
    grad_attended = jnp.where(core == 0, grad_attended, grad_attended[::-1]).reshape(
        2 * seq_len, slice_width
    )
    term_out = dot(attended_own, grad_attn, 0, 0, BF16)
    term_out = (
        term_out.reshape(Z, 2, C, shard, width)
        .transpose(1, 2, 0, 3, 4)
        .reshape(2, C * Z * shard, width)
    )
    term_out = jnp.where(core == 0, term_out, term_out[::-1])
    grad_w_out = scatter_z(scatter_plane(term_out[0], term_out[1]).astype(BF16))

    grad_q, grad_k, grad_v = attend_back(
        query_turned, key_turned, value, grad_attended, limit_column, place_rows, seq_len
    )
    grad_q = rotate(grad_q, cosine, sine, -1.0)
    grad_k = rotate(grad_k, cosine, sine, -1.0)
    term_gain_q = jnp.sum(grad_q * unit_q, axis=0)
    term_gain_k = jnp.sum(grad_k * unit_k, axis=0)
    weighted_q, weighted_k = grad_q * gain_q, grad_k * gain_k
    inner = jnp.stack([jnp.sum(weighted_q * unit_q, axis=1), jnp.sum(weighted_k * unit_k, axis=1)])
    inner_own, inner_other = sum_plane(inner[:, :seq_len], inner[:, seq_len:])
    inner = jnp.concatenate([inner_own, inner_other], axis=1) / width
    grad_raw = jnp.concatenate(
        [
            (factor_q * (weighted_q - unit_q * inner[0][:, None])).astype(BF16),
            (factor_k * (weighted_k - unit_k * inner[1][:, None])).astype(BF16),
            grad_v.astype(BF16),
        ],
        axis=1,
    )
    input_other = dot(grad_raw[seq_len:], full_qkv, 1, 1, BF16)
    input_own = dot(grad_raw[:seq_len], full_qkv, 1, 1, BF16)
    grad_input = grad_hidden + scatter_plane(input_own, input_other)
    grad_qkv = scatter_z(dot(x_all, grad_raw, 0, 0, BF16)).astype(BF16)
    grad_qkv = (
        exchange(grad_qkv)
        .reshape(A, shard, 3, slice_width)
        .transpose(2, 1, 0, 3)
        .reshape(3, shard, width)
        .astype(F32)
    )

    head_terms = lax.dynamic_update_slice(
        jnp.zeros((2, width), F32), jnp.stack([term_gain_q, term_gain_k]), (0, plane_at * slice_width)
    )
    gain_terms = jnp.concatenate([head_terms, term_gain_attn[None], term_gain_ffn[None]], axis=0)
    gain_sums = lax.dynamic_slice(sum_everywhere(gain_terms), (0, own_at * shard), (4, shard))

    return (
        output,
        grad_input,
        grad_qkv[0],
        grad_qkv[1],
        grad_qkv[2],
        grad_w_out,
        gain_sums[0],
        gain_sums[1],
        gain_sums[2],
        grad_gate_up[0],
        grad_gate_up[1],
        grad_w_down,
        gain_sums[3],
    )


def solution(mesh):
    split, line, copied = P(AXES, None), P(AXES), P()
    return jax.shard_map(
        functools.partial(layer, mesh.shape["ctx"], mesh.shape["dp"]),
        mesh=mesh,
        in_specs=(split,) * 5 + (line,) * 3 + (split,) * 3 + (line, copied, copied, split),
        out_specs=(split,) * 6 + (line,) * 3 + (split,) * 3 + (line,),
        check_vma=False,
    )
```

```python
import functools
import math

import jax
import jax.numpy as jnp
from jax import lax
from jax.experimental import pallas as pl
from jax.experimental.pallas import tpu as pltpu
from jax.sharding import PartitionSpec as P

HD = 128
IMG = 256
EPS = 1e-06
THETA = 500000.0
NEG = -1e30
AXES = ("dp", "ctx")
F32 = jnp.float32
BF16 = jnp.bfloat16
SCALE = 1.0 / math.sqrt(HD)
LOG2E = math.log2(math.e)


def dot(left, right, left_dim, right_dim, kind=F32):
    return lax.dot_general(
        left, right, (((left_dim,), (right_dim,)), ((), ())), preferred_element_type=kind
    )


def probs_of(q, k, limit, places):
    scores = dot(q, k, 1, 1)
    scores = jnp.where(places <= limit, scores, NEG)
    peak = jnp.max(scores, axis=-1, keepdims=True)
    weights = jnp.exp2((scores - peak) * (SCALE * LOG2E))
    return weights * (1.0 / jnp.sum(weights, axis=-1, keepdims=True))


def attend_kernel(q_ref, k_ref, v_ref, limit_ref, place_ref, out_ref):
    probs = probs_of(q_ref[...], k_ref[...], limit_ref[...], place_ref[0])
    out_ref[...] = dot(probs.astype(BF16), v_ref[...], 1, 0).astype(BF16)


def attend_back_kernel(
    q_ref, k_ref, v_ref, g_ref, limit_ref, place_ref, dq_ref, dk_ref, dv_ref
):
    step = pl.program_id(2)

    @pl.when(step == 0)
    def _():
        dk_ref[...] = jnp.zeros_like(dk_ref)
        dv_ref[...] = jnp.zeros_like(dv_ref)

    q, k, v, g = q_ref[...], k_ref[...], v_ref[...], g_ref[...]
    probs = probs_of(q, k, limit_ref[...], place_ref[0])
    grad_probs = dot(g, v, 1, 1)
    inner = jnp.sum(probs * grad_probs, axis=-1, keepdims=True)
    grad_scores = (probs * (grad_probs - inner)).astype(BF16)
    dq_ref[...] = dot(grad_scores, k, 1, 0) * SCALE
    dk_ref[...] += dot(grad_scores, q, 0, 0) * SCALE
    dv_ref[...] += dot(probs.astype(BF16), g, 0, 0)


def attention_specs(seq_len, rows):
    steps = seq_len // rows
    query = pl.BlockSpec((rows, HD), lambda s, h, i: (s * steps + i, h))
    keys = pl.BlockSpec((seq_len, HD), lambda s, h, i: (s, h))
    limit = pl.BlockSpec((rows, 1), lambda s, h, i: (s * steps + i, 0))
    places = pl.BlockSpec((1, 1, seq_len), lambda s, h, i: (s, 0, 0))
    return query, keys, limit, places


def attend(q, k, v, limits, places, seq_len):
    rows = min(256, seq_len)
    total, width = q.shape
    query, keys, limit, place = attention_specs(seq_len, rows)
    return pl.pallas_call(
        attend_kernel,
        out_shape=jax.ShapeDtypeStruct((total, width), BF16),
        grid=(total // seq_len, width // HD, seq_len // rows),
        in_specs=[query, keys, keys, limit, place],
        out_specs=query,
        compiler_params=pltpu.CompilerParams(vmem_limit_bytes=48 * 2**20),
        cost_estimate=pl.CostEstimate(
            flops=4 * total * seq_len * width,
            bytes_accessed=8 * total * width,
            transcendentals=total * seq_len * (width // HD),
        ),
        name="attend",
    )(q, k, v, limits, places)


def attend_back(q, k, v, g, limits, places, seq_len):
    rows = min(256, seq_len)
    total, width = q.shape
    query, keys, limit, place = attention_specs(seq_len, rows)
    shape = jax.ShapeDtypeStruct((total, width), F32)
    return pl.pallas_call(
        attend_back_kernel,
        out_shape=(shape, shape, shape),
        grid=(total // seq_len, width // HD, seq_len // rows),
        in_specs=[query, keys, keys, query, limit, place],
        out_specs=(query, keys, keys),
        compiler_params=pltpu.CompilerParams(vmem_limit_bytes=48 * 2**20),
        cost_estimate=pl.CostEstimate(
            flops=10 * total * seq_len * width,
            bytes_accessed=20 * total * width,
            transcendentals=total * seq_len * (width // HD),
        ),
        name="attend_back",
    )(q, k, v, g, limits, places)


MESH = pl.DeviceIdType.MESH
ANY = pl.BlockSpec(memory_space=pl.ANY)


def flipped(at, mask):
    bit = 1
    while bit <= mask:
        if mask & bit:
            at = at + bit - 2 * bit * lax.rem(lax.div(at, bit), 2)
        bit *= 2
    return at


def bit_orders(C):
    bits = [1 << b for b in range(C.bit_length() - 1)]
    return bits, bits[::-1]


def tree(order):
    found = [(0, order, 0)]
    for place, bit in enumerate(order):
        found += [(mask | bit, order[place + 1 :], bit) for mask, _, _ in list(found)]
    return found


def greet(peers):
    barrier = pltpu.get_barrier_semaphore()
    for peer in peers:
        pl.semaphore_signal(barrier, inc=1, device_id=peer, device_id_type=MESH)
    pl.semaphore_wait(barrier, len(peers))


def remote(src, dst, sent, arrived, device):
    return pltpu.make_async_remote_copy(
        src_ref=src, dst_ref=dst, send_sem=sent, recv_sem=arrived, device_id=device, device_id_type=MESH
    )


def places_of():
    dp, ctx = lax.axis_index("dp"), lax.axis_index("ctx")
    return dp, ctx, dp + 1 - 2 * lax.rem(dp, 2)


class Gather:
    def __init__(self, C, source, slot, over, from_over, sems):
        self.C = C
        self.source, self.slot, self.over, self.from_over = source, slot, over, from_over
        self.ctx_sent, self.ctx_came, self.core_sent, self.core_came = sems
        self.dp, self.ctx, self.twin = places_of()
        self.trees = [tree(order) for order in bit_orders(C)]
        self.sends = []

    def held(self, half, mask):
        return self.slot(flipped(self.ctx, mask), half) if mask else self.source(half)

    def by_ctx(self, half, mask, bit):
        return remote(
            self.held(half, mask),
            self.slot(flipped(self.ctx, mask), half),
            self.ctx_sent.at[half, mask | bit],
            self.ctx_came.at[half, mask | bit],
            (self.dp, flipped(self.ctx, bit)),
        )

    def by_core(self, half, mask):
        return remote(
            self.held(half, mask),
            self.over(flipped(self.ctx, mask), half),
            self.core_sent.at[half, mask],
            self.core_came.at[half, mask],
            (self.twin, self.ctx),
        )

    def landed(self, half, mask, bit):
        slot = self.slot(flipped(self.ctx, mask), half)
        remote(
            slot,
            slot,
            self.ctx_sent.at[half, mask],
            self.ctx_came.at[half, mask],
            (self.dp, flipped(self.ctx, bit)),
        ).wait_recv()

    def start(self, copy):
        copy.start()
        self.sends.append(copy)

    def step(self, index):
        for half in range(2):
            mask, onward, bit = self.trees[half][index]
            if mask:
                self.landed(half, mask, bit)
            for further in onward:
                self.start(self.by_ctx(half, mask, further))
            if mask:
                self.start(self.by_core(half, mask))
        if index == 0:
            for half in range(2):
                self.start(self.by_core(half, 0))

    def finish(self):
        for copy in self.sends:
            copy.wait_send()
        for half in range(2):
            for mask in range(self.C):
                slot = self.from_over(flipped(self.ctx, mask), half)
                remote(
                    slot,
                    slot,
                    self.core_sent.at[half, mask],
                    self.core_came.at[half, mask],
                    (self.twin, self.ctx),
                ).wait_recv()


def rows_gather(C, x_ref, out_ref, sems):
    count = x_ref.shape[0]
    size = count // 2

    def rows(seat, half):
        return pl.ds(seat * count + half * size, size)

    return Gather(
        C,
        lambda half: x_ref.at[pl.ds(half * size, size)],
        lambda seat, half: out_ref.at[0, rows(seat, half)],
        lambda seat, half: out_ref.at[1, rows(seat, half)],
        lambda seat, half: out_ref.at[1, rows(seat, half)],
        sems,
    )


class Spread:
    def __init__(self, C, Z, x_ref, out_ref, own_sem, ring_sent, ring_came, sems):
        dp, ctx, _ = places_of()
        core = lax.rem(dp, 2)
        self.Z, self.z, self.ctx = Z, lax.div(dp, 2), ctx
        self.ahead, self.behind = lax.rem(dp + 2, 2 * Z), lax.rem(dp + 2 * Z - 2, 2 * Z)
        self.out, self.place = out_ref, core * C + ctx
        self.ring_sent, self.ring_came = ring_sent, ring_came
        self.own = pltpu.make_async_copy(x_ref, out_ref.at[self.z, self.place], own_sem)
        size = Z // 2

        def slot(side, seat, half):
            return out_ref.at[pl.ds(half * size, size), side * C + seat]

        self.gather = Gather(
            C,
            lambda half: slot(core, ctx, half),
            lambda seat, half: slot(core, seat, half),
            lambda seat, half: slot(core, seat, half),
            lambda seat, half: slot(1 - core, seat, half),
            sems,
        )

    def hop(self, step):
        block = self.out.at[lax.rem(self.z + self.Z - step, self.Z), self.place]
        return remote(
            block, block, self.ring_sent.at[step], self.ring_came.at[step], (self.ahead, self.ctx)
        )

    def hop_landed(self, step):
        block = self.out.at[lax.rem(self.z + 2 * self.Z - 1 - step, self.Z), self.place]
        remote(
            block, block, self.ring_sent.at[step], self.ring_came.at[step], (self.behind, self.ctx)
        ).wait_recv()

    def finish(self):
        for step in range(self.Z - 1):
            self.hop(step).wait_send()
        self.gather.finish()


def gather_sems(C):
    return [pltpu.SemaphoreType.DMA((2, C))] * 4


def plane_neighbours(C):
    dp, ctx, twin = places_of()
    return [(dp, flipped(ctx, bit)) for bit in bit_orders(C)[0]] + [(twin, ctx)]


def comm_params(number, megabytes=16):
    return pltpu.CompilerParams(
        collective_id=number, has_side_effects=True, vmem_limit_bytes=megabytes * 2**20
    )


def cost_of(microseconds):
    return pl.CostEstimate(flops=int(microseconds * 1e6), bytes_accessed=1024, transcendentals=0)


def gather_kernel(C, x_ref, out_ref, own_sem, *sems):
    greet(plane_neighbours(C))
    count = x_ref.shape[0]
    own = pltpu.make_async_copy(
        x_ref, out_ref.at[0, pl.ds(lax.axis_index("ctx") * count, count)], own_sem
    )
    gather = rows_gather(C, x_ref, out_ref, sems)
    for index in range(C):
        gather.step(index)
        if index == 0:
            own.start()
    own.wait()
    gather.finish()


def gather_rows(x, C, number):
    return pl.pallas_call(
        functools.partial(gather_kernel, C),
        out_shape=jax.ShapeDtypeStruct((2, C * x.shape[0], x.shape[1]), x.dtype),
        in_specs=[ANY],
        out_specs=ANY,
        scratch_shapes=[pltpu.SemaphoreType.DMA] + gather_sems(C),
        compiler_params=comm_params(number),
        cost_estimate=cost_of(40),
        name="gather_rows",
    )(x)


def plane_peers(C):
    dp, ctx, twin = places_of()
    peers = [(there, flipped(ctx, mask)) for there in (dp, twin) for mask in range(C)]
    return list(enumerate(peers))[1:]


def place_in_plane(C, device):
    return lax.rem(device[0], 2) * C + device[1]


class Deal:
    def __init__(self, C, weights, wide, blocks, out_ref, row_at, sent, came, own_sem):
        self.C, self.out, self.wide, self.sems = C, out_ref, wide, (sent, came, own_sem)
        self.peers, self.row_at = plane_peers(C), row_at
        self.shard = weights[0].shape[0]
        dp, ctx, _ = places_of()
        self.parts = []
        for weight in weights:
            for block in range(blocks):
                self.parts.append((weight, block * 2 * C))
        self.own_device = (dp, ctx)
        self.copies = []

    def spot(self, device, number):
        rows = pl.ds(self.row_at(device), self.shard)
        return self.out.at[rows, pl.ds(number * self.wide, self.wide)]

    def start(self):
        sent, came, own_sem = self.sems
        for number, (weight, first) in enumerate(self.parts):
            for index, device in [(0, self.own_device)] + self.peers:
                at = (first + place_in_plane(self.C, device)) * self.wide
                source = weight.at[:, pl.ds(pl.multiple_of(at, 128), self.wide)]
                target = self.spot(self.own_device, number)
                if index == 0:
                    copy = pltpu.make_async_copy(source, target, own_sem.at[number])
                else:
                    copy = remote(
                        source, target, sent.at[number, index], came.at[number, index], device
                    )
                copy.start()
                self.copies.append((copy, index))

    def landed(self):
        sent, came, _ = self.sems
        for number in range(len(self.parts)):
            for index, device in self.peers:
                spot = self.spot(device, number)
                remote(
                    spot, spot, sent.at[number, index], came.at[number, index], device
                ).wait_recv()
        for copy, index in self.copies:
            if index:
                copy.wait_send()
            else:
                copy.wait()


def deal_sems(C, parts):
    return [
        pltpu.SemaphoreType.DMA((parts, 2 * C)),
        pltpu.SemaphoreType.DMA((parts, 2 * C)),
        pltpu.SemaphoreType.DMA((parts,)),
    ]


def first_kernel(C, Z, dealt, *refs):
    x_ref, wq_ref, wk_ref, wv_ref, wo_ref, gains_ref = refs[:6]
    refs = refs[6:]
    if dealt:
        (wg_ref, wu_ref), refs = refs[:2], refs[2:]
    x_out, w_out, wo_out, gains_out = refs[:4]
    refs = refs[4:]
    if dealt:
        gu_out, refs = refs[0], refs[1:]
    own_sem, gather_set, refs = refs[0], refs[1:5], refs[5:]
    deal_set, (ring_sent, ring_came), refs = refs[:3], refs[3:5], refs[5:]
    spread_sets, refs = (refs[:7], refs[7:14]), refs[14:]
    A = 2 * C
    dp, ctx, _ = places_of()
    z = lax.div(dp, 2)
    ahead, behind = lax.rem(dp + 2, 2 * Z), lax.rem(dp + 2 * Z - 2, 2 * Z)
    greet([device for _, device in plane_peers(C)] + [(ahead, ctx), (behind, ctx)])
    shard = wq_ref.shape[0]
    spreads = [
        Spread(C, Z, x, out, sems[0], sems[1], sems[2], sems[3:])
        for x, out, sems in ((gains_ref, gains_out, spread_sets[0]), (wo_ref, wo_out, spread_sets[1]))
    ]
    for spread in spreads:
        spread.own.start()
    deal = Deal(
        C, (wq_ref, wk_ref, wv_ref), wq_ref.shape[1] // A, 1, w_out,
        lambda device: (device[0] * C + device[1]) * shard, *deal_set,
    )
    deal.start()
    for spread in spreads:
        spread.own.wait()
        spread.hop(0).start()
    count = x_ref.shape[0]
    own = pltpu.make_async_copy(x_ref, x_out.at[0, pl.ds(ctx * count, count)], own_sem)
    own.start()
    gather = rows_gather(C, x_ref, x_out, gather_set)
    gather.step(0)

    def ring(step):
        block = w_out.at[pl.ds(lax.rem(z + Z - step, Z) * (A * shard), A * shard)]
        return remote(block, block, ring_sent.at[step], ring_came.at[step], (ahead, ctx))

    def ring_landed(step):
        block = w_out.at[pl.ds(lax.rem(z + 2 * Z - 1 - step, Z) * (A * shard), A * shard)]
        remote(block, block, ring_sent.at[step], ring_came.at[step], (behind, ctx)).wait_recv()

    deal.landed()
    ring(0).start()
    if dealt:
        columns = Deal(
            C, (wg_ref, wu_ref), wg_ref.shape[1] // (Z * A), Z, gu_out,
            lambda device: place_in_plane(C, device) * shard, *refs,
        )
        columns.start()
    for step in range(Z - 2):
        for spread in spreads:
            spread.hop_landed(step)
            spread.hop(step + 1).start()
        ring_landed(step)
        ring(step + 1).start()
        if step + 1 < C:
            gather.step(step + 1)
    for spread in spreads:
        spread.hop_landed(Z - 2)
    for index in range(Z - 1, C):
        gather.step(index)
    for index in range(C):
        for spread in spreads:
            spread.gather.step(index)
    if dealt:
        columns.landed()
    own.wait()
    gather.finish()
    for spread in spreads:
        spread.finish()
    ring_landed(Z - 2)
    for step in range(Z - 1):
        ring(step).wait_send()


def first_gather(x, w_query, w_key, w_value, w_out, gains, w_gate, w_up, dealt, C, Z, number):
    width = x.shape[1]
    A = 2 * C
    shard = w_query.shape[0]

    def shape(*sizes):
        return jax.ShapeDtypeStruct(sizes, x.dtype)

    outs = [
        shape(2, C * x.shape[0], width),
        shape(width, 3 * width // A),
        shape(Z, A, shard, width),
        shape(Z, A, *gains.shape),
    ]
    operands = [x, w_query, w_key, w_value, w_out, gains]
    spread = [
        pltpu.SemaphoreType.DMA,
        pltpu.SemaphoreType.DMA((Z,)),
        pltpu.SemaphoreType.DMA((Z,)),
    ] + gather_sems(C)
    scratch = (
        [pltpu.SemaphoreType.DMA]
        + gather_sems(C)
        + deal_sems(C, 3)
        + [pltpu.SemaphoreType.DMA((Z,))] * 2
        + spread * 2
    )
    if dealt:
        operands += [w_gate, w_up]
        outs.append(shape(A * shard, 2 * w_gate.shape[1] // A))
        scratch += deal_sems(C, 2 * Z)
    return pl.pallas_call(
        functools.partial(first_kernel, C, Z, dealt),
        out_shape=tuple(outs),
        in_specs=[ANY] * len(operands),
        out_specs=(ANY,) * len(outs),
        scratch_shapes=scratch,
        compiler_params=comm_params(number),
        cost_estimate=cost_of(100),
        name="first_gather",
    )(*operands)


ROWS = 256


def row_of_sums(values):
    high = values.astype(BF16)
    rest = (values - high.astype(F32)).astype(BF16)
    ones = jnp.ones((8, values.shape[1]), BF16)
    return dot(ones, high, 1, 1) + dot(ones, rest, 1, 1)


def pair_of_rows(first, second):
    return jnp.where(lax.broadcasted_iota(jnp.int32, first.shape, 0) == 0, first, second)


def columns_of(rows):
    eye = (
        lax.broadcasted_iota(jnp.int32, (8, 8), 0) == lax.broadcasted_iota(jnp.int32, (8, 8), 1)
    ).astype(BF16)
    high = rows.astype(BF16)
    rest = rows - high.astype(F32)
    middle = rest.astype(BF16)
    low = (rest - middle.astype(F32)).astype(BF16)
    return dot(high, eye, 0, 0) + dot(middle, eye, 0, 0) + dot(low, eye, 0, 0)


def start_sum(C, stats, landing, sent, came):
    for index, device in plane_peers(C):
        remote(stats, landing.at[index], sent.at[index], came.at[index], device).start()


def finish_sum(C, stats, landing, sent, came, total):
    blocks = stats.shape[0]
    for index, device in plane_peers(C):
        remote(stats, landing.at[index], sent.at[index], came.at[index], device).wait()
    for block in range(blocks):
        value = stats[block]
        for index in range(1, 2 * C):
            value = value + landing[index, block if index < C else (block + blocks // 2) % blocks]
        total[block] = value


def turned(value, cosine, sine):
    return value * cosine + pltpu.roll(value, HD // 2, 1) * sine


def project_kernel(
    C, x_ref, w_ref, gain_ref, cos_ref, sin_ref, rq_ref, rk_ref, v_ref, q_ref, k_ref, total,
    stats, landing, sent, came,
):
    greet([device for _, device in plane_peers(C)])
    wide = rq_ref.shape[1]
    width = x_ref.shape[1]
    blocks = stats.shape[0]

    def rows_at(block):
        return pl.ds(pl.multiple_of(block * ROWS, ROWS), ROWS)

    @pl.loop(0, blocks)
    def _(block):
        here = rows_at(block)
        raw = dot(x_ref[here, :], w_ref[...], 1, 0)
        query, key = raw[:, :wide], raw[:, wide : 2 * wide]
        rq_ref[here, :] = query
        rk_ref[here, :] = key
        v_ref[here, :] = raw[:, 2 * wide :].astype(BF16)
        stats[block] = pair_of_rows(row_of_sums(query * query), row_of_sums(key * key))

    start_sum(C, stats, landing, sent, came)
    finish_sum(C, stats, landing, sent, came, total)

    @pl.loop(0, blocks)
    def _(block):
        here = rows_at(block)
        factors = columns_of(lax.rsqrt(total[block] * (1.0 / width) + EPS))
        cosine, sine = cos_ref[here, :], sin_ref[here, :]
        for which, (raw, out) in enumerate(((rq_ref, q_ref), (rk_ref, k_ref))):
            factor = factors[:, which : which + 1]
            for head in range(wide // HD):
                lanes = slice(head * HD, (head + 1) * HD)
                value = raw[here, lanes] * factor * gain_ref[which : which + 1, lanes]
                out[here, lanes] = turned(value, cosine, sine).astype(BF16)


def plane_sum_scratch(C, blocks):
    return [
        pltpu.VMEM((blocks, 8, ROWS), F32),
        pltpu.VMEM((2 * C, blocks, 8, ROWS), F32),
        pltpu.SemaphoreType.DMA((2 * C,)),
        pltpu.SemaphoreType.DMA((2 * C,)),
    ]


VM = pl.BlockSpec(memory_space=pltpu.VMEM)


def project(x, w, gains, cosine, sine, C, number):
    total, width = x.shape
    wide = w.shape[1] // 3
    blocks = total // ROWS
    raw = jax.ShapeDtypeStruct((total, wide), F32)
    low = jax.ShapeDtypeStruct((total, wide), BF16)
    return pl.pallas_call(
        functools.partial(project_kernel, C),
        out_shape=(raw, raw, low, low, low, jax.ShapeDtypeStruct((blocks, 8, ROWS), F32)),
        in_specs=[VM] * 5,
        out_specs=(VM,) * 6,
        scratch_shapes=plane_sum_scratch(C, blocks),
        compiler_params=comm_params(number, 48),
        cost_estimate=cost_of(18),
        name="project",
    )(x, w, gains, cosine, sine)


def project_back_kernel(
    C, dq_ref, dk_ref, dv_ref, rq_ref, rk_ref, total, gain_ref, cos_ref, sin_ref,
    out_ref, term_ref, eq, ek, inner, stats, landing, sent, came,
):
    greet([device for _, device in plane_peers(C)])
    wide = rq_ref.shape[1]
    width = wide * 2 * C
    blocks = stats.shape[0]

    def rows_at(block):
        return pl.ds(pl.multiple_of(block * ROWS, ROWS), ROWS)

    def factors_of(block):
        return columns_of(lax.rsqrt(total[block] * (1.0 / width) + EPS))

    term_ref[...] = jnp.zeros_like(term_ref)

    @pl.loop(0, blocks)
    def _(block):
        here = rows_at(block)
        factors = factors_of(block)
        cosine, sine = cos_ref[here, :], sin_ref[here, :]
        sums = []
        for which, (grad, raw, kept) in enumerate(((dq_ref, rq_ref, eq), (dk_ref, rk_ref, ek))):
            for head in range(wide // HD):
                lanes = slice(head * HD, (head + 1) * HD)
                kept[here, lanes] = turned(grad[here, lanes], cosine, -sine)
            product = kept[here, :] * raw[here, :] * factors[:, which : which + 1]
            term_ref[which : which + 1, :] += jnp.sum(product, axis=0, keepdims=True)
            sums.append(row_of_sums(product * gain_ref[which : which + 1, :]))
        stats[block] = pair_of_rows(*sums)

    start_sum(C, stats, landing, sent, came)
    finish_sum(C, stats, landing, sent, came, inner)

    @pl.loop(0, blocks)
    def _(block):
        here = rows_at(block)
        factors = factors_of(block)
        means = columns_of(inner[block] * (1.0 / width))
        for which, (kept, raw) in enumerate(((eq, rq_ref), (ek, rk_ref))):
            factor, mean = factors[:, which : which + 1], means[:, which : which + 1]
            weighted = kept[here, :] * gain_ref[which : which + 1, :]
            value = factor * (weighted - raw[here, :] * factor * mean)
            out_ref[here, which * wide : (which + 1) * wide] = value.astype(BF16)
        out_ref[here, 2 * wide :] = dv_ref[here, :].astype(BF16)


def project_back(dq, dk, dv, raw_q, raw_k, sums, gains, cosine, sine, C, number):
    total, wide = dq.shape
    blocks = total // ROWS
    return pl.pallas_call(
        functools.partial(project_back_kernel, C),
        out_shape=(
            jax.ShapeDtypeStruct((total, 3 * wide), BF16),
            jax.ShapeDtypeStruct((8, wide), F32),
        ),
        in_specs=[VM] * 9,
        out_specs=(VM, VM),
        scratch_shapes=[
            pltpu.VMEM((total, wide), F32),
            pltpu.VMEM((total, wide), F32),
            pltpu.VMEM((blocks, 8, ROWS), F32),
        ]
        + plane_sum_scratch(C, blocks),
        compiler_params=comm_params(number, 48),
        cost_estimate=cost_of(15),
        name="project_back",
    )(dq, dk, dv, raw_q, raw_k, sums, gains, cosine, sine)


def return_kernel(C, groups, blocks, x_ref, *refs):
    outs, (landing, sent, came, own_sem) = refs[:groups], refs[groups:]
    A = 2 * C
    shard = outs[0].shape[0]
    part = outs[0].shape[1] // (blocks * A)
    dp, ctx, _ = places_of()
    own_at = place_in_plane(C, (dp, ctx))
    peers = plane_peers(C)
    greet([device for _, device in peers])
    own = pltpu.make_async_copy(
        x_ref.at[pl.ds(own_at * shard, shard)], landing.at[own_at], own_sem
    )
    own.start()

    def copy_to(index, device):
        rows = pl.ds(place_in_plane(C, device) * shard, shard)
        return remote(
            x_ref.at[rows], landing.at[own_at], sent.at[index], came.at[index], device
        )

    def landed(index, device):
        spot = landing.at[place_in_plane(C, device)]
        remote(spot, spot, sent.at[index], came.at[index], device).wait_recv()

    for index, device in peers:
        copy_to(index, device).start()
    own.wait()
    for index, device in peers:
        landed(index, device)
    for index, device in peers:
        copy_to(index, device).wait_send()
    for group in range(groups):
        for block in range(blocks):
            for at in range(A):
                lanes = (group * blocks + block) * part
                to = (block * A + at) * part
                outs[group][:, to : to + part] = landing[at, :, lanes : lanes + part]


def return_rows(x, C, groups, blocks, number):
    A = 2 * C
    shard = x.shape[0] // A
    width = x.shape[1] * A // groups
    return pl.pallas_call(
        functools.partial(return_kernel, C, groups, blocks),
        out_shape=(jax.ShapeDtypeStruct((shard, width), x.dtype),) * groups,
        in_specs=[ANY],
        out_specs=(VM,) * groups,
        scratch_shapes=[
            pltpu.VMEM((A, shard, x.shape[1]), x.dtype),
            pltpu.SemaphoreType.DMA((A,)),
            pltpu.SemaphoreType.DMA((A,)),
            pltpu.SemaphoreType.DMA,
        ],
        compiler_params=comm_params(number, 24),
        cost_estimate=cost_of(20),
        name="return_rows",
    )(x)


def scatter_kernel(
    C, own_ref, other_ref, out_ref, own, twin_part, landing,
    own_sem, core_sent, core_came, ctx_sent, ctx_came,
):
    count = out_ref.shape[0]
    half_rows = count // 2
    dp, ctx, twin = places_of()
    greet(plane_neighbours(C))
    trees = [tree(order)[::-1] for order in bit_orders(C)]

    def rows(half, mask):
        return pl.ds(flipped(ctx, mask) * count + half * half_rows, half_rows)

    def from_twin(half, mask):
        return remote(
            other_ref.at[rows(half, mask)],
            twin_part.at[rows(half, mask)],
            core_sent.at[half, mask],
            core_came.at[half, mask],
            (twin, ctx),
        )

    def local_copy(half, mask):
        return pltpu.make_async_copy(
            own_ref.at[rows(half, mask)], own.at[rows(half, mask)], own_sem.at[half, mask]
        )

    def onward(half, mask, bit):
        return remote(
            own.at[rows(half, mask)],
            landing.at[half, mask],
            ctx_sent.at[half, mask],
            ctx_came.at[half, mask],
            (dp, flipped(ctx, bit)),
        )

    for index in range(C):
        for half in range(2):
            mask = trees[half][index][0]
            local_copy(half, mask).start()
            from_twin(half, mask).start()
    for index in range(C):
        for half in range(2):
            mask, along, bit = trees[half][index]
            local_copy(half, mask).wait()
            from_twin(half, mask).wait_recv()
            here = rows(half, mask)
            total = own[here, :].astype(F32) + twin_part[here, :].astype(F32)
            for came in along:
                onward(half, mask | came, came).wait_recv()
                total = total + landing[half, mask | came].astype(F32)
            if mask:
                own[here, :] = total.astype(BF16)
                onward(half, mask, bit).start()
            else:
                out_ref[pl.ds(half * half_rows, half_rows), :] = total
    for half in range(2):
        for mask, _, bit in trees[half]:
            from_twin(half, mask).wait_send()
            if mask:
                onward(half, mask, bit).wait_send()


def scatter_rows(own, other, C, number):
    total, width = own.shape
    count = total // C
    return pl.pallas_call(
        functools.partial(scatter_kernel, C),
        out_shape=jax.ShapeDtypeStruct((count, width), F32),
        in_specs=[ANY, ANY],
        out_specs=pl.BlockSpec(memory_space=pltpu.VMEM),
        scratch_shapes=[
            pltpu.VMEM((total, width), BF16),
            pltpu.VMEM((total, width), BF16),
            pltpu.VMEM((2, C, count // 2, width), BF16),
        ]
        + [pltpu.SemaphoreType.DMA((2, C))] * 5,
        compiler_params=comm_params(number, 40),
        cost_estimate=cost_of(40),
        name="scatter_rows",
    )(own, other)


def rope_tables(places):
    half = HD // 2
    frequency = THETA ** (-(jnp.arange(half, dtype=F32) * 2.0) / HD)
    angles = places.astype(F32)[:, None] * frequency[None, :]
    cosine, sine = jnp.cos(angles), jnp.sin(angles)
    return jnp.concatenate([cosine, cosine], axis=1), jnp.concatenate([-sine, sine], axis=1)


def row_norm(tensor):
    factor = lax.rsqrt(jnp.mean(tensor * tensor, axis=-1, keepdims=True) + EPS)
    return tensor * factor, factor


def row_norm_back(unit, factor, gain, incoming):
    weighted = incoming * gain
    inner = jnp.mean(weighted * unit, axis=-1, keepdims=True)
    return factor * (weighted - unit * inner), jnp.sum(incoming * unit, axis=0)


def layer(
    ctx_size,
    dp_size,
    tokens,
    w_query,
    w_key,
    w_value,
    w_out,
    gain_query,
    gain_key,
    gain_attn,
    w_gate,
    w_up,
    w_down,
    gain_ffn,
    positions,
    image_starts,
    cotangent,
):
    C, Z = ctx_size, dp_size // 2
    A = 2 * C
    N = Z * A
    ctx, dp = lax.axis_index("ctx"), lax.axis_index("dp")
    core, z = lax.rem(dp, 2), lax.div(dp, 2)
    plane_at = core * C + ctx
    own_at = dp * C + ctx
    rows, width = tokens.shape
    ffn_width = w_gate.shape[1]
    shard = w_query.shape[0]
    down_shard = w_down.shape[0]
    seq_len = rows * C
    slice_width = width // A
    ffn_slice = ffn_width // A
    bits = [1 << b for b in range(C.bit_length() - 1)]
    planes = [[zz * A + p for p in range(A)] for zz in range(Z)]
    columns = [[zz * 2 + k for zz in range(Z)] for k in range(2)]

    def swap(x, bit):
        return lax.ppermute(x, AXES, [(i, i ^ bit) for i in range(N)])

    def swap_core(x):
        return swap(x, C)

    def ring(x):
        return lax.ppermute(x, AXES, [(i, (i + A) % N) for i in range(N)])

    def rows_of(x, at, count):
        return lax.dynamic_slice_in_dim(x, at, count, 0)

    def put(x, part, at):
        return lax.dynamic_update_slice_in_dim(x, part, at, 0)

    def gather_z_aside(x):
        return lax.all_gather(x, "dp", axis=0, tiled=True, axis_index_groups=columns)

    def scatter_z_aside(x):
        return lax.psum_scatter(
            x, "dp", scatter_dimension=0, tiled=True, axis_index_groups=columns
        )

    def exchange(x):
        return lax.all_to_all(x, AXES, 0, 0, tiled=True, axis_index_groups=planes)

    def sum_everywhere(x):
        for power in range(N.bit_length() - 1):
            x = x + swap(x, 1 << power)
        return x

    def sorted_cores(own, other):
        return jnp.where(core == 0, jnp.stack([own, other]), jnp.stack([other, own]))

    full_down = gather_z_aside(w_down)
    part = down_shard
    dealt = part % 128 == 0
    gains = jnp.stack([gain_query, gain_key, gain_attn, gain_ffn])
    gains = jnp.pad(gains, ((0, 12), (0, -shard % 128)))
    x_both, full_qkv, full_out, all_gains, *gate_up = first_gather(
        tokens, w_query, w_key, w_value, w_out, gains, w_gate, w_up, dealt, C, Z, 1
    )
    if dealt:
        gate_up = gate_up[0]
    else:
        gate_up = jnp.stack([w.reshape(shard, Z, A, part) for w in (w_gate, w_up)], axis=1)
        gate_up = exchange(gate_up.transpose(3, 0, 1, 2, 4).reshape(A * shard, 2 * ffn_slice))
    full_qkv, full_down, gate_up = lax.optimization_barrier((full_qkv, full_down, gate_up))
    full_gate_up = gather_z_aside(gate_up)
    full_out = full_out.reshape(width, width)
    all_gains = all_gains[:, :, :4, :shard].astype(F32).transpose(2, 0, 1, 3).reshape(4, width)
    head_gains = lax.dynamic_slice(all_gains, (0, plane_at * slice_width), (2, slice_width))
    head_gains = jnp.pad(head_gains, ((0, 6), (0, 0)))
    gain_a, gain_f = all_gains[2:3], all_gains[3:4]

    x_all = x_both.reshape(2 * seq_len, width)
    other_dp = dp + 1 - 2 * core
    places = jnp.concatenate(
        [rows_of(positions, dp * seq_len, seq_len), rows_of(positions, other_dp * seq_len, seq_len)]
    )
    starts = jnp.concatenate([rows_of(image_starts, dp, 1), rows_of(image_starts, other_dp, 1)])
    start_rows = jnp.repeat(starts, seq_len, axis=0)
    inside = (places[:, None] >= start_rows) & (places[:, None] < start_rows + IMG)
    limits = jnp.max(jnp.where(inside, start_rows + (IMG - 1), places[:, None]), axis=1)
    limit_column = limits[:, None]
    place_rows = places.reshape(2, 1, seq_len)
    cosine, sine = rope_tables(places)
    raw_q, raw_k, value, query_turned, key_turned, squares = project(
        x_all, full_qkv, head_gains, cosine, sine, C, 8
    )
    attended = attend(query_turned, key_turned, value, limit_column, place_rows, seq_len)
    by_core = sorted_cores(attended[:seq_len], attended[seq_len:])
    attended_own = (
        exchange(by_core.reshape(A * rows, slice_width))
        .reshape(A, rows, slice_width)
        .transpose(1, 0, 2)
        .reshape(rows, width)
    )
    attn_proj = dot(attended_own, full_out, 1, 0)
    attn_unit, attn_factor = row_norm(attn_proj)
    hidden = tokens.astype(F32) + attn_unit * gain_a

    h_both = gather_rows(hidden.astype(BF16), C, 2)
    h_own, h_other, h_all = h_both[0], h_both[1], h_both.reshape(2 * seq_len, width)

    def mix(h):
        pre = dot(h, full_gate_up, 1, 0)
        gate, up = pre[:, :ffn_slice], pre[:, ffn_slice:]
        return gate, up, (gate * jax.nn.sigmoid(gate) * up).astype(BF16)

    gate_other, up_other, mixed_other = mix(h_other)
    gate_own, up_own, mixed_own = mix(h_own)
    ffn_other = dot(mixed_other, full_down, 1, 0, BF16)
    ffn_own = dot(mixed_own, full_down, 1, 0, BF16)
    ffn_proj = scatter_rows(ffn_own, ffn_other, C, 4)
    ffn_unit, ffn_factor = row_norm(ffn_proj)
    output = (hidden + ffn_unit * gain_f).astype(BF16)

    grad_out = cotangent.astype(F32)
    grad_ffn, term_gain_ffn = row_norm_back(ffn_unit, ffn_factor, gain_f, grad_out)
    f_both = gather_rows(grad_ffn.astype(BF16), C, 3)
    f_own, f_other, f_all = f_both[0], f_both[1], f_both.reshape(2 * seq_len, width)
    mixed_all = jnp.concatenate([mixed_own, mixed_other], axis=0)
    term_down = dot(mixed_all, f_all, 0, 0, BF16)
    term_down, f_both = lax.optimization_barrier((term_down, f_both))
    f_own, f_other = f_both[0], f_both[1]
    grad_w_down = scatter_z_aside(term_down).astype(F32)

    def mix_back(f, gate, up):
        grad_mixed = dot(f, full_down, 1, 1)
        sig = jax.nn.sigmoid(gate)
        grad_gate = grad_mixed * up * sig * (1.0 + gate * (1.0 - sig))
        return jnp.concatenate([grad_gate.astype(BF16), (grad_mixed * (gate * sig)).astype(BF16)], axis=1)

    b_other = mix_back(f_other, gate_other, up_other)
    b_own = mix_back(f_own, gate_own, up_own)
    b_all = jnp.concatenate([b_own, b_other], axis=0)
    term_gate_up = dot(h_all, b_all, 0, 0, BF16)
    back_other = dot(b_other, full_gate_up, 1, 1, BF16)
    back_own = dot(b_own, full_gate_up, 1, 1, BF16)
    term_gate_up, back_own, back_other, grad_w_down = lax.optimization_barrier(
        (term_gate_up, back_own, back_other, grad_w_down)
    )
    grad_gate_up = scatter_z_aside(term_gate_up)
    grad_hidden = grad_out + scatter_rows(back_own, back_other, C, 5)

    grad_attn, term_gain_attn = row_norm_back(attn_unit, attn_factor, gain_a, grad_hidden)
    a_all = gather_rows(grad_attn.astype(BF16), C, 7).reshape(2 * seq_len, width)
    grad_attended = dot(
        a_all, rows_of(full_out, plane_at * slice_width, slice_width), 1, 1, BF16
    )
    term_out = dot(attended, a_all, 0, 0, BF16)
    grad_q, grad_k, grad_v = attend_back(
        query_turned, key_turned, value, grad_attended, limit_column, place_rows, seq_len
    )
    grad_raw, head_terms = project_back(
        grad_q, grad_k, grad_v, raw_q, raw_k, squares, head_gains, cosine, sine, C, 9
    )
    term_qkv = dot(x_all, grad_raw, 0, 0, BF16)
    last = jnp.concatenate(
        [term_qkv, term_out.reshape(width, slice_width)], axis=1
    )
    last, grad_raw, grad_gate_up = lax.optimization_barrier((last, grad_raw, grad_gate_up))
    last = scatter_z_aside(last)
    input_other = dot(grad_raw[seq_len:], full_qkv, 1, 1, BF16)
    input_own = dot(grad_raw[:seq_len], full_qkv, 1, 1, BF16)
    if dealt:
        grad_gate_up = return_rows(grad_gate_up, C, 2, Z, 10)
        *grad_gate_up, input_own, input_other = lax.optimization_barrier(
            (*grad_gate_up, input_own, input_other)
        )
    else:
        grad_gate_up = (
            exchange(grad_gate_up)
            .reshape(A, shard, 2, Z, part)
            .transpose(2, 1, 3, 0, 4)
            .reshape(2, shard, ffn_width)
        )
    grad_input = grad_hidden + scatter_rows(input_own, input_other, C, 6)
    grad_qkv = return_rows(last[:, : 3 * slice_width], C, 3, 1, 11)
    grad_w_out = lax.ppermute(
        last[:, 3 * slice_width :].reshape(shard, width),
        AXES,
        [(zz * A + p, p * Z + zz) for zz in range(Z) for p in range(A)],
    ).astype(F32)

    head_terms = lax.dynamic_update_slice(
        jnp.zeros((2, width), F32), head_terms[:2], (0, plane_at * slice_width)
    )
    gain_terms = jnp.concatenate([head_terms, term_gain_attn[None], term_gain_ffn[None]], axis=0)
    gain_sums = lax.dynamic_slice(sum_everywhere(gain_terms), (0, own_at * shard), (4, shard))

    return (
        output,
        grad_input,
        grad_qkv[0].astype(F32),
        grad_qkv[1].astype(F32),
        grad_qkv[2].astype(F32),
        grad_w_out,
        gain_sums[0],
        gain_sums[1],
        gain_sums[2],
        grad_gate_up[0].astype(F32),
        grad_gate_up[1].astype(F32),
        grad_w_down,
        gain_sums[3],
    )


def solution(mesh):
    split, line, copied = P(AXES, None), P(AXES), P()
    return jax.shard_map(
        functools.partial(layer, mesh.shape["ctx"], mesh.shape["dp"]),
        mesh=mesh,
        in_specs=(split,) * 5 + (line,) * 3 + (split,) * 3 + (line, copied, copied, split),
        out_specs=(split,) * 6 + (line,) * 3 + (split,) * 3 + (line,),
        check_vma=False,
    )
```

```python
import functools
import math

import jax
import jax.numpy as jnp
from jax import lax
from jax.experimental import pallas as pl
from jax.experimental.pallas import tpu as pltpu
from jax.sharding import PartitionSpec as P

HD = 128
IMG = 256
EPS = 1e-06
THETA = 500000.0
NEG = -1e30
AXES = ("dp", "ctx")
F32 = jnp.float32
BF16 = jnp.bfloat16
SCALE = 1.0 / math.sqrt(HD)
LOG2E = math.log2(math.e)


def dot(left, right, left_dim, right_dim, kind=F32):
    return lax.dot_general(
        left, right, (((left_dim,), (right_dim,)), ((), ())), preferred_element_type=kind
    )


def probs_of(q, k, limit, places):
    scores = dot(q, k, 1, 1)
    scores = jnp.where(places <= limit, scores, NEG)
    peak = jnp.max(scores, axis=-1, keepdims=True)
    weights = jnp.exp2((scores - peak) * (SCALE * LOG2E))
    return weights * (1.0 / jnp.sum(weights, axis=-1, keepdims=True))


def attend_kernel(q_ref, k_ref, v_ref, limit_ref, place_ref, out_ref):
    probs = probs_of(q_ref[...], k_ref[...], limit_ref[...], place_ref[0])
    out_ref[...] = dot(probs.astype(BF16), v_ref[...], 1, 0).astype(BF16)


def attend_back_kernel(
    q_ref, k_ref, v_ref, g_ref, limit_ref, place_ref, dq_ref, dk_ref, dv_ref
):
    step = pl.program_id(2)

    @pl.when(step == 0)
    def _():
        dk_ref[...] = jnp.zeros_like(dk_ref)
        dv_ref[...] = jnp.zeros_like(dv_ref)

    q, k, v, g = q_ref[...], k_ref[...], v_ref[...], g_ref[...]
    probs = probs_of(q, k, limit_ref[...], place_ref[0])
    grad_probs = dot(g, v, 1, 1)
    inner = jnp.sum(probs * grad_probs, axis=-1, keepdims=True)
    grad_scores = (probs * (grad_probs - inner)).astype(BF16)
    dq_ref[...] = dot(grad_scores, k, 1, 0) * SCALE
    dk_ref[...] += dot(grad_scores, q, 0, 0) * SCALE
    dv_ref[...] += dot(probs.astype(BF16), g, 0, 0)


def attention_specs(seq_len, rows):
    steps = seq_len // rows
    query = pl.BlockSpec((rows, HD), lambda s, h, i: (s * steps + i, h))
    keys = pl.BlockSpec((seq_len, HD), lambda s, h, i: (s, h))
    limit = pl.BlockSpec((rows, 1), lambda s, h, i: (s * steps + i, 0))
    places = pl.BlockSpec((1, 1, seq_len), lambda s, h, i: (s, 0, 0))
    return query, keys, limit, places


def attend(q, k, v, limits, places, seq_len):
    rows = min(256, seq_len)
    total, width = q.shape
    query, keys, limit, place = attention_specs(seq_len, rows)
    return pl.pallas_call(
        attend_kernel,
        out_shape=jax.ShapeDtypeStruct((total, width), BF16),
        grid=(total // seq_len, width // HD, seq_len // rows),
        in_specs=[query, keys, keys, limit, place],
        out_specs=query,
        compiler_params=pltpu.CompilerParams(vmem_limit_bytes=48 * 2**20),
        cost_estimate=pl.CostEstimate(
            flops=4 * total * seq_len * width,
            bytes_accessed=8 * total * width,
            transcendentals=total * seq_len * (width // HD),
        ),
        name="attend",
    )(q, k, v, limits, places)


def attend_back(q, k, v, g, limits, places, seq_len):
    rows = min(256, seq_len)
    total, width = q.shape
    query, keys, limit, place = attention_specs(seq_len, rows)
    shape = jax.ShapeDtypeStruct((total, width), F32)
    return pl.pallas_call(
        attend_back_kernel,
        out_shape=(shape, shape, shape),
        grid=(total // seq_len, width // HD, seq_len // rows),
        in_specs=[query, keys, keys, query, limit, place],
        out_specs=(query, keys, keys),
        compiler_params=pltpu.CompilerParams(vmem_limit_bytes=48 * 2**20),
        cost_estimate=pl.CostEstimate(
            flops=10 * total * seq_len * width,
            bytes_accessed=20 * total * width,
            transcendentals=total * seq_len * (width // HD),
        ),
        name="attend_back",
    )(q, k, v, g, limits, places)


MESH = pl.DeviceIdType.MESH
ANY = pl.BlockSpec(memory_space=pl.ANY)


def flipped(at, mask):
    bit = 1
    while bit <= mask:
        if mask & bit:
            at = at + bit - 2 * bit * lax.rem(lax.div(at, bit), 2)
        bit *= 2
    return at


def bit_orders(C):
    bits = [1 << b for b in range(C.bit_length() - 1)]
    return bits, bits[::-1]


def tree(order):
    found = [(0, order, 0)]
    for place, bit in enumerate(order):
        found += [(mask | bit, order[place + 1 :], bit) for mask, _, _ in list(found)]
    return found


def signal_barrier(peers):
    barrier = pltpu.get_barrier_semaphore()
    for peer in peers:
        pl.semaphore_signal(barrier, inc=1, device_id=peer, device_id_type=MESH)
    return barrier


def greet(peers):
    pl.semaphore_wait(signal_barrier(peers), len(peers))


def remote(src, dst, sent, arrived, device):
    return pltpu.make_async_remote_copy(
        src_ref=src, dst_ref=dst, send_sem=sent, recv_sem=arrived, device_id=device, device_id_type=MESH
    )


def places_of():
    dp, ctx = lax.axis_index("dp"), lax.axis_index("ctx")
    return dp, ctx, dp + 1 - 2 * lax.rem(dp, 2)


class Gather:
    def __init__(self, C, source, slot, over, from_over, sems):
        self.C = C
        self.source, self.slot, self.over, self.from_over = source, slot, over, from_over
        self.ctx_sent, self.ctx_came, self.core_sent, self.core_came = sems
        self.dp, self.ctx, self.twin = places_of()
        self.trees = [tree(order) for order in bit_orders(C)]
        self.sends = []

    def held(self, half, mask):
        return self.slot(flipped(self.ctx, mask), half) if mask else self.source(half)

    def by_ctx(self, half, mask, bit):
        return remote(
            self.held(half, mask),
            self.slot(flipped(self.ctx, mask), half),
            self.ctx_sent.at[half, mask | bit],
            self.ctx_came.at[half, mask | bit],
            (self.dp, flipped(self.ctx, bit)),
        )

    def by_core(self, half, mask):
        return remote(
            self.held(half, mask),
            self.over(flipped(self.ctx, mask), half),
            self.core_sent.at[half, mask],
            self.core_came.at[half, mask],
            (self.twin, self.ctx),
        )

    def landed(self, half, mask, bit):
        slot = self.slot(flipped(self.ctx, mask), half)
        remote(
            slot,
            slot,
            self.ctx_sent.at[half, mask],
            self.ctx_came.at[half, mask],
            (self.dp, flipped(self.ctx, bit)),
        ).wait_recv()

    def start(self, copy):
        copy.start()
        self.sends.append(copy)

    def step(self, index):
        for half in range(2):
            mask, onward, bit = self.trees[half][index]
            if mask:
                self.landed(half, mask, bit)
            for further in onward:
                self.start(self.by_ctx(half, mask, further))
            if mask:
                self.start(self.by_core(half, mask))
        if index == 0:
            for half in range(2):
                self.start(self.by_core(half, 0))

    def crossed(self, half, mask):
        slot = self.from_over(flipped(self.ctx, mask), half)
        remote(
            slot,
            slot,
            self.core_sent.at[half, mask],
            self.core_came.at[half, mask],
            (self.twin, self.ctx),
        ).wait_recv()

    def sent(self):
        for copy in self.sends:
            copy.wait_send()

    def finish(self):
        self.sent()
        for half in range(2):
            for mask in range(self.C):
                self.crossed(half, mask)

    def complete(self, index):
        place = [{m: at for at, (m, _, _) in enumerate(tree)} for tree in self.trees]
        return [m for m in range(self.C) if max(place[0][m], place[1][m]) == index]


def rows_gather(C, x_ref, out_ref, sems):
    count = x_ref.shape[0]
    size = count // 2

    def rows(seat, half):
        return pl.ds(seat * count + half * size, size)

    return Gather(
        C,
        lambda half: x_ref.at[pl.ds(half * size, size)],
        lambda seat, half: out_ref.at[0, rows(seat, half)],
        lambda seat, half: out_ref.at[1, rows(seat, half)],
        lambda seat, half: out_ref.at[1, rows(seat, half)],
        sems,
    )


class Ring:
    def __init__(self, Z, block, sent, came, way=1):
        dp, ctx, _ = places_of()
        self.Z, self.z, self.block, self.sems, self.way = Z, lax.div(dp, 2), block, (sent, came), way
        self.ahead = lax.rem(dp + 2 * Z + 2 * way, 2 * Z), ctx
        self.behind = lax.rem(dp + 2 * Z - 2 * way, 2 * Z), ctx

    def hop(self, step):
        spot = self.block(lax.rem(self.z + self.Z - self.way * step, self.Z))
        return remote(spot, spot, self.sems[0].at[step], self.sems[1].at[step], self.ahead)

    def landed(self, step):
        spot = self.block(lax.rem(self.z + 2 * self.Z - self.way * (1 + step), self.Z))
        remote(spot, spot, self.sems[0].at[step], self.sems[1].at[step], self.behind).wait_recv()

    def sent(self):
        for step in range(self.Z - 1):
            self.hop(step).wait_send()


def lines_gather(C, line_ref, out_ref, sems):
    dp, ctx, _ = places_of()
    core = lax.rem(dp, 2)
    size = line_ref.shape[0] // 2

    def slot(side, seat, half):
        return out_ref.at[pl.ds(half * size, size), side * C + seat]

    return Gather(
        C,
        lambda half: line_ref.at[pl.ds(half * size, size)],
        lambda seat, half: slot(core, seat, half),
        lambda seat, half: slot(core, seat, half),
        lambda seat, half: slot(1 - core, seat, half),
        sems,
    )


def gather_sems(C):
    return [pltpu.SemaphoreType.DMA((2, C))] * 4


def plane_neighbours(C):
    dp, ctx, twin = places_of()
    return [(dp, flipped(ctx, bit)) for bit in bit_orders(C)[0]] + [(twin, ctx)]


def comm_params(number, megabytes=16):
    return pltpu.CompilerParams(
        collective_id=number, has_side_effects=True, vmem_limit_bytes=megabytes * 2**20
    )


def cost_of(microseconds):
    return pl.CostEstimate(flops=int(microseconds * 1e6), bytes_accessed=1024, transcendentals=0)


def gather_kernel(C, x_ref, out_ref, own_sem, *sems):
    greet(plane_neighbours(C))
    count = x_ref.shape[0]
    own = pltpu.make_async_copy(
        x_ref, out_ref.at[0, pl.ds(lax.axis_index("ctx") * count, count)], own_sem
    )
    gather = rows_gather(C, x_ref, out_ref, sems)
    for index in range(C):
        gather.step(index)
        if index == 0:
            own.start()
    own.wait()
    gather.finish()


def gather_rows(x, C, number):
    return pl.pallas_call(
        functools.partial(gather_kernel, C),
        out_shape=jax.ShapeDtypeStruct((2, C * x.shape[0], x.shape[1]), x.dtype),
        in_specs=[ANY],
        out_specs=ANY,
        scratch_shapes=[pltpu.SemaphoreType.DMA] + gather_sems(C),
        compiler_params=comm_params(number),
        cost_estimate=cost_of(40),
        name="gather_rows",
    )(x)


def plane_peers(C):
    dp, ctx, twin = places_of()
    peers = [(there, flipped(ctx, mask)) for there in (dp, twin) for mask in range(C)]
    return list(enumerate(peers))[1:]


def place_in_plane(C, device):
    return lax.rem(device[0], 2) * C + device[1]


class Deal:
    def __init__(self, C, weights, wide, blocks, out_ref, row_at, sent, came, own_sem):
        self.C, self.out, self.wide, self.sems = C, out_ref, wide, (sent, came, own_sem)
        self.peers, self.row_at = plane_peers(C), row_at
        self.shard = weights[0].shape[0]
        dp, ctx, _ = places_of()
        self.parts = []
        for weight in weights:
            for block in range(blocks):
                self.parts.append((weight, block * 2 * C))
        self.own_device = (dp, ctx)
        self.copies = []

    def spot(self, device, number):
        rows = pl.ds(self.row_at(device), self.shard)
        return self.out.at[rows, pl.ds(number * self.wide, self.wide)]

    def start(self):
        sent, came, own_sem = self.sems
        for number, (weight, first) in enumerate(self.parts):
            for index, device in [(0, self.own_device)] + self.peers:
                at = (first + place_in_plane(self.C, device)) * self.wide
                source = weight.at[:, pl.ds(pl.multiple_of(at, 128), self.wide)]
                target = self.spot(self.own_device, number)
                if index == 0:
                    copy = pltpu.make_async_copy(source, target, own_sem.at[number])
                else:
                    copy = remote(
                        source, target, sent.at[number, index], came.at[number, index], device
                    )
                copy.start()
                self.copies.append((copy, index))

    def landed(self):
        sent, came, _ = self.sems
        for number in range(len(self.parts)):
            for index, device in self.peers:
                spot = self.spot(device, number)
                remote(
                    spot, spot, sent.at[number, index], came.at[number, index], device
                ).wait_recv()
        for copy, index in self.copies:
            if index:
                copy.wait_send()
            else:
                copy.wait()


def deal_sems(C, parts):
    return [
        pltpu.SemaphoreType.DMA((parts, 2 * C)),
        pltpu.SemaphoreType.DMA((parts, 2 * C)),
        pltpu.SemaphoreType.DMA((parts,)),
    ]


def first_kernel(C, Z, dealt, *refs):
    x_ref, wq_ref, wk_ref, wv_ref, wo_ref, gains_ref = refs[:6]
    refs = refs[6:]
    if dealt:
        (wg_ref, wu_ref), refs = refs[:2], refs[2:]
    x_out, w_out, wo_out, gains_line, gains_out = refs[:5]
    refs = refs[5:]
    if dealt:
        gu_out, refs = refs[0], refs[1:]
    own_sem, ring_sent, ring_came, gather_set, refs = refs[0], refs[1], refs[2], refs[3:7], refs[7:]
    gains_set, deal_set, refs = refs[:4], refs[4:7], refs[7:]
    A = 2 * C
    dp, ctx, _ = places_of()
    z, place = lax.div(dp, 2), lax.rem(dp, 2) * C + ctx
    shard = wq_ref.shape[0]
    rings = [
        Ring(Z, lambda at: gains_line.at[at], ring_sent.at[0], ring_came.at[0]),
        Ring(Z, lambda at: wo_out.at[at], ring_sent.at[1], ring_came.at[1]),
    ]
    size = A * shard // 2
    for half, way in enumerate((1, -1)):
        rings.append(
            Ring(
                Z,
                lambda at, half=half: w_out.at[pl.ds(at * (A * shard) + half * size, size)],
                ring_sent.at[2 + half],
                ring_came.at[2 + half],
                way,
            )
        )
    greet([device for _, device in plane_peers(C)] + [rings[0].ahead, rings[0].behind])
    lines = [
        pltpu.make_async_copy(gains_ref, gains_line.at[z], own_sem.at[0]),
        pltpu.make_async_copy(wo_ref, wo_out.at[z], own_sem.at[1]),
    ]
    for line in lines:
        line.start()
    deal = Deal(
        C, (wq_ref, wk_ref, wv_ref), wq_ref.shape[1] // A, 1, w_out,
        lambda device: (device[0] * C + device[1]) * shard, *deal_set,
    )
    deal.start()
    for line, ring in zip(lines, rings):
        line.wait()
        ring.hop(0).start()
    count = x_ref.shape[0]
    own = pltpu.make_async_copy(x_ref, x_out.at[0, pl.ds(ctx * count, count)], own_sem.at[2])
    own.start()
    gather = rows_gather(C, x_ref, x_out, gather_set)
    gather.step(0)
    deal.landed()
    for ring in rings[2:]:
        ring.hop(0).start()
    if dealt:
        columns = Deal(
            C, (wg_ref, wu_ref), wg_ref.shape[1] // (Z * A), Z, gu_out,
            lambda device: place_in_plane(C, device) * shard, *refs,
        )
        columns.start()
    for step in range(Z - 2):
        for ring in rings:
            ring.landed(step)
            ring.hop(step + 1).start()
        if step + 1 < C:
            gather.step(step + 1)
    for ring in rings[:2]:
        ring.landed(Z - 2)
    own_gains = pltpu.make_async_copy(gains_line, gains_out.at[:, place], own_sem.at[3])
    own_gains.start()
    for index in range(Z - 1, C):
        gather.step(index)
    gains = lines_gather(C, gains_line, gains_out, gains_set)
    for index in range(C):
        gains.step(index)
    if dealt:
        columns.landed()
    own.wait()
    own_gains.wait()
    gather.finish()
    gains.finish()
    for ring in rings[2:]:
        ring.landed(Z - 2)
    for ring in rings:
        ring.sent()


def first_gather(x, w_query, w_key, w_value, w_out, gains, w_gate, w_up, dealt, C, Z, number):
    width = x.shape[1]
    A = 2 * C
    shard = w_query.shape[0]

    def shape(*sizes):
        return jax.ShapeDtypeStruct(sizes, x.dtype)

    outs = [
        shape(2, C * x.shape[0], width),
        shape(width, 3 * width // A),
        shape(Z, shard, width),
        shape(Z, *gains.shape),
        shape(Z, A, *gains.shape),
    ]
    operands = [x, w_query, w_key, w_value, w_out, gains]
    scratch = (
        [pltpu.SemaphoreType.DMA((4,))]
        + [pltpu.SemaphoreType.DMA((4, Z))] * 2
        + gather_sems(C) * 2
        + deal_sems(C, 3)
    )
    if dealt:
        operands += [w_gate, w_up]
        outs.append(shape(A * shard, 2 * w_gate.shape[1] // A))
        scratch += deal_sems(C, 2 * Z)
    return pl.pallas_call(
        functools.partial(first_kernel, C, Z, dealt),
        out_shape=tuple(outs),
        in_specs=[ANY] * len(operands),
        out_specs=(ANY,) * len(outs),
        scratch_shapes=scratch,
        compiler_params=comm_params(number, 60),
        cost_estimate=cost_of(100),
        name="first_gather",
    )(*operands)


ROWS = 256


def row_of_sums(values):
    high = values.astype(BF16)
    rest = (values - high.astype(F32)).astype(BF16)
    ones = jnp.ones((8, values.shape[1]), BF16)
    return dot(ones, high, 1, 1) + dot(ones, rest, 1, 1)


def pair_of_rows(first, second):
    return jnp.where(lax.broadcasted_iota(jnp.int32, first.shape, 0) == 0, first, second)


def columns_of(rows):
    eye = (
        lax.broadcasted_iota(jnp.int32, (8, 8), 0) == lax.broadcasted_iota(jnp.int32, (8, 8), 1)
    ).astype(BF16)
    high = rows.astype(BF16)
    rest = rows - high.astype(F32)
    middle = rest.astype(BF16)
    low = (rest - middle.astype(F32)).astype(BF16)
    return dot(high, eye, 0, 0) + dot(middle, eye, 0, 0) + dot(low, eye, 0, 0)


def start_sum(C, stats, landing, sent, came):
    for index, device in plane_peers(C):
        remote(stats, landing.at[index], sent.at[index], came.at[index], device).start()


def finish_sum(C, stats, landing, sent, came, total):
    blocks = stats.shape[0]
    for index, device in plane_peers(C):
        remote(stats, landing.at[index], sent.at[index], came.at[index], device).wait()
    for block in range(blocks):
        value = stats[block]
        for index in range(1, 2 * C):
            value = value + landing[index, block if index < C else (block + blocks // 2) % blocks]
        total[block] = value


def turned(value, cosine, sine):
    return value * cosine + pltpu.roll(value, HD // 2, 1) * sine


def project_kernel(
    C, x_ref, w_ref, gain_ref, cos_ref, sin_ref, line_ref,
    rq_ref, rk_ref, v_ref, q_ref, k_ref, total, out_ref,
    own_sem, ctx_sent, ctx_came, core_sent, core_came, stats, landing, sent, came,
):
    greet([device for _, device in plane_peers(C)])
    dp, ctx, _ = places_of()
    gather = lines_gather(C, line_ref, out_ref, (ctx_sent, ctx_came, core_sent, core_came))
    own = pltpu.make_async_copy(line_ref, out_ref.at[:, lax.rem(dp, 2) * C + ctx], own_sem)
    own.start()
    gather.step(0)
    wide = rq_ref.shape[1]
    width = x_ref.shape[1]
    blocks = stats.shape[0]

    def rows_at(block):
        return pl.ds(pl.multiple_of(block * ROWS, ROWS), ROWS)

    @pl.loop(0, blocks)
    def _(block):
        here = rows_at(block)
        raw = dot(x_ref[here, :], w_ref[...], 1, 0)
        query, key = raw[:, :wide], raw[:, wide : 2 * wide]
        rq_ref[here, :] = query
        rk_ref[here, :] = key
        v_ref[here, :] = raw[:, 2 * wide :].astype(BF16)
        stats[block] = pair_of_rows(row_of_sums(query * query), row_of_sums(key * key))

    start_sum(C, stats, landing, sent, came)
    finish_sum(C, stats, landing, sent, came, total)
    gather.step(1)

    @pl.loop(0, blocks)
    def _(block):
        here = rows_at(block)
        factors = columns_of(lax.rsqrt(total[block] * (1.0 / width) + EPS))
        cosine, sine = cos_ref[here, :], sin_ref[here, :]
        for which, (raw, out) in enumerate(((rq_ref, q_ref), (rk_ref, k_ref))):
            factor = factors[:, which : which + 1]
            for head in range(wide // HD):
                lanes = slice(head * HD, (head + 1) * HD)
                value = raw[here, lanes] * factor * gain_ref[which : which + 1, lanes]
                out[here, lanes] = turned(value, cosine, sine).astype(BF16)

    for index in range(2, C):
        gather.step(index)
    own.wait()
    gather.finish()


def plane_sum_scratch(C, blocks):
    return [
        pltpu.VMEM((blocks, 8, ROWS), F32),
        pltpu.VMEM((2 * C, blocks, 8, ROWS), F32),
        pltpu.SemaphoreType.DMA((2 * C,)),
        pltpu.SemaphoreType.DMA((2 * C,)),
    ]


VM = pl.BlockSpec(memory_space=pltpu.VMEM)


def project(x, w, gains, cosine, sine, lines, C, number):
    total, width = x.shape
    wide = w.shape[1] // 3
    blocks = total // ROWS
    raw = jax.ShapeDtypeStruct((total, wide), F32)
    low = jax.ShapeDtypeStruct((total, wide), BF16)
    return pl.pallas_call(
        functools.partial(project_kernel, C),
        out_shape=(
            raw, raw, low, low, low,
            jax.ShapeDtypeStruct((blocks, 8, ROWS), F32),
            jax.ShapeDtypeStruct((lines.shape[0], 2 * C) + lines.shape[1:], BF16),
        ),
        in_specs=[VM] * 5 + [ANY],
        out_specs=(VM,) * 6 + (ANY,),
        scratch_shapes=[pltpu.SemaphoreType.DMA] + gather_sems(C) + plane_sum_scratch(C, blocks),
        compiler_params=comm_params(number, 48),
        cost_estimate=cost_of(18),
        name="project",
    )(x, w, gains, cosine, sine, lines)


def project_back_kernel(
    C, dq_ref, dk_ref, dv_ref, rq_ref, rk_ref, total, gain_ref, cos_ref, sin_ref, known_ref,
    out_ref, sum_ref, term_ref, own_terms, all_terms, terms_sent, terms_came,
    eq, ek, inner, stats, landing, sent, came,
):
    greet([device for _, device in plane_peers(C)])
    wide = rq_ref.shape[1]
    width = wide * 2 * C
    blocks = stats.shape[0]

    def rows_at(block):
        return pl.ds(pl.multiple_of(block * ROWS, ROWS), ROWS)

    def factors_of(block):
        return columns_of(lax.rsqrt(total[block] * (1.0 / width) + EPS))

    term_ref[...] = jnp.zeros_like(term_ref)

    @pl.loop(0, blocks)
    def _(block):
        here = rows_at(block)
        factors = factors_of(block)
        cosine, sine = cos_ref[here, :], sin_ref[here, :]
        sums = []
        for which, (grad, raw, kept) in enumerate(((dq_ref, rq_ref, eq), (dk_ref, rk_ref, ek))):
            for head in range(wide // HD):
                lanes = slice(head * HD, (head + 1) * HD)
                kept[here, lanes] = turned(grad[here, lanes], cosine, -sine)
            product = kept[here, :] * raw[here, :] * factors[:, which : which + 1]
            term_ref[which : which + 1, :] += jnp.sum(product, axis=0, keepdims=True)
            sums.append(row_of_sums(product * gain_ref[which : which + 1, :]))
        stats[block] = pair_of_rows(*sums)

    start_sum(C, stats, landing, sent, came)
    dp, ctx, _ = places_of()
    lanes = pl.ds(pl.multiple_of(place_in_plane(C, (dp, ctx)) * wide, 128), wide)
    own_terms[...] = known_ref[...]
    own_terms[:, lanes] = own_terms[:, lanes] + term_ref[...]
    for index, device in plane_peers(C):
        remote(
            own_terms, all_terms.at[index], terms_sent.at[index], terms_came.at[index], device
        ).start()
    finish_sum(C, stats, landing, sent, came, inner)

    @pl.loop(0, blocks)
    def _(block):
        here = rows_at(block)
        factors = factors_of(block)
        means = columns_of(inner[block] * (1.0 / width))
        for which, (kept, raw) in enumerate(((eq, rq_ref), (ek, rk_ref))):
            factor, mean = factors[:, which : which + 1], means[:, which : which + 1]
            weighted = kept[here, :] * gain_ref[which : which + 1, :]
            value = factor * (weighted - raw[here, :] * factor * mean)
            out_ref[here, which * wide : (which + 1) * wide] = value.astype(BF16)
        out_ref[here, 2 * wide :] = dv_ref[here, :].astype(BF16)

    terms = own_terms[...]
    for index, device in plane_peers(C):
        remote(
            own_terms, all_terms.at[index], terms_sent.at[index], terms_came.at[index], device
        ).wait()
        terms = terms + all_terms[index]
    sum_ref[...] = terms


def project_back(dq, dk, dv, raw_q, raw_k, sums, gains, cosine, sine, terms, C, number):
    total, wide = dq.shape
    blocks = total // ROWS
    return pl.pallas_call(
        functools.partial(project_back_kernel, C),
        out_shape=(
            jax.ShapeDtypeStruct((total, 3 * wide), BF16),
            jax.ShapeDtypeStruct(terms.shape, F32),
        ),
        in_specs=[VM] * 10,
        out_specs=(VM, VM),
        scratch_shapes=[
            pltpu.VMEM((8, wide), F32),
            pltpu.VMEM(terms.shape, F32),
            pltpu.VMEM((2 * C,) + terms.shape, F32),
            pltpu.SemaphoreType.DMA((2 * C,)),
            pltpu.SemaphoreType.DMA((2 * C,)),
            pltpu.VMEM((total, wide), F32),
            pltpu.VMEM((total, wide), F32),
            pltpu.VMEM((blocks, 8, ROWS), F32),
        ]
        + plane_sum_scratch(C, blocks),
        compiler_params=comm_params(number, 48),
        cost_estimate=cost_of(15),
        name="project_back",
    )(dq, dk, dv, raw_q, raw_k, sums, gains, cosine, sine, terms)


def attention_out_kernel(
    C, attended_ref, w_ref, tokens_ref, gain_ref, heads, proj, hidden_ref, h_out,
    low, own_sem, part_sent, part_came, copy_sem, *sems,
):
    count, width = tokens_ref.shape
    wide = width // (2 * C)
    dp, ctx, _ = places_of()
    here = place_in_plane(C, (dp, ctx))
    peers = plane_peers(C)
    greet([device for _, device in peers])

    def columns(at):
        return heads.at[:, pl.ds(pl.multiple_of(at * wide, 128), wide)]

    own = pltpu.make_async_copy(attended_ref.at[pl.ds(ctx * count, count)], columns(here), own_sem)
    own.start()
    copies = []
    for index, device in peers:
        rows = pl.ds(index // C * (C * count) + device[1] * count, count)
        copy = remote(
            attended_ref.at[rows], columns(here), part_sent.at[index], part_came.at[index], device
        )
        copy.start()
        copies.append(copy)
    own.wait()
    for index, device in peers:
        spot = columns(place_in_plane(C, device))
        remote(spot, spot, part_sent.at[index], part_came.at[index], device).wait_recv()
    for copy in copies:
        copy.wait_send()
    outs, size = tiles(width, 512)

    @pl.loop(0, outs)
    def _(number):
        lanes = at_tile(number, size)
        proj[:, lanes] = dot(heads[...], w_ref[:, lanes], 1, 0)

    chunks, chunk = tiles(count, 32)
    gain = gain_ref[0:1, :]

    @pl.loop(0, chunks)
    def _(number):
        rows = at_tile(number, chunk)
        value = proj[rows, :]
        factor = lax.rsqrt(jnp.mean(value * value, axis=-1, keepdims=True) + EPS)
        hidden = tokens_ref[rows, :].astype(F32) + value * factor * gain
        hidden_ref[rows, :] = hidden
        low[rows, :] = hidden.astype(BF16)

    gather = rows_gather(C, low, h_out, sems)
    copy = pltpu.make_async_copy(low, h_out.at[0, pl.ds(ctx * count, count)], copy_sem)
    for index in range(C):
        gather.step(index)
        if index == 0:
            copy.start()
    copy.wait()
    gather.finish()


def attention_out(attended, w, tokens, gain, C, number):
    count, width = tokens.shape
    whole = jax.ShapeDtypeStruct((count, width), F32)
    return pl.pallas_call(
        functools.partial(attention_out_kernel, C),
        out_shape=(
            jax.ShapeDtypeStruct((count, width), BF16),
            whole,
            whole,
            jax.ShapeDtypeStruct((2, C * count, width), BF16),
        ),
        in_specs=[VM] * 4,
        out_specs=(VM, VM, VM, ANY),
        scratch_shapes=[
            pltpu.VMEM((count, width), BF16),
            pltpu.SemaphoreType.DMA,
            pltpu.SemaphoreType.DMA((2 * C,)),
            pltpu.SemaphoreType.DMA((2 * C,)),
            pltpu.SemaphoreType.DMA,
        ]
        + gather_sems(C),
        compiler_params=comm_params(number, 40),
        cost_estimate=cost_of(60),
        name="attention_out",
    )(attended, w, tokens, gain)


def return_kernel(C, Z, groups, blocks, carried, x_ref, *refs):
    outs, refs = refs[:groups], refs[groups:]
    if carried:
        y_out, refs = refs[0], refs[1:]
    landing, sent, came, own_sem = refs[:4]
    A = 2 * C
    shard = outs[0].shape[0]
    part = outs[0].shape[1] // (blocks * A)
    wide = groups * blocks * part
    dp, ctx, _ = places_of()
    own_at = place_in_plane(C, (dp, ctx))
    peers = plane_peers(C)
    if not carried:
        greet([device for _, device in peers])
    else:
        y_sent, y_came = refs[4:]
        here = dp * C + ctx
        target = own_at * Z + lax.div(dp, 2)
        origin = lax.rem(here, Z) * A + lax.div(here, Z)
        ahead = lax.div(target, C), lax.rem(target, C)
        behind = lax.div(origin, C), lax.rem(origin, C)
        y_ref = x_ref.at[:, pl.ds(wide, carried)]
        carry = remote(y_ref, y_out, y_sent, y_came, ahead)

        barrier = signal_barrier([device for _, device in peers])

        @pl.when(target != here)
        def _():
            signal_barrier([ahead, behind])
            pl.semaphore_wait(barrier, len(peers) + 2)
            carry.start()

        @pl.when(target == here)
        def _():
            pl.semaphore_wait(barrier, len(peers))

    own = pltpu.make_async_copy(
        x_ref.at[pl.ds(own_at * shard, shard), pl.ds(0, wide)], landing.at[own_at], own_sem
    )
    own.start()

    def copy_to(index, device):
        rows = pl.ds(place_in_plane(C, device) * shard, shard)
        return remote(
            x_ref.at[rows, pl.ds(0, wide)],
            landing.at[own_at],
            sent.at[index],
            came.at[index],
            device,
        )

    def landed(index, device):
        spot = landing.at[place_in_plane(C, device)]
        remote(spot, spot, sent.at[index], came.at[index], device).wait_recv()

    for index, device in peers:
        copy_to(index, device).start()
    own.wait()
    for index, device in peers:
        landed(index, device)
    for index, device in peers:
        copy_to(index, device).wait_send()
    for group in range(groups):
        for block in range(blocks):
            for at in range(A):
                lanes = (group * blocks + block) * part
                to = (block * A + at) * part
                outs[group][:, to : to + part] = landing[at, :, lanes : lanes + part]
    if carried:

        @pl.when(target != here)
        def _():
            carry.wait()

        @pl.when(target == here)
        def _():
            keep = pltpu.make_async_copy(y_ref, y_out, y_sent)
            keep.start()
            keep.wait()


def return_rows(x, C, Z, groups, blocks, number, carried=0):
    A = 2 * C
    shard = x.shape[0] // A
    wide = x.shape[1] - carried
    shapes = (jax.ShapeDtypeStruct((shard, wide * A // groups), x.dtype),) * groups
    scratch = [
        pltpu.VMEM((A, shard, wide), x.dtype),
        pltpu.SemaphoreType.DMA((A,)),
        pltpu.SemaphoreType.DMA((A,)),
        pltpu.SemaphoreType.DMA,
    ]
    if carried:
        shapes += (jax.ShapeDtypeStruct((x.shape[0], carried), x.dtype),)
        scratch += [pltpu.SemaphoreType.DMA, pltpu.SemaphoreType.DMA]
    return pl.pallas_call(
        functools.partial(return_kernel, C, Z, groups, blocks, carried),
        out_shape=shapes,
        in_specs=[ANY],
        out_specs=(VM,) * len(shapes),
        scratch_shapes=scratch,
        compiler_params=comm_params(number, 24),
        cost_estimate=cost_of(20),
        name="return_rows",
    )(x)


class Scatter:
    def __init__(self, C, count, own, other, twin_part, landing, sems, final):
        self.C, self.count, self.half = C, count, count // 2
        self.own, self.other, self.twin_part, self.landing = own, other, twin_part, landing
        self.core_sent, self.core_came, self.ctx_sent, self.ctx_came = sems
        self.dp, self.ctx, self.twin = places_of()
        self.onward = [{m: (bits, bit) for m, bits, bit in tree(order)} for order in bit_orders(C)]
        self.final = final

    def rows(self, half, mask):
        return pl.ds(flipped(self.ctx, mask) * self.count + half * self.half, self.half)

    def block(self, mask):
        return pl.ds(flipped(self.ctx, mask) * self.count, self.count)

    def across(self, half, mask):
        return remote(
            self.other.at[self.rows(half, mask)],
            self.twin_part.at[self.rows(half, mask)],
            self.core_sent.at[half, mask],
            self.core_came.at[half, mask],
            (self.twin, self.ctx),
        )

    def back(self, half, mask, bit):
        return remote(
            self.own.at[self.rows(half, mask)],
            self.landing.at[half, mask],
            self.ctx_sent.at[half, mask],
            self.ctx_came.at[half, mask],
            (self.dp, flipped(self.ctx, bit)),
        )

    def settle(self, half, mask):
        along, bit = self.onward[half][mask]
        self.across(half, mask).wait_recv()
        here = self.rows(half, mask)
        total = self.own[here, :].astype(F32) + self.twin_part[here, :].astype(F32)
        for came in along:
            self.back(half, mask | came, came).wait_recv()
            total = total + self.landing[half, mask | came].astype(F32)
        if mask:
            self.own[here, :] = total.astype(BF16)
            self.back(half, mask, bit).start()
        else:
            self.final(half, total)

    def order(self):
        return sorted(range(self.C), key=lambda mask: (-bin(mask).count("1"), mask))

    def run(self, compute):
        waiting = []
        for mask in self.order():
            compute(1, mask)
            for half in range(2):
                self.across(half, mask).start()
            compute(0, mask)
            ready = [half for half in range(2) if mask and not self.onward[half][mask][0]]
            for half in ready:
                self.settle(half, mask)
            for half, earlier in waiting:
                self.settle(half, earlier)
            waiting = [(half, mask) for half in range(2) if half not in ready]
        for half, earlier in waiting:
            self.settle(half, earlier)
        for half in range(2):
            for mask in range(self.C):
                self.across(half, mask).wait_send()
                if mask:
                    self.back(half, mask, self.onward[half][mask][1]).wait_send()


def scatter_scratch(C, count, width):
    rows = pltpu.VMEM((C * count, width), BF16)
    return [rows, rows, rows, pltpu.VMEM((2, C, count // 2, width), BF16)] + [
        pltpu.SemaphoreType.DMA((2, C))
    ] * 4


def tiles(total, size):
    size = min(total, size)
    return total // size, size


def at_tile(number, size, base=0):
    return pl.ds(pl.multiple_of(base + number * size, size), size)


def mix_kernel(h_ref, wgu_ref, gu_ref, mixed_ref, turned_ref):
    ffn = mixed_ref.shape[1]
    steps, tile = tiles(ffn, 256)
    for number in range(steps):
        first = slice(number * tile, (number + 1) * tile)
        second = slice(ffn + number * tile, ffn + (number + 1) * tile)
        gate = dot(h_ref[...], wgu_ref[:, first], 1, 0)
        up = dot(h_ref[...], wgu_ref[:, second], 1, 0)
        gu_ref[:, first] = gate.astype(BF16)
        gu_ref[:, second] = up.astype(BF16)
        mixed = gate * jax.nn.sigmoid(gate) * up
        mixed_ref[:, first] = mixed.astype(BF16)
        turned_ref[first, :] = mixed.T.astype(BF16)


def mix(h, w_gate_up):
    total, width = h.shape
    ffn = w_gate_up.shape[1] // 2
    rows = min(256, total)
    return pl.pallas_call(
        mix_kernel,
        out_shape=(
            jax.ShapeDtypeStruct((total, 2 * ffn), BF16),
            jax.ShapeDtypeStruct((total, ffn), BF16),
            jax.ShapeDtypeStruct((ffn, total), BF16),
        ),
        grid=(total // rows,),
        in_specs=[
            pl.BlockSpec((rows, width), lambda i: (i, 0)),
            pl.BlockSpec((width, 2 * ffn), lambda i: (0, 0)),
        ],
        out_specs=(
            pl.BlockSpec((rows, 2 * ffn), lambda i: (i, 0)),
            pl.BlockSpec((rows, ffn), lambda i: (i, 0)),
            pl.BlockSpec((ffn, rows), lambda i: (0, i)),
        ),
        compiler_params=pltpu.CompilerParams(vmem_limit_bytes=48 * 2**20),
        cost_estimate=cost_of(20),
        name="mix",
    )(h, w_gate_up)


def feed_forward_kernel(
    C, mixed_ref, turned_ref, gu_ref, wd_ref, hidden_ref, cot_ref, gain_ref,
    out_ref, f_out, b_out, down_ref, term_ref,
    mixed_buf, proj, f_own, f_buf, turned_buf, gu_buf, b_buf, total,
    mixed_sem, f_sem, turned_sem, gu_sem, b_sem, own_sem,
    ctx_sent, ctx_came, core_sent, core_came,
    own, other, twin_part, landing, *sems,
):
    greet(plane_neighbours(C))
    count, width = hidden_ref.shape
    ffn = wd_ref.shape[0]
    seq = C * count
    half_rows = count // 2

    def final(half, value):
        proj[pl.ds(half * half_rows, half_rows), :] = value

    scatter = Scatter(C, count, own, other, twin_part, landing, sems, final)
    sequence = [(side, mask) for mask in scatter.order() for side in (1, 0)]

    def rows_of(side, mask):
        return pl.ds(pl.multiple_of(side * seq + flipped(scatter.ctx, mask) * count, count), count)

    def fetch(index):
        return pltpu.make_async_copy(
            mixed_ref.at[rows_of(*sequence[index])], mixed_buf.at[index % 2], mixed_sem.at[index % 2]
        )

    fetch(0).start()
    steps, tile = tiles(ffn, 256)
    outs, wide = tiles(width, 512)

    def compute(side, mask):
        index = sequence.index((side, mask))
        slot = index % 2
        fetch(index).wait()
        if index + 1 < len(sequence):
            fetch(index + 1).start()
        target, here = (own, other)[side], scatter.block(mask)

        @pl.loop(0, outs)
        def _(number):
            lanes = at_tile(number, wide)
            target[here, lanes] = dot(mixed_buf[slot], wd_ref[:, lanes], 1, 0).astype(BF16)

    scatter.run(compute)
    gain = gain_ref[0:1, :]
    term_ref[...] = jnp.zeros_like(term_ref)
    chunks, chunk = tiles(count, 32)

    @pl.loop(0, chunks)
    def _(number):
        here = at_tile(number, chunk)
        value = proj[here, :]
        factor = lax.rsqrt(jnp.mean(value * value, axis=-1, keepdims=True) + EPS)
        unit = value * factor
        out_ref[here, :] = (hidden_ref[here, :] + unit * gain).astype(BF16)
        incoming = cot_ref[here, :].astype(F32)
        weighted = incoming * gain
        inner = jnp.mean(weighted * unit, axis=-1, keepdims=True)
        f_own[here, :] = (factor * (weighted - unit * inner)).astype(BF16)
        term_ref[0:1, :] += jnp.sum(incoming * unit, axis=0, keepdims=True)

    gather = rows_gather(C, f_own, f_out, (ctx_sent, ctx_came, core_sent, core_came))
    copy = pltpu.make_async_copy(f_own, f_out.at[0, pl.ds(scatter.ctx * count, count)], own_sem)
    blocks = [
        (side, mask, index)
        for index in range(C)
        for mask in gather.complete(index)
        for side in (0, 1)
    ]

    def fetch_kept(number):
        side, mask, _ = blocks[number]
        slot, rows = number % 2, rows_of(side, mask)
        return (
            pltpu.make_async_copy(turned_ref.at[:, rows], turned_buf.at[slot], turned_sem.at[slot]),
            pltpu.make_async_copy(gu_ref.at[rows], gu_buf.at[slot], gu_sem.at[slot]),
        )

    def fetch_grad(number):
        side, mask, _ = blocks[number]
        return pltpu.make_async_copy(
            f_out.at[side, scatter.block(mask)], f_buf.at[number % 2], f_sem.at[number % 2]
        )

    def keep(number):
        side, mask, _ = blocks[number]
        return pltpu.make_async_copy(
            b_buf.at[number % 2], b_out.at[rows_of(side, mask)], b_sem.at[number % 2]
        )

    def back(number, grads):
        slot = number % 2
        for arrived in fetch_kept(number):
            arrived.wait()
        if number >= 2:
            keep(number - 2).wait()

        @pl.loop(0, steps)
        def _(at):
            first, second = at_tile(at, tile), at_tile(at, tile, ffn)
            grad = dot(grads[...], wd_ref[first, :], 1, 1)
            gate, up = gu_buf[slot, :, first].astype(F32), gu_buf[slot, :, second].astype(F32)
            sig = jax.nn.sigmoid(gate)
            b_buf[slot, :, first] = (grad * up * sig * (1.0 + gate * (1.0 - sig))).astype(BF16)
            b_buf[slot, :, second] = (grad * (gate * sig)).astype(BF16)

        keep(number).start()

        @pl.loop(0, outs)
        def _(at):
            lanes = at_tile(at, wide)
            value = dot(turned_buf[slot], grads[:, lanes], 1, 0)
            if number == 0:
                total[:, lanes] = value
            elif number < len(blocks) - 1:
                total[:, lanes] += value
            else:
                down_ref[:, lanes] = (total[:, lanes] + value).astype(BF16)

    for arriving in fetch_kept(0):
        arriving.start()
    done = 0
    for index in range(C):
        gather.step(index)
        if index == 0:
            copy.start()
        while done < len(blocks) and blocks[done][2] == index:
            side, mask, _ = blocks[done]
            if done + 1 < len(blocks):
                for arriving in fetch_kept(done + 1):
                    arriving.start()
            if (side, mask) == (0, 0):
                back(done, f_own)
            else:
                if side:
                    for half in range(2):
                        gather.crossed(half, mask)
                fetch_grad(done).start()
                fetch_grad(done).wait()
                back(done, f_buf.at[done % 2])
            done += 1
    for number in (len(blocks) - 2, len(blocks) - 1):
        keep(number).wait()
    copy.wait()
    gather.sent()


def feed_forward(mixed, turned_units, gate_up, w_down, hidden, cotangent, gain, C, number):
    count, width = hidden.shape
    total, ffn = 2 * C * count, w_down.shape[0]
    pair = pltpu.SemaphoreType.DMA((2,))
    return pl.pallas_call(
        functools.partial(feed_forward_kernel, C),
        out_shape=(
            jax.ShapeDtypeStruct((count, width), BF16),
            jax.ShapeDtypeStruct((2, C * count, width), BF16),
            jax.ShapeDtypeStruct((total, 2 * ffn), BF16),
            jax.ShapeDtypeStruct((ffn, width), BF16),
            jax.ShapeDtypeStruct((8, width), F32),
        ),
        in_specs=[ANY] * 3 + [VM] * 4,
        out_specs=(VM, ANY, ANY, VM, VM),
        scratch_shapes=[
            pltpu.VMEM((2, count, ffn), BF16),
            pltpu.VMEM((count, width), F32),
            pltpu.VMEM((count, width), BF16),
            pltpu.VMEM((2, count, width), BF16),
            pltpu.VMEM((2, ffn, count), BF16),
            pltpu.VMEM((2, count, 2 * ffn), BF16),
            pltpu.VMEM((2, count, 2 * ffn), BF16),
            pltpu.VMEM((ffn, width), F32),
            pair,
            pair,
            pair,
            pair,
            pair,
            pltpu.SemaphoreType.DMA,
        ]
        + gather_sems(C)
        + scatter_scratch(C, count, width),
        compiler_params=comm_params(number, 60),
        cost_estimate=cost_of(80),
        name="feed_forward",
    )(mixed, turned_units, gate_up, w_down, hidden, cotangent, gain)


def back_scatter_kernel(
    C, b_ref, w_ref, add_ref, out_ref, b_buf, b_sem, own, other, twin_part, landing, *sems
):
    greet(plane_neighbours(C))
    count, width = out_ref.shape
    seq = C * count
    half_rows = count // 2

    def final(half, total):
        rows = pl.ds(half * half_rows, half_rows)
        out_ref[rows, :] = total + add_ref[rows, :].astype(F32)

    scatter = Scatter(C, count, own, other, twin_part, landing, sems, final)
    sequence = [(side, mask) for mask in scatter.order() for side in (1, 0)]

    def fetch(index):
        side, mask = sequence[index]
        rows = pl.ds(side * seq + flipped(scatter.ctx, mask) * count, count)
        return pltpu.make_async_copy(b_ref.at[rows], b_buf.at[index % 2], b_sem.at[index % 2])

    fetch(0).start()
    outs, wide = tiles(width, 512)

    def compute(side, mask):
        index = sequence.index((side, mask))
        slot = index % 2
        fetch(index).wait()
        if index + 1 < len(sequence):
            fetch(index + 1).start()
        target, here = (own, other)[side], scatter.block(mask)

        @pl.loop(0, outs)
        def _(number):
            lanes = at_tile(number, wide)
            target[here, lanes] = dot(b_buf[slot], w_ref[lanes, :], 1, 1).astype(BF16)

    scatter.run(compute)


def back_scatter(b, w, add, C, number):
    count, width = add.shape
    return pl.pallas_call(
        functools.partial(back_scatter_kernel, C),
        out_shape=jax.ShapeDtypeStruct((count, width), F32),
        in_specs=[ANY, VM, VM],
        out_specs=VM,
        scratch_shapes=[
            pltpu.VMEM((2, count, b.shape[1]), BF16),
            pltpu.SemaphoreType.DMA((2,)),
        ]
        + scatter_scratch(C, count, width),
        compiler_params=comm_params(number, 48),
        cost_estimate=cost_of(50),
        name="back_scatter",
    )(b, w, add)


def rope_tables(places):
    half = HD // 2
    frequency = THETA ** (-(jnp.arange(half, dtype=F32) * 2.0) / HD)
    angles = places.astype(F32)[:, None] * frequency[None, :]
    cosine, sine = jnp.cos(angles), jnp.sin(angles)
    return jnp.concatenate([cosine, cosine], axis=1), jnp.concatenate([-sine, sine], axis=1)


def row_norm(tensor):
    factor = lax.rsqrt(jnp.mean(tensor * tensor, axis=-1, keepdims=True) + EPS)
    return tensor * factor, factor


def row_norm_back(unit, factor, gain, incoming):
    weighted = incoming * gain
    inner = jnp.mean(weighted * unit, axis=-1, keepdims=True)
    return factor * (weighted - unit * inner), jnp.sum(incoming * unit, axis=0)


def layer(
    ctx_size,
    dp_size,
    tokens,
    w_query,
    w_key,
    w_value,
    w_out,
    gain_query,
    gain_key,
    gain_attn,
    w_gate,
    w_up,
    w_down,
    gain_ffn,
    positions,
    image_starts,
    cotangent,
):
    C, Z = ctx_size, dp_size // 2
    A = 2 * C
    N = Z * A
    ctx, dp = lax.axis_index("ctx"), lax.axis_index("dp")
    core, z = lax.rem(dp, 2), lax.div(dp, 2)
    plane_at = core * C + ctx
    own_at = dp * C + ctx
    rows, width = tokens.shape
    ffn_width = w_gate.shape[1]
    shard = w_query.shape[0]
    down_shard = w_down.shape[0]
    seq_len = rows * C
    slice_width = width // A
    ffn_slice = ffn_width // A
    planes = [[zz * A + p for p in range(A)] for zz in range(Z)]
    columns = [[zz * 2 + k for zz in range(Z)] for k in range(2)]

    def swap(x, bit):
        return lax.ppermute(x, AXES, [(i, i ^ bit) for i in range(N)])

    def rows_of(x, at, count):
        return lax.dynamic_slice_in_dim(x, at, count, 0)

    def gather_z_aside(x):
        return lax.all_gather(x, "dp", axis=0, tiled=True, axis_index_groups=columns)

    def scatter_z_aside(x):
        return lax.psum_scatter(
            x, "dp", scatter_dimension=0, tiled=True, axis_index_groups=columns
        )

    def exchange(x):
        return lax.all_to_all(x, AXES, 0, 0, tiled=True, axis_index_groups=planes)

    part = down_shard
    dealt = part % 128 == 0
    gains = jnp.stack([gain_query, gain_key, gain_attn, gain_ffn])
    gains = jnp.pad(gains, ((0, 12), (0, -shard % 128)))
    x_both, full_qkv, out_lines, _, all_gains, *gate_up = first_gather(
        tokens, w_query, w_key, w_value, w_out, gains, w_gate, w_up, dealt, C, Z, 1
    )
    if dealt:
        gate_up = gate_up[0]
    else:
        gate_up = jnp.stack([w.reshape(shard, Z, A, part) for w in (w_gate, w_up)], axis=1)
        gate_up = exchange(gate_up.transpose(3, 0, 1, 2, 4).reshape(A * shard, 2 * ffn_slice))
    full_qkv, gate_up = lax.optimization_barrier((full_qkv, gate_up))
    full_gate_up = gather_z_aside(gate_up)
    all_gains = all_gains[:, :, :4, :shard].astype(F32).transpose(2, 0, 1, 3).reshape(4, width)
    head_gains = lax.dynamic_slice(all_gains, (0, plane_at * slice_width), (2, slice_width))
    head_gains = jnp.pad(head_gains, ((0, 6), (0, 0)))
    gain_a, gain_f = all_gains[2:3], all_gains[3:4]

    x_all = x_both.reshape(2 * seq_len, width)
    other_dp = dp + 1 - 2 * core
    places = jnp.concatenate(
        [rows_of(positions, dp * seq_len, seq_len), rows_of(positions, other_dp * seq_len, seq_len)]
    )
    starts = jnp.concatenate([rows_of(image_starts, dp, 1), rows_of(image_starts, other_dp, 1)])
    start_rows = jnp.repeat(starts, seq_len, axis=0)
    inside = (places[:, None] >= start_rows) & (places[:, None] < start_rows + IMG)
    limits = jnp.max(jnp.where(inside, start_rows + (IMG - 1), places[:, None]), axis=1)
    limit_column = limits[:, None]
    place_rows = places.reshape(2, 1, seq_len)
    cosine, sine = rope_tables(places)
    raw_q, raw_k, value, query_turned, key_turned, squares, full_out = project(
        x_all, full_qkv, head_gains, cosine, sine, out_lines, C, 8
    )
    full_out = full_out.reshape(width, width)
    attended = attend(query_turned, key_turned, value, limit_column, place_rows, seq_len)
    attended_own, attn_proj, hidden, h_both = attention_out(
        attended, full_out, tokens, jnp.pad(gain_a, ((0, 7), (0, 0))), C, 2
    )

    h_all = h_both.reshape(2 * seq_len, width)
    full_gate_up, w_down, h_all = lax.optimization_barrier((full_gate_up, w_down, h_all))
    full_down = gather_z_aside(w_down)
    gate_up_low, mixed, turned_units = mix(h_all, full_gate_up)
    output, f_both, b_all, term_down, term_gain_ffn = feed_forward(
        mixed, turned_units, gate_up_low, full_down, hidden, cotangent,
        jnp.pad(gain_f, ((0, 7), (0, 0))), C, 3,
    )

    term_down, b_all = lax.optimization_barrier((term_down, b_all))
    grad_w_down = scatter_z_aside(term_down)
    grad_hidden = back_scatter(b_all, full_gate_up, cotangent, C, 5)
    term_gate_up = dot(h_all, b_all, 0, 0, BF16)
    term_gate_up, grad_hidden, grad_w_down = lax.optimization_barrier(
        (term_gate_up, grad_hidden, grad_w_down)
    )
    grad_gate_up = scatter_z_aside(term_gate_up)

    attn_unit, attn_factor = row_norm(attn_proj)
    grad_attn, term_gain_attn = row_norm_back(attn_unit, attn_factor, gain_a, grad_hidden)
    a_all = gather_rows(grad_attn.astype(BF16), C, 7).reshape(2 * seq_len, width)
    grad_attended = dot(
        a_all, rows_of(full_out, plane_at * slice_width, slice_width), 1, 1, BF16
    )
    term_out = dot(attended, a_all, 0, 0, BF16)
    grad_q, grad_k, grad_v = attend_back(
        query_turned, key_turned, value, grad_attended, limit_column, place_rows, seq_len
    )
    known = jnp.concatenate(
        [jnp.zeros((2, width), F32), term_gain_attn[None], term_gain_ffn[:1], jnp.zeros((4, width), F32)]
    )
    grad_raw, gain_terms = project_back(
        grad_q, grad_k, grad_v, raw_q, raw_k, squares, head_gains, cosine, sine, known, C, 9
    )
    term_qkv = dot(x_all, grad_raw, 0, 0, BF16)
    last = jnp.concatenate([term_qkv, term_out.reshape(width, slice_width)], axis=1)
    last, grad_raw, grad_gate_up, gain_terms = lax.optimization_barrier(
        (last, grad_raw, grad_gate_up, gain_terms)
    )
    last = scatter_z_aside(last)
    if dealt:
        grad_gate_up = return_rows(grad_gate_up, C, Z, 2, Z, 10)
    else:
        grad_gate_up = (
            exchange(grad_gate_up)
            .reshape(A, shard, 2, Z, part)
            .transpose(2, 1, 3, 0, 4)
            .reshape(2, shard, ffn_width)
        )
    gain_terms = gain_terms[:4]
    gain_terms = gain_terms + swap(gain_terms, A)
    *grad_gate_up, gain_terms, grad_raw = lax.optimization_barrier(
        (grad_gate_up[0].astype(F32), grad_gate_up[1].astype(F32), gain_terms, grad_raw)
    )
    for power in range(1, Z.bit_length() - 1):
        gain_terms = gain_terms + swap(gain_terms, A << power)
    grad_input = back_scatter(grad_raw, full_qkv, grad_hidden, C, 6)
    last, grad_input = lax.optimization_barrier((last, grad_input))
    *grad_qkv, grad_w_out = return_rows(last, C, Z, 3, 1, 11, slice_width)
    gain_sums = lax.dynamic_slice(gain_terms, (0, own_at * shard), (4, shard))

    return (
        output,
        grad_input,
        grad_qkv[0].astype(F32),
        grad_qkv[1].astype(F32),
        grad_qkv[2].astype(F32),
        grad_w_out.reshape(shard, width).astype(F32),
        gain_sums[0],
        gain_sums[1],
        gain_sums[2],
        grad_gate_up[0],
        grad_gate_up[1],
        grad_w_down.astype(F32),
        gain_sums[3],
    )


def solution(mesh):
    split, line, copied = P(AXES, None), P(AXES), P()
    return jax.shard_map(
        functools.partial(layer, mesh.shape["ctx"], mesh.shape["dp"]),
        mesh=mesh,
        in_specs=(split,) * 5 + (line,) * 3 + (split,) * 3 + (line, copied, copied, split),
        out_specs=(split,) * 6 + (line,) * 3 + (split,) * 3 + (line,),
        check_vma=False,
    )
```

```python
import functools
import math

import jax
import jax.numpy as jnp
from jax import lax
from jax.experimental import pallas as pl
from jax.experimental.pallas import tpu as pltpu
from jax.sharding import PartitionSpec as P

HD = 128
IMG = 256
EPS = 1e-06
THETA = 500000.0
NEG = -1e30
AXES = ("dp", "ctx")
F32 = jnp.float32
BF16 = jnp.bfloat16
SCALE = 1.0 / math.sqrt(HD)
LOG2E = math.log2(math.e)


def dot(left, right, left_dim, right_dim, kind=F32):
    return lax.dot_general(
        left, right, (((left_dim,), (right_dim,)), ((), ())), preferred_element_type=kind
    )


def probs_of(q, k, limit, places):
    scores = dot(q, k, 1, 1)
    scores = jnp.where(places <= limit, scores, NEG)
    peak = jnp.max(scores, axis=-1, keepdims=True)
    weights = jnp.exp2((scores - peak) * (SCALE * LOG2E))
    return weights * (1.0 / jnp.sum(weights, axis=-1, keepdims=True))


def attend_kernel(q_ref, k_ref, v_ref, limit_ref, place_ref, out_ref):
    probs = probs_of(q_ref[...], k_ref[...], limit_ref[...], place_ref[0])
    out_ref[...] = dot(probs.astype(BF16), v_ref[...], 1, 0).astype(BF16)


def attend_back_kernel(
    q_ref, k_ref, v_ref, g_ref, limit_ref, place_ref, dq_ref, dk_ref, dv_ref
):
    step = pl.program_id(2)

    @pl.when(step == 0)
    def _():
        dk_ref[...] = jnp.zeros_like(dk_ref)
        dv_ref[...] = jnp.zeros_like(dv_ref)

    q, k, v, g = q_ref[...], k_ref[...], v_ref[...], g_ref[...]
    probs = probs_of(q, k, limit_ref[...], place_ref[0])
    grad_probs = dot(g, v, 1, 1)
    inner = jnp.sum(probs * grad_probs, axis=-1, keepdims=True)
    grad_scores = (probs * (grad_probs - inner)).astype(BF16)
    dq_ref[...] = dot(grad_scores, k, 1, 0) * SCALE
    dk_ref[...] += dot(grad_scores, q, 0, 0) * SCALE
    dv_ref[...] += dot(probs.astype(BF16), g, 0, 0)


def attention_specs(seq_len, rows):
    steps = seq_len // rows
    query = pl.BlockSpec((rows, HD), lambda s, h, i: (s * steps + i, h))
    keys = pl.BlockSpec((seq_len, HD), lambda s, h, i: (s, h))
    limit = pl.BlockSpec((rows, 1), lambda s, h, i: (s * steps + i, 0))
    places = pl.BlockSpec((1, 1, seq_len), lambda s, h, i: (s, 0, 0))
    return query, keys, limit, places


def attend(q, k, v, limits, places, seq_len):
    rows = min(256, seq_len)
    total, width = q.shape
    query, keys, limit, place = attention_specs(seq_len, rows)
    return pl.pallas_call(
        attend_kernel,
        out_shape=jax.ShapeDtypeStruct((total, width), BF16),
        grid=(total // seq_len, width // HD, seq_len // rows),
        in_specs=[query, keys, keys, limit, place],
        out_specs=query,
        compiler_params=pltpu.CompilerParams(vmem_limit_bytes=48 * 2**20),
        cost_estimate=pl.CostEstimate(
            flops=4 * total * seq_len * width,
            bytes_accessed=8 * total * width,
            transcendentals=total * seq_len * (width // HD),
        ),
        name="attend",
    )(q, k, v, limits, places)


def attend_back(q, k, v, g, limits, places, seq_len):
    rows = min(256, seq_len)
    total, width = q.shape
    query, keys, limit, place = attention_specs(seq_len, rows)
    shape = jax.ShapeDtypeStruct((total, width), F32)
    return pl.pallas_call(
        attend_back_kernel,
        out_shape=(shape, shape, shape),
        grid=(total // seq_len, width // HD, seq_len // rows),
        in_specs=[query, keys, keys, query, limit, place],
        out_specs=(query, keys, keys),
        compiler_params=pltpu.CompilerParams(vmem_limit_bytes=48 * 2**20),
        cost_estimate=pl.CostEstimate(
            flops=10 * total * seq_len * width,
            bytes_accessed=20 * total * width,
            transcendentals=total * seq_len * (width // HD),
        ),
        name="attend_back",
    )(q, k, v, g, limits, places)


MESH = pl.DeviceIdType.MESH
ANY = pl.BlockSpec(memory_space=pl.ANY)


def flipped(at, mask):
    bit = 1
    while bit <= mask:
        if mask & bit:
            at = at + bit - 2 * bit * lax.rem(lax.div(at, bit), 2)
        bit *= 2
    return at


def bit_orders(C):
    bits = [1 << b for b in range(C.bit_length() - 1)]
    return bits, bits[::-1]


def tree(order):
    found = [(0, order, 0)]
    for place, bit in enumerate(order):
        found += [(mask | bit, order[place + 1 :], bit) for mask, _, _ in list(found)]
    return found


def signal_barrier(peers):
    barrier = pltpu.get_barrier_semaphore()
    for peer in peers:
        pl.semaphore_signal(barrier, inc=1, device_id=peer, device_id_type=MESH)
    return barrier


def greet(peers):
    pl.semaphore_wait(signal_barrier(peers), len(peers))


def remote(src, dst, sent, arrived, device):
    return pltpu.make_async_remote_copy(
        src_ref=src, dst_ref=dst, send_sem=sent, recv_sem=arrived, device_id=device, device_id_type=MESH
    )


def places_of():
    dp, ctx = lax.axis_index("dp"), lax.axis_index("ctx")
    return dp, ctx, dp + 1 - 2 * lax.rem(dp, 2)


class Gather:
    def __init__(self, C, source, slot, over, from_over, sems):
        self.C = C
        self.source, self.slot, self.over, self.from_over = source, slot, over, from_over
        self.ctx_sent, self.ctx_came, self.core_sent, self.core_came = sems
        self.dp, self.ctx, self.twin = places_of()
        self.trees = [tree(order) for order in bit_orders(C)]
        self.sends = []

    def held(self, half, mask):
        return self.slot(flipped(self.ctx, mask), half) if mask else self.source(half)

    def by_ctx(self, half, mask, bit):
        return remote(
            self.held(half, mask),
            self.slot(flipped(self.ctx, mask), half),
            self.ctx_sent.at[half, mask | bit],
            self.ctx_came.at[half, mask | bit],
            (self.dp, flipped(self.ctx, bit)),
        )

    def by_core(self, half, mask):
        return remote(
            self.held(half, mask),
            self.over(flipped(self.ctx, mask), half),
            self.core_sent.at[half, mask],
            self.core_came.at[half, mask],
            (self.twin, self.ctx),
        )

    def landed(self, half, mask, bit):
        slot = self.slot(flipped(self.ctx, mask), half)
        remote(
            slot,
            slot,
            self.ctx_sent.at[half, mask],
            self.ctx_came.at[half, mask],
            (self.dp, flipped(self.ctx, bit)),
        ).wait_recv()

    def start(self, copy):
        copy.start()
        self.sends.append(copy)

    def step(self, index):
        for half in range(2):
            mask, onward, bit = self.trees[half][index]
            if mask:
                self.landed(half, mask, bit)
            for further in onward:
                self.start(self.by_ctx(half, mask, further))
            if mask:
                self.start(self.by_core(half, mask))
        if index == 0:
            for half in range(2):
                self.start(self.by_core(half, 0))

    def crossed(self, half, mask):
        slot = self.from_over(flipped(self.ctx, mask), half)
        remote(
            slot,
            slot,
            self.core_sent.at[half, mask],
            self.core_came.at[half, mask],
            (self.twin, self.ctx),
        ).wait_recv()

    def sent(self):
        for copy in self.sends:
            copy.wait_send()

    def finish(self):
        self.sent()
        for half in range(2):
            for mask in range(self.C):
                self.crossed(half, mask)

    def complete(self, index):
        place = [{m: at for at, (m, _, _) in enumerate(tree)} for tree in self.trees]
        return [m for m in range(self.C) if max(place[0][m], place[1][m]) == index]


def rows_gather(C, x_ref, out_ref, sems):
    count = x_ref.shape[0]
    size = count // 2

    def rows(seat, half):
        return pl.ds(seat * count + half * size, size)

    return Gather(
        C,
        lambda half: x_ref.at[pl.ds(half * size, size)],
        lambda seat, half: out_ref.at[0, rows(seat, half)],
        lambda seat, half: out_ref.at[1, rows(seat, half)],
        lambda seat, half: out_ref.at[1, rows(seat, half)],
        sems,
    )


class Ring:
    def __init__(self, Z, block, sent, came, way=1):
        dp, ctx, _ = places_of()
        self.Z, self.z, self.block, self.sems, self.way = Z, lax.div(dp, 2), block, (sent, came), way
        self.ahead = lax.rem(dp + 2 * Z + 2 * way, 2 * Z), ctx
        self.behind = lax.rem(dp + 2 * Z - 2 * way, 2 * Z), ctx

    def hop(self, step):
        spot = self.block(lax.rem(self.z + self.Z - self.way * step, self.Z))
        return remote(spot, spot, self.sems[0].at[step], self.sems[1].at[step], self.ahead)

    def landed(self, step):
        spot = self.block(lax.rem(self.z + 2 * self.Z - self.way * (1 + step), self.Z))
        remote(spot, spot, self.sems[0].at[step], self.sems[1].at[step], self.behind).wait_recv()

    def sent(self):
        for step in range(self.Z - 1):
            self.hop(step).wait_send()


def lines_gather(C, line_ref, out_ref, sems):
    dp, ctx, _ = places_of()
    core = lax.rem(dp, 2)
    size = line_ref.shape[0] // 2

    def slot(side, seat, half):
        return out_ref.at[pl.ds(half * size, size), side * C + seat]

    return Gather(
        C,
        lambda half: line_ref.at[pl.ds(half * size, size)],
        lambda seat, half: slot(core, seat, half),
        lambda seat, half: slot(core, seat, half),
        lambda seat, half: slot(1 - core, seat, half),
        sems,
    )


def gather_sems(C):
    return [pltpu.SemaphoreType.DMA((2, C))] * 4


def plane_neighbours(C):
    dp, ctx, twin = places_of()
    return [(dp, flipped(ctx, bit)) for bit in bit_orders(C)[0]] + [(twin, ctx)]


def comm_params(number, megabytes=16):
    return pltpu.CompilerParams(
        collective_id=number, has_side_effects=True, vmem_limit_bytes=megabytes * 2**20
    )


def cost_of(microseconds):
    return pl.CostEstimate(flops=int(microseconds * 1e6), bytes_accessed=1024, transcendentals=0)


def gather_kernel(C, x_ref, out_ref, own_sem, *sems):
    greet(plane_neighbours(C))
    count = x_ref.shape[0]
    own = pltpu.make_async_copy(
        x_ref, out_ref.at[0, pl.ds(lax.axis_index("ctx") * count, count)], own_sem
    )
    gather = rows_gather(C, x_ref, out_ref, sems)
    for index in range(C):
        gather.step(index)
        if index == 0:
            own.start()
    own.wait()
    gather.finish()


def gather_rows(x, C, number):
    return pl.pallas_call(
        functools.partial(gather_kernel, C),
        out_shape=jax.ShapeDtypeStruct((2, C * x.shape[0], x.shape[1]), x.dtype),
        in_specs=[ANY],
        out_specs=ANY,
        scratch_shapes=[pltpu.SemaphoreType.DMA] + gather_sems(C),
        compiler_params=comm_params(number),
        cost_estimate=cost_of(40),
        name="gather_rows",
    )(x)


def plane_peers(C):
    dp, ctx, twin = places_of()
    peers = [(there, flipped(ctx, mask)) for there in (dp, twin) for mask in range(C)]
    return list(enumerate(peers))[1:]


def place_in_plane(C, device):
    return lax.rem(device[0], 2) * C + device[1]


class Deal:
    def __init__(self, C, weights, wide, blocks, out_ref, row_at, sent, came, own_sem):
        self.C, self.out, self.wide, self.sems = C, out_ref, wide, (sent, came, own_sem)
        self.peers, self.row_at = plane_peers(C), row_at
        self.shard = weights[0].shape[0]
        dp, ctx, _ = places_of()
        self.parts = []
        for weight in weights:
            for block in range(blocks):
                self.parts.append((weight, block * 2 * C))
        self.own_device = (dp, ctx)
        self.copies = []

    def spot(self, device, number):
        rows = pl.ds(self.row_at(device), self.shard)
        return self.out.at[rows, pl.ds(number * self.wide, self.wide)]

    def start(self):
        sent, came, own_sem = self.sems
        for number, (weight, first) in enumerate(self.parts):
            for index, device in [(0, self.own_device)] + self.peers:
                at = (first + place_in_plane(self.C, device)) * self.wide
                source = weight.at[:, pl.ds(pl.multiple_of(at, 128), self.wide)]
                target = self.spot(self.own_device, number)
                if index == 0:
                    copy = pltpu.make_async_copy(source, target, own_sem.at[number])
                else:
                    copy = remote(
                        source, target, sent.at[number, index], came.at[number, index], device
                    )
                copy.start()
                self.copies.append((copy, index))

    def landed(self):
        sent, came, _ = self.sems
        for number in range(len(self.parts)):
            for index, device in self.peers:
                spot = self.spot(device, number)
                remote(
                    spot, spot, sent.at[number, index], came.at[number, index], device
                ).wait_recv()
        for copy, index in self.copies:
            if index:
                copy.wait_send()
            else:
                copy.wait()


def deal_sems(C, parts):
    return [
        pltpu.SemaphoreType.DMA((parts, 2 * C)),
        pltpu.SemaphoreType.DMA((parts, 2 * C)),
        pltpu.SemaphoreType.DMA((parts,)),
    ]


def first_kernel(C, Z, dealt, *refs):
    x_ref, wq_ref, wk_ref, wv_ref, wo_ref, gains_ref = refs[:6]
    refs = refs[6:]
    if dealt:
        (wg_ref, wu_ref), refs = refs[:2], refs[2:]
    x_out, w_out, wo_out, gains_line, gains_out = refs[:5]
    refs = refs[5:]
    if dealt:
        gu_out, refs = refs[0], refs[1:]
    own_sem, ring_sent, ring_came, gather_set, refs = refs[0], refs[1], refs[2], refs[3:7], refs[7:]
    gains_set, deal_set, refs = refs[:4], refs[4:7], refs[7:]
    A = 2 * C
    dp, ctx, _ = places_of()
    z, place = lax.div(dp, 2), lax.rem(dp, 2) * C + ctx
    shard = wq_ref.shape[0]
    rings = [
        Ring(Z, lambda at: gains_line.at[at], ring_sent.at[0], ring_came.at[0]),
        Ring(Z, lambda at: wo_out.at[at], ring_sent.at[1], ring_came.at[1]),
    ]
    size = A * shard // 2
    for half, way in enumerate((1, -1)):
        rings.append(
            Ring(
                Z,
                lambda at, half=half: w_out.at[pl.ds(at * (A * shard) + half * size, size)],
                ring_sent.at[2 + half],
                ring_came.at[2 + half],
                way,
            )
        )
    greet([device for _, device in plane_peers(C)] + [rings[0].ahead, rings[0].behind])
    lines = [
        pltpu.make_async_copy(gains_ref, gains_line.at[z], own_sem.at[0]),
        pltpu.make_async_copy(wo_ref, wo_out.at[z], own_sem.at[1]),
    ]
    for line in lines:
        line.start()
    deal = Deal(
        C, (wq_ref, wk_ref, wv_ref), wq_ref.shape[1] // A, 1, w_out,
        lambda device: (device[0] * C + device[1]) * shard, *deal_set,
    )
    deal.start()
    for line, ring in zip(lines, rings):
        line.wait()
        ring.hop(0).start()
    count = x_ref.shape[0]
    own = pltpu.make_async_copy(x_ref, x_out.at[0, pl.ds(ctx * count, count)], own_sem.at[2])
    own.start()
    gather = rows_gather(C, x_ref, x_out, gather_set)
    gather.step(0)
    deal.landed()
    for ring in rings[2:]:
        ring.hop(0).start()
    if dealt:
        columns = Deal(
            C, (wg_ref, wu_ref), wg_ref.shape[1] // (Z * A), Z, gu_out,
            lambda device: place_in_plane(C, device) * shard, *refs,
        )
        columns.start()
    for step in range(Z - 2):
        for ring in rings:
            ring.landed(step)
            ring.hop(step + 1).start()
        if step + 1 < C:
            gather.step(step + 1)
    for ring in rings[:2]:
        ring.landed(Z - 2)
    own_gains = pltpu.make_async_copy(gains_line, gains_out.at[:, place], own_sem.at[3])
    own_gains.start()
    for index in range(Z - 1, C):
        gather.step(index)
    gains = lines_gather(C, gains_line, gains_out, gains_set)
    for index in range(C):
        gains.step(index)
    if dealt:
        columns.landed()
    own.wait()
    own_gains.wait()
    gather.finish()
    gains.finish()
    for ring in rings[2:]:
        ring.landed(Z - 2)
    for ring in rings:
        ring.sent()


def first_gather(x, w_query, w_key, w_value, w_out, gains, w_gate, w_up, dealt, C, Z, number):
    width = x.shape[1]
    A = 2 * C
    shard = w_query.shape[0]

    def shape(*sizes):
        return jax.ShapeDtypeStruct(sizes, x.dtype)

    outs = [
        shape(2, C * x.shape[0], width),
        shape(width, 3 * width // A),
        shape(Z, shard, width),
        shape(Z, *gains.shape),
        shape(Z, A, *gains.shape),
    ]
    operands = [x, w_query, w_key, w_value, w_out, gains]
    scratch = (
        [pltpu.SemaphoreType.DMA((4,))]
        + [pltpu.SemaphoreType.DMA((4, Z))] * 2
        + gather_sems(C) * 2
        + deal_sems(C, 3)
    )
    if dealt:
        operands += [w_gate, w_up]
        outs.append(shape(A * shard, 2 * w_gate.shape[1] // A))
        scratch += deal_sems(C, 2 * Z)
    return pl.pallas_call(
        functools.partial(first_kernel, C, Z, dealt),
        out_shape=tuple(outs),
        in_specs=[ANY] * len(operands),
        out_specs=(ANY,) * len(outs),
        scratch_shapes=scratch,
        compiler_params=comm_params(number, 60),
        cost_estimate=cost_of(100),
        name="first_gather",
    )(*operands)


ROWS = 256


def row_of_sums(values):
    high = values.astype(BF16)
    rest = (values - high.astype(F32)).astype(BF16)
    ones = jnp.ones((8, values.shape[1]), BF16)
    return dot(ones, high, 1, 1) + dot(ones, rest, 1, 1)


def pair_of_rows(first, second):
    return jnp.where(lax.broadcasted_iota(jnp.int32, first.shape, 0) == 0, first, second)


def columns_of(rows):
    eye = (
        lax.broadcasted_iota(jnp.int32, (8, 8), 0) == lax.broadcasted_iota(jnp.int32, (8, 8), 1)
    ).astype(BF16)
    high = rows.astype(BF16)
    rest = rows - high.astype(F32)
    middle = rest.astype(BF16)
    low = (rest - middle.astype(F32)).astype(BF16)
    return dot(high, eye, 0, 0) + dot(middle, eye, 0, 0) + dot(low, eye, 0, 0)


def start_sum(C, stats, landing, sent, came):
    for index, device in plane_peers(C):
        remote(stats, landing.at[index], sent.at[index], came.at[index], device).start()


def finish_sum(C, stats, landing, sent, came, total):
    blocks = stats.shape[0]
    for index, device in plane_peers(C):
        remote(stats, landing.at[index], sent.at[index], came.at[index], device).wait()
    for block in range(blocks):
        value = stats[block]
        for index in range(1, 2 * C):
            value = value + landing[index, block if index < C else (block + blocks // 2) % blocks]
        total[block] = value


def turned(value, cosine, sine):
    return value * cosine + pltpu.roll(value, HD // 2, 1) * sine


def project_kernel(
    C, x_ref, w_ref, gain_ref, cos_ref, sin_ref, line_ref,
    rq_ref, rk_ref, v_ref, q_ref, k_ref, total, out_ref,
    own_sem, ctx_sent, ctx_came, core_sent, core_came, stats, landing, sent, came,
):
    greet([device for _, device in plane_peers(C)])
    dp, ctx, _ = places_of()
    gather = lines_gather(C, line_ref, out_ref, (ctx_sent, ctx_came, core_sent, core_came))
    own = pltpu.make_async_copy(line_ref, out_ref.at[:, lax.rem(dp, 2) * C + ctx], own_sem)
    own.start()
    gather.step(0)
    wide = rq_ref.shape[1]
    width = x_ref.shape[1]
    blocks = stats.shape[0]

    def rows_at(block):
        return pl.ds(pl.multiple_of(block * ROWS, ROWS), ROWS)

    @pl.loop(0, blocks)
    def _(block):
        here = rows_at(block)
        raw = dot(x_ref[here, :], w_ref[...], 1, 0)
        query, key = raw[:, :wide], raw[:, wide : 2 * wide]
        rq_ref[here, :] = query
        rk_ref[here, :] = key
        v_ref[here, :] = raw[:, 2 * wide :].astype(BF16)
        stats[block] = pair_of_rows(row_of_sums(query * query), row_of_sums(key * key))

    start_sum(C, stats, landing, sent, came)
    finish_sum(C, stats, landing, sent, came, total)
    gather.step(1)

    @pl.loop(0, blocks)
    def _(block):
        here = rows_at(block)
        factors = columns_of(lax.rsqrt(total[block] * (1.0 / width) + EPS))
        cosine, sine = cos_ref[here, :], sin_ref[here, :]
        for which, (raw, out) in enumerate(((rq_ref, q_ref), (rk_ref, k_ref))):
            factor = factors[:, which : which + 1]
            for head in range(wide // HD):
                lanes = slice(head * HD, (head + 1) * HD)
                value = raw[here, lanes] * factor * gain_ref[which : which + 1, lanes]
                out[here, lanes] = turned(value, cosine, sine).astype(BF16)

    for index in range(2, C):
        gather.step(index)
    own.wait()
    gather.finish()


def plane_sum_scratch(C, blocks):
    return [
        pltpu.VMEM((blocks, 8, ROWS), F32),
        pltpu.VMEM((2 * C, blocks, 8, ROWS), F32),
        pltpu.SemaphoreType.DMA((2 * C,)),
        pltpu.SemaphoreType.DMA((2 * C,)),
    ]


VM = pl.BlockSpec(memory_space=pltpu.VMEM)


def project(x, w, gains, cosine, sine, lines, C, number):
    total, width = x.shape
    wide = w.shape[1] // 3
    blocks = total // ROWS
    raw = jax.ShapeDtypeStruct((total, wide), F32)
    low = jax.ShapeDtypeStruct((total, wide), BF16)
    return pl.pallas_call(
        functools.partial(project_kernel, C),
        out_shape=(
            raw, raw, low, low, low,
            jax.ShapeDtypeStruct((blocks, 8, ROWS), F32),
            jax.ShapeDtypeStruct((lines.shape[0], 2 * C) + lines.shape[1:], BF16),
        ),
        in_specs=[VM] * 5 + [ANY],
        out_specs=(VM,) * 6 + (ANY,),
        scratch_shapes=[pltpu.SemaphoreType.DMA] + gather_sems(C) + plane_sum_scratch(C, blocks),
        compiler_params=comm_params(number, 48),
        cost_estimate=cost_of(18),
        name="project",
    )(x, w, gains, cosine, sine, lines)


def project_back_kernel(
    C, dq_ref, dk_ref, dv_ref, rq_ref, rk_ref, total, gain_ref, cos_ref, sin_ref, known_ref, deal_ref,
    out_ref, sum_ref, dealt_ref, deal_sent, deal_came, deal_own, term_ref, own_terms, all_terms, terms_sent, terms_came,
    eq, ek, inner, stats, landing, sent, came,
):
    greet([device for _, device in plane_peers(C)])
    wide = rq_ref.shape[1]
    width = wide * 2 * C
    blocks = stats.shape[0]

    def rows_at(block):
        return pl.ds(pl.multiple_of(block * ROWS, ROWS), ROWS)

    Z, shard, _ = dealt_ref.shape
    dp, ctx, _ = places_of()
    line = dp - lax.rem(dp, 2)
    seat = place_in_plane(C, (dp, ctx))

    def deal(number):
        at = seat * Z + number
        to = lax.rem(at, 2 * C)
        source, target = deal_ref.at[pl.ds(number * shard, shard)], dealt_ref.at[lax.div(at, 2 * C)]
        device = line + lax.div(to, C), lax.rem(to, C)
        away = remote(source, target, deal_sent.at[number], deal_came.at[lax.div(at, 2 * C)], device)
        return to, away, pltpu.make_async_copy(source, target, deal_own.at[number])

    for number in range(Z):
        to, away, stay = deal(number)

        @pl.when(to != seat)
        def _():
            away.start()

        @pl.when(to == seat)
        def _():
            stay.start()

    def factors_of(block):
        return columns_of(lax.rsqrt(total[block] * (1.0 / width) + EPS))

    term_ref[...] = jnp.zeros_like(term_ref)

    @pl.loop(0, blocks)
    def _(block):
        here = rows_at(block)
        factors = factors_of(block)
        cosine, sine = cos_ref[here, :], sin_ref[here, :]
        sums = []
        for which, (grad, raw, kept) in enumerate(((dq_ref, rq_ref, eq), (dk_ref, rk_ref, ek))):
            for head in range(wide // HD):
                lanes = slice(head * HD, (head + 1) * HD)
                kept[here, lanes] = turned(grad[here, lanes], cosine, -sine)
            product = kept[here, :] * raw[here, :] * factors[:, which : which + 1]
            term_ref[which : which + 1, :] += jnp.sum(product, axis=0, keepdims=True)
            sums.append(row_of_sums(product * gain_ref[which : which + 1, :]))
        stats[block] = pair_of_rows(*sums)

    start_sum(C, stats, landing, sent, came)
    lanes = pl.ds(pl.multiple_of(seat * wide, 128), wide)
    own_terms[...] = known_ref[...]
    own_terms[:, lanes] = own_terms[:, lanes] + term_ref[...]
    for index, device in plane_peers(C):
        remote(
            own_terms, all_terms.at[index], terms_sent.at[index], terms_came.at[index], device
        ).start()
    finish_sum(C, stats, landing, sent, came, inner)

    @pl.loop(0, blocks)
    def _(block):
        here = rows_at(block)
        factors = factors_of(block)
        means = columns_of(inner[block] * (1.0 / width))
        for which, (kept, raw) in enumerate(((eq, rq_ref), (ek, rk_ref))):
            factor, mean = factors[:, which : which + 1], means[:, which : which + 1]
            weighted = kept[here, :] * gain_ref[which : which + 1, :]
            value = factor * (weighted - raw[here, :] * factor * mean)
            out_ref[here, which * wide : (which + 1) * wide] = value.astype(BF16)
        out_ref[here, 2 * wide :] = dv_ref[here, :].astype(BF16)

    terms = own_terms[...]
    for index, device in plane_peers(C):
        remote(
            own_terms, all_terms.at[index], terms_sent.at[index], terms_came.at[index], device
        ).wait()
        terms = terms + all_terms[index]
    sum_ref[...] = terms
    for number in range(Z):
        to, away, stay = deal(number)

        @pl.when(to != seat)
        def _():
            away.wait_send()

        @pl.when(to == seat)
        def _():
            stay.wait()

    for number in range(Z):
        origin = lax.div(number * 2 * C + seat, Z)
        spot = dealt_ref.at[number]
        device = line + lax.div(origin, C), lax.rem(origin, C)

        @pl.when(origin != seat)
        def _():
            remote(spot, spot, deal_sent.at[number], deal_came.at[number], device).wait_recv()


def project_back(dq, dk, dv, raw_q, raw_k, sums, gains, cosine, sine, terms, dealt, C, Z, number):
    total, wide = dq.shape
    blocks = total // ROWS
    return pl.pallas_call(
        functools.partial(project_back_kernel, C),
        out_shape=(
            jax.ShapeDtypeStruct((total, 3 * wide), BF16),
            jax.ShapeDtypeStruct(terms.shape, F32),
            jax.ShapeDtypeStruct((Z, dealt.shape[0] // Z, dealt.shape[1]), BF16),
        ),
        in_specs=[VM] * 10 + [ANY],
        out_specs=(VM, VM, ANY),
        scratch_shapes=[
            pltpu.SemaphoreType.DMA((Z,)),
            pltpu.SemaphoreType.DMA((Z,)),
            pltpu.SemaphoreType.DMA((Z,)),
            pltpu.VMEM((8, wide), F32),
            pltpu.VMEM(terms.shape, F32),
            pltpu.VMEM((2 * C,) + terms.shape, F32),
            pltpu.SemaphoreType.DMA((2 * C,)),
            pltpu.SemaphoreType.DMA((2 * C,)),
            pltpu.VMEM((total, wide), F32),
            pltpu.VMEM((total, wide), F32),
            pltpu.VMEM((blocks, 8, ROWS), F32),
        ]
        + plane_sum_scratch(C, blocks),
        compiler_params=comm_params(number, 48),
        cost_estimate=cost_of(15),
        name="project_back",
    )(dq, dk, dv, raw_q, raw_k, sums, gains, cosine, sine, terms, dealt)


def attention_out_kernel(
    C, attended_ref, w_ref, tokens_ref, gain_ref, heads, proj, hidden_ref, h_out,
    low, own_sem, part_sent, part_came, copy_sem, *sems,
):
    count, width = tokens_ref.shape
    wide = width // (2 * C)
    dp, ctx, _ = places_of()
    here = place_in_plane(C, (dp, ctx))
    peers = plane_peers(C)
    greet([device for _, device in peers])

    def columns(at):
        return heads.at[:, pl.ds(pl.multiple_of(at * wide, 128), wide)]

    own = pltpu.make_async_copy(attended_ref.at[pl.ds(ctx * count, count)], columns(here), own_sem)
    own.start()
    copies = []
    for index, device in peers:
        rows = pl.ds(index // C * (C * count) + device[1] * count, count)
        copy = remote(
            attended_ref.at[rows], columns(here), part_sent.at[index], part_came.at[index], device
        )
        copy.start()
        copies.append(copy)
    own.wait()
    for index, device in peers:
        spot = columns(place_in_plane(C, device))
        remote(spot, spot, part_sent.at[index], part_came.at[index], device).wait_recv()
    for copy in copies:
        copy.wait_send()
    outs, size = tiles(width, 512)

    @pl.loop(0, outs)
    def _(number):
        lanes = at_tile(number, size)
        proj[:, lanes] = dot(heads[...], w_ref[:, lanes], 1, 0)

    chunks, chunk = tiles(count, 32)
    gain = gain_ref[0:1, :]

    @pl.loop(0, chunks)
    def _(number):
        rows = at_tile(number, chunk)
        value = proj[rows, :]
        factor = lax.rsqrt(jnp.mean(value * value, axis=-1, keepdims=True) + EPS)
        hidden = tokens_ref[rows, :].astype(F32) + value * factor * gain
        hidden_ref[rows, :] = hidden
        low[rows, :] = hidden.astype(BF16)

    gather = rows_gather(C, low, h_out, sems)
    copy = pltpu.make_async_copy(low, h_out.at[0, pl.ds(ctx * count, count)], copy_sem)
    for index in range(C):
        gather.step(index)
        if index == 0:
            copy.start()
    copy.wait()
    gather.finish()


def attention_out(attended, w, tokens, gain, C, number):
    count, width = tokens.shape
    whole = jax.ShapeDtypeStruct((count, width), F32)
    return pl.pallas_call(
        functools.partial(attention_out_kernel, C),
        out_shape=(
            jax.ShapeDtypeStruct((count, width), BF16),
            whole,
            whole,
            jax.ShapeDtypeStruct((2, C * count, width), BF16),
        ),
        in_specs=[VM] * 4,
        out_specs=(VM, VM, VM, ANY),
        scratch_shapes=[
            pltpu.VMEM((count, width), BF16),
            pltpu.SemaphoreType.DMA,
            pltpu.SemaphoreType.DMA((2 * C,)),
            pltpu.SemaphoreType.DMA((2 * C,)),
            pltpu.SemaphoreType.DMA,
        ]
        + gather_sems(C),
        compiler_params=comm_params(number, 60),
        cost_estimate=cost_of(60),
        name="attention_out",
    )(attended, w, tokens, gain)


def return_kernel(C, groups, blocks, x_ref, *refs):
    outs, (landing, sent, came, own_sem) = refs[:groups], refs[groups:]
    A = 2 * C
    shard = outs[0].shape[0]
    part = outs[0].shape[1] // (blocks * A)
    wide = groups * blocks * part
    dp, ctx, _ = places_of()
    own_at = place_in_plane(C, (dp, ctx))
    peers = plane_peers(C)
    greet([device for _, device in peers])
    own = pltpu.make_async_copy(
        x_ref.at[pl.ds(own_at * shard, shard), pl.ds(0, wide)], landing.at[own_at], own_sem
    )
    own.start()

    def copy_to(index, device):
        rows = pl.ds(place_in_plane(C, device) * shard, shard)
        return remote(
            x_ref.at[rows, pl.ds(0, wide)],
            landing.at[own_at],
            sent.at[index],
            came.at[index],
            device,
        )

    def landed(index, device):
        spot = landing.at[place_in_plane(C, device)]
        remote(spot, spot, sent.at[index], came.at[index], device).wait_recv()

    for index, device in peers:
        copy_to(index, device).start()
    own.wait()
    for index, device in peers:
        landed(index, device)
    for index, device in peers:
        copy_to(index, device).wait_send()
    for group in range(groups):
        for block in range(blocks):
            for at in range(A):
                lanes = (group * blocks + block) * part
                to = (block * A + at) * part
                outs[group][:, to : to + part] = landing[at, :, lanes : lanes + part]


def return_rows(x, wide, C, groups, blocks, number):
    A = 2 * C
    shard = x.shape[0] // A
    return pl.pallas_call(
        functools.partial(return_kernel, C, groups, blocks),
        out_shape=(jax.ShapeDtypeStruct((shard, wide * A // groups), x.dtype),) * groups,
        in_specs=[ANY],
        out_specs=(VM,) * groups,
        scratch_shapes=[
            pltpu.VMEM((A, shard, wide), x.dtype),
            pltpu.SemaphoreType.DMA((A,)),
            pltpu.SemaphoreType.DMA((A,)),
            pltpu.SemaphoreType.DMA,
        ],
        compiler_params=comm_params(number, 24),
        cost_estimate=cost_of(20),
        name="return_rows",
    )(x)


class Scatter:
    def __init__(self, C, count, own, other, twin_part, landing, sems, final):
        self.C, self.count, self.half = C, count, count // 2
        self.own, self.other, self.twin_part, self.landing = own, other, twin_part, landing
        self.core_sent, self.core_came, self.ctx_sent, self.ctx_came = sems
        self.dp, self.ctx, self.twin = places_of()
        self.onward = [{m: (bits, bit) for m, bits, bit in tree(order)} for order in bit_orders(C)]
        self.final = final

    def rows(self, half, mask):
        return pl.ds(flipped(self.ctx, mask) * self.count + half * self.half, self.half)

    def block(self, mask):
        return pl.ds(flipped(self.ctx, mask) * self.count, self.count)

    def across(self, half, mask):
        return remote(
            self.other.at[self.rows(half, mask)],
            self.twin_part.at[self.rows(half, mask)],
            self.core_sent.at[half, mask],
            self.core_came.at[half, mask],
            (self.twin, self.ctx),
        )

    def back(self, half, mask, bit):
        return remote(
            self.own.at[self.rows(half, mask)],
            self.landing.at[half, mask],
            self.ctx_sent.at[half, mask],
            self.ctx_came.at[half, mask],
            (self.dp, flipped(self.ctx, bit)),
        )

    def settle(self, half, mask):
        along, bit = self.onward[half][mask]
        self.across(half, mask).wait_recv()
        here = self.rows(half, mask)
        total = self.own[here, :].astype(F32) + self.twin_part[here, :].astype(F32)
        for came in along:
            self.back(half, mask | came, came).wait_recv()
            total = total + self.landing[half, mask | came].astype(F32)
        if mask:
            self.own[here, :] = total.astype(BF16)
            self.back(half, mask, bit).start()
        else:
            self.final(half, total)

    def order(self):
        return sorted(range(self.C), key=lambda mask: (-bin(mask).count("1"), mask))

    def run(self, compute):
        waiting = []
        for mask in self.order():
            compute(1, mask)
            for half in range(2):
                self.across(half, mask).start()
            compute(0, mask)
            ready = [half for half in range(2) if mask and not self.onward[half][mask][0]]
            for half in ready:
                self.settle(half, mask)
            for half, earlier in waiting:
                self.settle(half, earlier)
            waiting = [(half, mask) for half in range(2) if half not in ready]
        for half, earlier in waiting:
            self.settle(half, earlier)
        for half in range(2):
            for mask in range(self.C):
                self.across(half, mask).wait_send()
                if mask:
                    self.back(half, mask, self.onward[half][mask][1]).wait_send()


def scatter_scratch(C, count, width):
    rows = pltpu.VMEM((C * count, width), BF16)
    return [rows, rows, rows, pltpu.VMEM((2, C, count // 2, width), BF16)] + [
        pltpu.SemaphoreType.DMA((2, C))
    ] * 4


def tiles(total, size):
    size = min(total, size)
    return total // size, size


def at_tile(number, size, base=0):
    return pl.ds(pl.multiple_of(base + number * size, size), size)


def mix_kernel(h_ref, wgu_ref, gu_ref, mixed_ref, turned_ref):
    ffn = mixed_ref.shape[1]
    steps, tile = tiles(ffn, 256)
    for number in range(steps):
        first = slice(number * tile, (number + 1) * tile)
        second = slice(ffn + number * tile, ffn + (number + 1) * tile)
        gate = dot(h_ref[...], wgu_ref[:, first], 1, 0)
        up = dot(h_ref[...], wgu_ref[:, second], 1, 0)
        gu_ref[:, first] = gate.astype(BF16)
        gu_ref[:, second] = up.astype(BF16)
        mixed = gate * jax.nn.sigmoid(gate) * up
        mixed_ref[:, first] = mixed.astype(BF16)
        turned_ref[first, :] = mixed.T.astype(BF16)


def mix(h, w_gate_up):
    total, width = h.shape
    ffn = w_gate_up.shape[1] // 2
    rows = min(256, total)
    return pl.pallas_call(
        mix_kernel,
        out_shape=(
            jax.ShapeDtypeStruct((total, 2 * ffn), BF16),
            jax.ShapeDtypeStruct((total, ffn), BF16),
            jax.ShapeDtypeStruct((ffn, total), BF16),
        ),
        grid=(total // rows,),
        in_specs=[
            pl.BlockSpec((rows, width), lambda i: (i, 0)),
            pl.BlockSpec((width, 2 * ffn), lambda i: (0, 0)),
        ],
        out_specs=(
            pl.BlockSpec((rows, 2 * ffn), lambda i: (i, 0)),
            pl.BlockSpec((rows, ffn), lambda i: (i, 0)),
            pl.BlockSpec((ffn, rows), lambda i: (0, i)),
        ),
        compiler_params=pltpu.CompilerParams(vmem_limit_bytes=60 * 2**20),
        cost_estimate=cost_of(20),
        name="mix",
    )(h, w_gate_up)


def feed_forward_kernel(
    C, mixed_ref, turned_ref, gu_ref, first_wd, second_wd, hidden_in, cot_in, gain_ref,
    out_hbm, b_out, down_hbm, term_ref,
    wd_ref, hidden_ref, cot_ref, out_ref,
    mixed_buf, proj, f_own, f_all, turned_buf, gu_buf, b_buf, total,
    mixed_sem, turned_sem, gu_sem, b_sem, down_sem, load_sem,
    ctx_sent, ctx_came, core_sent, core_came,
    own, other, twin_part, landing, *sems,
):
    split = first_wd.shape[1]
    loads = [
        pltpu.make_async_copy(first_wd, wd_ref.at[:, pl.ds(0, split)], load_sem.at[0]),
        pltpu.make_async_copy(
            second_wd, wd_ref.at[:, pl.ds(split, second_wd.shape[1])], load_sem.at[1]
        ),
        pltpu.make_async_copy(hidden_in, hidden_ref, load_sem.at[2]),
        pltpu.make_async_copy(cot_in, cot_ref, load_sem.at[3]),
    ]
    for load in loads:
        load.start()
    greet(plane_neighbours(C))
    count, width = hidden_ref.shape
    ffn = wd_ref.shape[0]
    seq = C * count
    half_rows = count // 2

    def final(half, value):
        proj[pl.ds(half * half_rows, half_rows), :] = value

    scatter = Scatter(C, count, own, other, twin_part, landing, sems, final)
    sequence = [(side, mask) for mask in scatter.order() for side in (1, 0)]

    def rows_of(side, mask):
        return pl.ds(pl.multiple_of(side * seq + flipped(scatter.ctx, mask) * count, count), count)

    def fetch(index):
        return pltpu.make_async_copy(
            mixed_ref.at[rows_of(*sequence[index])], mixed_buf.at[index % 2], mixed_sem.at[index % 2]
        )

    fetch(0).start()
    steps, tile = tiles(ffn, 256)
    outs, wide = tiles(width, 512)

    def compute(side, mask):
        index = sequence.index((side, mask))
        slot = index % 2
        fetch(index).wait()
        if index + 1 < len(sequence):
            fetch(index + 1).start()
        target, here = (own, other)[side], scatter.block(mask)

        @pl.loop(0, outs)
        def _(number):
            lanes = at_tile(number, wide)
            target[here, lanes] = dot(mixed_buf[slot], wd_ref[:, lanes], 1, 0).astype(BF16)

    for load in loads[:2]:
        load.wait()
    scatter.run(compute)
    for load in loads[2:]:
        load.wait()
    gain = gain_ref[0:1, :]
    term_ref[...] = jnp.zeros_like(term_ref)
    chunks, chunk = tiles(count, 32)

    @pl.loop(0, chunks)
    def _(number):
        here = at_tile(number, chunk)
        value = proj[here, :]
        factor = lax.rsqrt(jnp.mean(value * value, axis=-1, keepdims=True) + EPS)
        unit = value * factor
        out_ref[here, :] = hidden_ref[here, :] + unit * gain
        incoming = cot_ref[here, :].astype(F32)
        weighted = incoming * gain
        inner = jnp.mean(weighted * unit, axis=-1, keepdims=True)
        f_own[here, :] = (factor * (weighted - unit * inner)).astype(BF16)
        term_ref[0:1, :] += jnp.sum(incoming * unit, axis=0, keepdims=True)

    gather = rows_gather(C, f_own, f_all, (ctx_sent, ctx_came, core_sent, core_came))
    output = pltpu.make_async_copy(out_ref, out_hbm, load_sem.at[4])
    blocks = [
        (side, mask, index)
        for index in range(C)
        for mask in gather.complete(index)
        for side in (0, 1)
    ]

    def fetch_kept(number):
        side, mask, _ = blocks[number]
        slot, rows = number % 2, rows_of(side, mask)
        return (
            pltpu.make_async_copy(turned_ref.at[:, rows], turned_buf.at[slot], turned_sem.at[slot]),
            pltpu.make_async_copy(gu_ref.at[rows], gu_buf.at[slot], gu_sem.at[slot]),
        )

    def keep(number):
        side, mask, _ = blocks[number]
        return pltpu.make_async_copy(
            b_buf.at[number % 2], b_out.at[rows_of(side, mask)], b_sem.at[number % 2]
        )

    def sum_out(at):
        lanes = pl.ds(at * wide, wide)
        rows = pl.ds(0, ffn)
        return pltpu.make_async_copy(
            other.at[rows, lanes], down_hbm.at[:, lanes], down_sem.at[at]
        )

    def back(number, grads):
        slot = number % 2
        for arrived in fetch_kept(number):
            arrived.wait()
        if number >= 2:
            keep(number - 2).wait()

        @pl.loop(0, steps)
        def _(at):
            first, second = at_tile(at, tile), at_tile(at, tile, ffn)
            grad = dot(grads[...], wd_ref[first, :], 1, 1)
            gate, up = gu_buf[slot, :, first].astype(F32), gu_buf[slot, :, second].astype(F32)
            sig = jax.nn.sigmoid(gate)
            b_buf[slot, :, first] = (grad * up * sig * (1.0 + gate * (1.0 - sig))).astype(BF16)
            b_buf[slot, :, second] = (grad * (gate * sig)).astype(BF16)

        keep(number).start()

        if number < len(blocks) - 1:

            @pl.loop(0, outs)
            def _(at):
                lanes = at_tile(at, wide)
                value = dot(turned_buf[slot], grads[:, lanes], 1, 0)
                if number == 0:
                    total[:, lanes] = value
                else:
                    total[:, lanes] += value

        else:
            for at in range(outs):
                lanes = slice(at * wide, (at + 1) * wide)
                value = dot(turned_buf[slot], grads[:, lanes], 1, 0)
                other[0:ffn, lanes] = (total[:, lanes] + value).astype(BF16)
                sum_out(at).start()

    for arriving in fetch_kept(0):
        arriving.start()
    done = 0
    for index in range(C):
        gather.step(index)
        if index == 0:
            output.start()
        while done < len(blocks) and blocks[done][2] == index:
            side, mask, _ = blocks[done]
            if done + 1 < len(blocks):
                for arriving in fetch_kept(done + 1):
                    arriving.start()
            if (side, mask) == (0, 0):
                back(done, f_own)
            else:
                if side:
                    for half in range(2):
                        gather.crossed(half, mask)
                back(done, f_all.at[side, scatter.block(mask)])
            done += 1
    for number in (len(blocks) - 2, len(blocks) - 1):
        keep(number).wait()
    for at in range(outs):
        sum_out(at).wait()
    output.wait()
    gather.sent()


def feed_forward(mixed, turned_units, gate_up, w_down, hidden, cotangent, gain, C, number):
    count, width = hidden.shape
    total, ffn = 2 * C * count, w_down[0].shape[0]
    pair = pltpu.SemaphoreType.DMA((2,))
    return pl.pallas_call(
        functools.partial(feed_forward_kernel, C),
        out_shape=(
            jax.ShapeDtypeStruct((count, width), F32),
            jax.ShapeDtypeStruct((total, 2 * ffn), BF16),
            jax.ShapeDtypeStruct((ffn, width), BF16),
            jax.ShapeDtypeStruct((8, width), F32),
        ),
        in_specs=[ANY] * 7 + [VM],
        out_specs=(ANY, ANY, ANY, VM),
        scratch_shapes=[
            pltpu.VMEM((ffn, width), BF16),
            pltpu.VMEM((count, width), F32),
            pltpu.VMEM((count, width), BF16),
            pltpu.VMEM((count, width), F32),
            pltpu.VMEM((2, count, ffn), BF16),
            pltpu.VMEM((count, width), F32),
            pltpu.VMEM((count, width), BF16),
            pltpu.VMEM((2, C * count, width), BF16),
            pltpu.VMEM((2, ffn, count), BF16),
            pltpu.VMEM((2, count, 2 * ffn), BF16),
            pltpu.VMEM((2, count, 2 * ffn), BF16),
            pltpu.VMEM((ffn, width), F32),
            pair,
            pair,
            pair,
            pair,
            pltpu.SemaphoreType.DMA((tiles(width, 512)[0],)),
            pltpu.SemaphoreType.DMA((5,)),
        ]
        + gather_sems(C)
        + scatter_scratch(C, count, width),
        compiler_params=comm_params(number, 60),
        cost_estimate=cost_of(80),
        name="feed_forward",
    )(mixed, turned_units, gate_up, *w_down, hidden, cotangent, gain)


def back_scatter_kernel(
    C, b_ref, w_in, add_in, out_hbm, out_ref, out_sem, w_ref, add_ref, load_sem, b_buf, b_sem,
    own, other, twin_part, landing, *sems,
):
    loads = [
        pltpu.make_async_copy(w_in, w_ref, load_sem.at[0]),
        pltpu.make_async_copy(add_in, add_ref, load_sem.at[1]),
    ]
    for load in loads:
        load.start()
    greet(plane_neighbours(C))
    count, width = out_ref.shape
    seq = C * count
    half_rows = count // 2

    def final(half, total):
        rows = pl.ds(half * half_rows, half_rows)
        out_ref[rows, :] = total + add_ref[rows, :].astype(F32)
        leave(half).start()

    def leave(half):
        rows = pl.ds(half * half_rows, half_rows)
        return pltpu.make_async_copy(out_ref.at[rows], out_hbm.at[rows], out_sem.at[half])

    scatter = Scatter(C, count, own, other, twin_part, landing, sems, final)
    sequence = [(side, mask) for mask in scatter.order() for side in (1, 0)]

    def fetch(index):
        side, mask = sequence[index]
        rows = pl.ds(side * seq + flipped(scatter.ctx, mask) * count, count)
        return pltpu.make_async_copy(b_ref.at[rows], b_buf.at[index % 2], b_sem.at[index % 2])

    fetch(0).start()
    outs, wide = tiles(width, 512)

    def compute(side, mask):
        index = sequence.index((side, mask))
        slot = index % 2
        fetch(index).wait()
        if index + 1 < len(sequence):
            fetch(index + 1).start()
        target, here = (own, other)[side], scatter.block(mask)

        @pl.loop(0, outs)
        def _(number):
            lanes = at_tile(number, wide)
            target[here, lanes] = dot(b_buf[slot], w_ref[lanes, :], 1, 1).astype(BF16)

    for load in loads:
        load.wait()
    scatter.run(compute)
    for half in range(2):
        leave(half).wait()


def back_scatter(b, w, add, C, number):
    count, width = add.shape
    return pl.pallas_call(
        functools.partial(back_scatter_kernel, C),
        out_shape=jax.ShapeDtypeStruct((count, width), F32),
        in_specs=[ANY, ANY, ANY],
        out_specs=ANY,
        scratch_shapes=[
            pltpu.VMEM((count, width), F32),
            pltpu.SemaphoreType.DMA((2,)),
            pltpu.VMEM(w.shape, w.dtype),
            pltpu.VMEM(add.shape, add.dtype),
            pltpu.SemaphoreType.DMA((2,)),
            pltpu.VMEM((2, count, b.shape[1]), BF16),
            pltpu.SemaphoreType.DMA((2,)),
        ]
        + scatter_scratch(C, count, width),
        compiler_params=comm_params(number, 48),
        cost_estimate=cost_of(50),
        name="back_scatter",
    )(b, w, add)


def rope_tables(places):
    half = HD // 2
    frequency = THETA ** (-(jnp.arange(half, dtype=F32) * 2.0) / HD)
    angles = places.astype(F32)[:, None] * frequency[None, :]
    cosine, sine = jnp.cos(angles), jnp.sin(angles)
    return jnp.concatenate([cosine, cosine], axis=1), jnp.concatenate([-sine, sine], axis=1)


def row_norm(tensor):
    factor = lax.rsqrt(jnp.mean(tensor * tensor, axis=-1, keepdims=True) + EPS)
    return tensor * factor, factor


def row_norm_back(unit, factor, gain, incoming):
    weighted = incoming * gain
    inner = jnp.mean(weighted * unit, axis=-1, keepdims=True)
    return factor * (weighted - unit * inner), jnp.sum(incoming * unit, axis=0)


def layer(
    ctx_size,
    dp_size,
    tokens,
    w_query,
    w_key,
    w_value,
    w_out,
    gain_query,
    gain_key,
    gain_attn,
    w_gate,
    w_up,
    w_down,
    gain_ffn,
    positions,
    image_starts,
    cotangent,
):
    C, Z = ctx_size, dp_size // 2
    A = 2 * C
    N = Z * A
    ctx, dp = lax.axis_index("ctx"), lax.axis_index("dp")
    core, z = lax.rem(dp, 2), lax.div(dp, 2)
    plane_at = core * C + ctx
    own_at = dp * C + ctx
    rows, width = tokens.shape
    ffn_width = w_gate.shape[1]
    shard = w_query.shape[0]
    down_shard = w_down.shape[0]
    seq_len = rows * C
    slice_width = width // A
    ffn_slice = ffn_width // A
    planes = [[zz * A + p for p in range(A)] for zz in range(Z)]
    columns = [[zz * 2 + k for zz in range(Z)] for k in range(2)]

    def swap(x, bit):
        return lax.ppermute(x, AXES, [(i, i ^ bit) for i in range(N)])

    def rows_of(x, at, count):
        return lax.dynamic_slice_in_dim(x, at, count, 0)

    def gather_z_aside(x):
        return lax.all_gather(x, "dp", axis=0, tiled=True, axis_index_groups=columns)

    def scatter_z_aside(x):
        return lax.psum_scatter(
            x, "dp", scatter_dimension=0, tiled=True, axis_index_groups=columns
        )

    def exchange(x):
        return lax.all_to_all(x, AXES, 0, 0, tiled=True, axis_index_groups=planes)

    split = width * 3 // 4
    first_down = gather_z_aside(w_down[:, :split])
    part = down_shard
    dealt = part % 128 == 0
    gains = jnp.stack([gain_query, gain_key, gain_attn, gain_ffn])
    gains = jnp.pad(gains, ((0, 12), (0, -shard % 128)))
    x_both, full_qkv, out_lines, _, all_gains, *gate_up = first_gather(
        tokens, w_query, w_key, w_value, w_out, gains, w_gate, w_up, dealt, C, Z, 1
    )
    if dealt:
        gate_up = gate_up[0]
    else:
        gate_up = jnp.stack([w.reshape(shard, Z, A, part) for w in (w_gate, w_up)], axis=1)
        gate_up = exchange(gate_up.transpose(3, 0, 1, 2, 4).reshape(A * shard, 2 * ffn_slice))
    second_down = w_down[:, split:]
    full_qkv, gate_up, first_down, second_down = lax.optimization_barrier(
        (full_qkv, gate_up, first_down, second_down)
    )
    full_gate_up = gather_z_aside(gate_up)
    all_gains = all_gains[:, :, :4, :shard].astype(F32).transpose(2, 0, 1, 3).reshape(4, width)
    head_gains = lax.dynamic_slice(all_gains, (0, plane_at * slice_width), (2, slice_width))
    head_gains = jnp.pad(head_gains, ((0, 6), (0, 0)))
    gain_a, gain_f = all_gains[2:3], all_gains[3:4]

    x_all = x_both.reshape(2 * seq_len, width)
    other_dp = dp + 1 - 2 * core
    places = jnp.concatenate(
        [rows_of(positions, dp * seq_len, seq_len), rows_of(positions, other_dp * seq_len, seq_len)]
    )
    starts = jnp.concatenate([rows_of(image_starts, dp, 1), rows_of(image_starts, other_dp, 1)])
    start_rows = jnp.repeat(starts, seq_len, axis=0)
    inside = (places[:, None] >= start_rows) & (places[:, None] < start_rows + IMG)
    limits = jnp.max(jnp.where(inside, start_rows + (IMG - 1), places[:, None]), axis=1)
    limit_column = limits[:, None]
    place_rows = places.reshape(2, 1, seq_len)
    cosine, sine = rope_tables(places)
    raw_q, raw_k, value, query_turned, key_turned, squares, full_out = project(
        x_all, full_qkv, head_gains, cosine, sine, out_lines, C, 8
    )
    full_out = full_out.reshape(width, width)
    attended = attend(query_turned, key_turned, value, limit_column, place_rows, seq_len)
    attended_own, attn_proj, hidden, h_both = attention_out(
        attended, full_out, tokens, jnp.pad(gain_a, ((0, 7), (0, 0))), C, 2
    )

    h_all = h_both.reshape(2 * seq_len, width)
    full_gate_up, second_down, h_all = lax.optimization_barrier((full_gate_up, second_down, h_all))
    second_down = gather_z_aside(second_down)
    gate_up_low, mixed, turned_units = mix(h_all, full_gate_up)
    output, b_all, term_down, term_gain_ffn = feed_forward(
        mixed, turned_units, gate_up_low, (first_down, second_down), hidden, cotangent,
        jnp.pad(gain_f, ((0, 7), (0, 0))), C, 3,
    )

    term_down, b_all = lax.optimization_barrier((term_down, b_all))
    grad_w_down = scatter_z_aside(term_down)
    grad_hidden = back_scatter(b_all, full_gate_up, cotangent, C, 5)
    term_gate_up = dot(h_all, b_all, 0, 0, BF16)
    term_gate_up, grad_hidden, grad_w_down = lax.optimization_barrier(
        (term_gate_up, grad_hidden, grad_w_down)
    )
    grad_gate_up = scatter_z_aside(term_gate_up)

    attn_unit, attn_factor = row_norm(attn_proj)
    grad_attn, term_gain_attn = row_norm_back(attn_unit, attn_factor, gain_a, grad_hidden)
    a_all = gather_rows(grad_attn.astype(BF16), C, 7).reshape(2 * seq_len, width)
    grad_attended = dot(
        a_all, rows_of(full_out, plane_at * slice_width, slice_width), 1, 1, BF16
    )
    term_out = dot(attended, a_all, 0, 0, BF16)
    grad_q, grad_k, grad_v = attend_back(
        query_turned, key_turned, value, grad_attended, limit_column, place_rows, seq_len
    )
    known = jnp.concatenate(
        [jnp.zeros((2, width), F32), term_gain_attn[None], term_gain_ffn[:1], jnp.zeros((4, width), F32)]
    )
    grad_raw, gain_terms, term_out = project_back(
        grad_q, grad_k, grad_v, raw_q, raw_k, squares, head_gains, cosine, sine, known, term_out,
        C, Z, 9,
    )
    term_qkv = dot(x_all, grad_raw, 0, 0, BF16)
    last = jnp.concatenate([term_qkv, term_out.reshape(width, slice_width)], axis=1)
    last, grad_raw, grad_gate_up, gain_terms, output, grad_w_down = lax.optimization_barrier(
        (last, grad_raw, grad_gate_up, gain_terms, output.astype(BF16), grad_w_down.astype(F32))
    )
    last = scatter_z_aside(last)
    if dealt:
        grad_gate_up = return_rows(grad_gate_up, 2 * ffn_slice, C, 2, Z, 10)
    else:
        grad_gate_up = (
            exchange(grad_gate_up)
            .reshape(A, shard, 2, Z, part)
            .transpose(2, 1, 3, 0, 4)
            .reshape(2, shard, ffn_width)
        )
    gain_terms = gain_terms[:4]
    gain_terms = gain_terms + swap(gain_terms, A)
    *grad_gate_up, gain_terms, grad_raw = lax.optimization_barrier(
        (grad_gate_up[0].astype(F32), grad_gate_up[1].astype(F32), gain_terms, grad_raw)
    )
    for power in range(1, Z.bit_length() - 1):
        gain_terms = gain_terms + swap(gain_terms, A << power)
    grad_input = back_scatter(grad_raw, full_qkv, grad_hidden, C, 6)
    last, grad_input = lax.optimization_barrier((last, grad_input))
    grad_qkv = return_rows(last, 3 * slice_width, C, 3, 1, 11)
    grad_w_out = last[:, 3 * slice_width :]
    gain_sums = lax.dynamic_slice(gain_terms, (0, own_at * shard), (4, shard))

    return (
        output,
        grad_input,
        grad_qkv[0].astype(F32),
        grad_qkv[1].astype(F32),
        grad_qkv[2].astype(F32),
        grad_w_out.reshape(shard, width).astype(F32),
        gain_sums[0],
        gain_sums[1],
        gain_sums[2],
        grad_gate_up[0],
        grad_gate_up[1],
        grad_w_down,
        gain_sums[3],
    )


def solution(mesh):
    split, line, copied = P(AXES, None), P(AXES), P()
    return jax.shard_map(
        functools.partial(layer, mesh.shape["ctx"], mesh.shape["dp"]),
        mesh=mesh,
        in_specs=(split,) * 5 + (line,) * 3 + (split,) * 3 + (line, copied, copied, split),
        out_specs=(split,) * 6 + (line,) * 3 + (split,) * 3 + (line,),
        check_vma=False,
    )
```

```python
import functools
import math

import jax
import jax.numpy as jnp
from jax import lax
from jax.experimental import pallas as pl
from jax.experimental.pallas import tpu as pltpu
from jax.sharding import PartitionSpec as P

HD = 128
IMG = 256
EPS = 1e-06
THETA = 500000.0
NEG = -1e30
AXES = ("dp", "ctx")
F32 = jnp.float32
BF16 = jnp.bfloat16
SCALE = 1.0 / math.sqrt(HD)
LOG2E = math.log2(math.e)


def dot(left, right, left_dim, right_dim, kind=F32):
    return lax.dot_general(
        left, right, (((left_dim,), (right_dim,)), ((), ())), preferred_element_type=kind
    )


def probs_of(q, k, limit, places):
    scores = dot(q, k, 1, 1)
    scores = jnp.where(places <= limit, scores, NEG)
    peak = jnp.max(scores, axis=-1, keepdims=True)
    weights = jnp.exp2((scores - peak) * (SCALE * LOG2E))
    return weights * (1.0 / jnp.sum(weights, axis=-1, keepdims=True))


def attend_kernel(q_ref, k_ref, v_ref, limit_ref, place_ref, out_ref):
    probs = probs_of(q_ref[...], k_ref[...], limit_ref[...], place_ref[0])
    out_ref[...] = dot(probs.astype(BF16), v_ref[...], 1, 0).astype(BF16)


def attend_back_kernel(
    q_ref, k_ref, v_ref, g_ref, limit_ref, place_ref, dq_ref, dk_ref, dv_ref
):
    step = pl.program_id(2)

    @pl.when(step == 0)
    def _():
        dk_ref[...] = jnp.zeros_like(dk_ref)
        dv_ref[...] = jnp.zeros_like(dv_ref)

    q, k, v, g = q_ref[...], k_ref[...], v_ref[...], g_ref[...]
    probs = probs_of(q, k, limit_ref[...], place_ref[0])
    grad_probs = dot(g, v, 1, 1)
    inner = jnp.sum(probs * grad_probs, axis=-1, keepdims=True)
    grad_scores = (probs * (grad_probs - inner)).astype(BF16)
    dq_ref[...] = dot(grad_scores, k, 1, 0) * SCALE
    dk_ref[...] += dot(grad_scores, q, 0, 0) * SCALE
    dv_ref[...] += dot(probs.astype(BF16), g, 0, 0)


def attention_specs(seq_len, rows):
    steps = seq_len // rows
    query = pl.BlockSpec((rows, HD), lambda s, h, i: (s * steps + i, h))
    keys = pl.BlockSpec((seq_len, HD), lambda s, h, i: (s, h))
    limit = pl.BlockSpec((rows, 1), lambda s, h, i: (s * steps + i, 0))
    places = pl.BlockSpec((1, 1, seq_len), lambda s, h, i: (s, 0, 0))
    return query, keys, limit, places


def attend(q, k, v, limits, places, seq_len):
    rows = min(256, seq_len)
    total, width = q.shape
    query, keys, limit, place = attention_specs(seq_len, rows)
    return pl.pallas_call(
        attend_kernel,
        out_shape=jax.ShapeDtypeStruct((total, width), BF16),
        grid=(total // seq_len, width // HD, seq_len // rows),
        in_specs=[query, keys, keys, limit, place],
        out_specs=query,
        compiler_params=pltpu.CompilerParams(vmem_limit_bytes=48 * 2**20),
        cost_estimate=pl.CostEstimate(
            flops=4 * total * seq_len * width,
            bytes_accessed=8 * total * width,
            transcendentals=total * seq_len * (width // HD),
        ),
        name="attend",
    )(q, k, v, limits, places)


def attend_back(q, k, v, g, limits, places, seq_len):
    rows = min(256, seq_len)
    total, width = q.shape
    query, keys, limit, place = attention_specs(seq_len, rows)
    shape = jax.ShapeDtypeStruct((total, width), F32)
    return pl.pallas_call(
        attend_back_kernel,
        out_shape=(shape, shape, shape),
        grid=(total // seq_len, width // HD, seq_len // rows),
        in_specs=[query, keys, keys, query, limit, place],
        out_specs=(query, keys, keys),
        compiler_params=pltpu.CompilerParams(vmem_limit_bytes=48 * 2**20),
        cost_estimate=pl.CostEstimate(
            flops=10 * total * seq_len * width,
            bytes_accessed=20 * total * width,
            transcendentals=total * seq_len * (width // HD),
        ),
        name="attend_back",
    )(q, k, v, g, limits, places)


MESH = pl.DeviceIdType.MESH
ANY = pl.BlockSpec(memory_space=pl.ANY)


def flipped(at, mask):
    bit = 1
    while bit <= mask:
        if mask & bit:
            at = at + bit - 2 * bit * lax.rem(lax.div(at, bit), 2)
        bit *= 2
    return at


def bit_orders(C):
    bits = [1 << b for b in range(C.bit_length() - 1)]
    return bits, bits[::-1]


def tree(order):
    found = [(0, order, 0)]
    for place, bit in enumerate(order):
        found += [(mask | bit, order[place + 1 :], bit) for mask, _, _ in list(found)]
    return found


def signal_barrier(peers):
    barrier = pltpu.get_barrier_semaphore()
    for peer in peers:
        pl.semaphore_signal(barrier, inc=1, device_id=peer, device_id_type=MESH)
    return barrier


def greet(peers):
    pl.semaphore_wait(signal_barrier(peers), len(peers))


def remote(src, dst, sent, arrived, device):
    return pltpu.make_async_remote_copy(
        src_ref=src, dst_ref=dst, send_sem=sent, recv_sem=arrived, device_id=device, device_id_type=MESH
    )


def places_of():
    dp, ctx = lax.axis_index("dp"), lax.axis_index("ctx")
    return dp, ctx, dp + 1 - 2 * lax.rem(dp, 2)


class Gather:
    def __init__(self, C, source, slot, over, from_over, sems):
        self.C = C
        self.source, self.slot, self.over, self.from_over = source, slot, over, from_over
        self.ctx_sent, self.ctx_came, self.core_sent, self.core_came = sems
        self.dp, self.ctx, self.twin = places_of()
        self.trees = [tree(order) for order in bit_orders(C)]
        self.sends = []

    def held(self, half, mask):
        return self.slot(flipped(self.ctx, mask), half) if mask else self.source(half)

    def by_ctx(self, half, mask, bit):
        return remote(
            self.held(half, mask),
            self.slot(flipped(self.ctx, mask), half),
            self.ctx_sent.at[half, mask | bit],
            self.ctx_came.at[half, mask | bit],
            (self.dp, flipped(self.ctx, bit)),
        )

    def by_core(self, half, mask):
        return remote(
            self.held(half, mask),
            self.over(flipped(self.ctx, mask), half),
            self.core_sent.at[half, mask],
            self.core_came.at[half, mask],
            (self.twin, self.ctx),
        )

    def landed(self, half, mask, bit):
        slot = self.slot(flipped(self.ctx, mask), half)
        remote(
            slot,
            slot,
            self.ctx_sent.at[half, mask],
            self.ctx_came.at[half, mask],
            (self.dp, flipped(self.ctx, bit)),
        ).wait_recv()

    def start(self, copy):
        copy.start()
        self.sends.append(copy)

    def step(self, index):
        for half in range(2):
            mask, onward, bit = self.trees[half][index]
            if mask:
                self.landed(half, mask, bit)
            for further in onward:
                self.start(self.by_ctx(half, mask, further))
            if mask:
                self.start(self.by_core(half, mask))
        if index == 0:
            for half in range(2):
                self.start(self.by_core(half, 0))

    def crossed(self, half, mask):
        slot = self.from_over(flipped(self.ctx, mask), half)
        remote(
            slot,
            slot,
            self.core_sent.at[half, mask],
            self.core_came.at[half, mask],
            (self.twin, self.ctx),
        ).wait_recv()

    def sent(self):
        for copy in self.sends:
            copy.wait_send()

    def finish(self):
        self.sent()
        for half in range(2):
            for mask in range(self.C):
                self.crossed(half, mask)

    def complete(self, index):
        place = [{m: at for at, (m, _, _) in enumerate(tree)} for tree in self.trees]
        return [m for m in range(self.C) if max(place[0][m], place[1][m]) == index]


def rows_gather(C, x_ref, out_ref, sems):
    count = x_ref.shape[0]
    size = count // 2

    def rows(seat, half):
        return pl.ds(seat * count + half * size, size)

    return Gather(
        C,
        lambda half: x_ref.at[pl.ds(half * size, size)],
        lambda seat, half: out_ref.at[0, rows(seat, half)],
        lambda seat, half: out_ref.at[1, rows(seat, half)],
        lambda seat, half: out_ref.at[1, rows(seat, half)],
        sems,
    )


class Ring:
    def __init__(self, Z, block, sent, came, way=1):
        dp, ctx, _ = places_of()
        self.Z, self.z, self.block, self.sems, self.way = Z, lax.div(dp, 2), block, (sent, came), way
        self.ahead = lax.rem(dp + 2 * Z + 2 * way, 2 * Z), ctx
        self.behind = lax.rem(dp + 2 * Z - 2 * way, 2 * Z), ctx

    def hop(self, step):
        spot = self.block(lax.rem(self.z + self.Z - self.way * step, self.Z))
        return remote(spot, spot, self.sems[0].at[step], self.sems[1].at[step], self.ahead)

    def landed(self, step):
        spot = self.block(lax.rem(self.z + 2 * self.Z - self.way * (1 + step), self.Z))
        remote(spot, spot, self.sems[0].at[step], self.sems[1].at[step], self.behind).wait_recv()

    def sent(self):
        for step in range(self.Z - 1):
            self.hop(step).wait_send()


def lines_gather(C, line_ref, out_ref, sems):
    dp, ctx, _ = places_of()
    core = lax.rem(dp, 2)
    size = line_ref.shape[0] // 2

    def slot(side, seat, half):
        return out_ref.at[pl.ds(half * size, size), side * C + seat]

    return Gather(
        C,
        lambda half: line_ref.at[pl.ds(half * size, size)],
        lambda seat, half: slot(core, seat, half),
        lambda seat, half: slot(core, seat, half),
        lambda seat, half: slot(1 - core, seat, half),
        sems,
    )


def gather_sems(C):
    return [pltpu.SemaphoreType.DMA((2, C))] * 4


def plane_neighbours(C):
    dp, ctx, twin = places_of()
    return [(dp, flipped(ctx, bit)) for bit in bit_orders(C)[0]] + [(twin, ctx)]


def comm_params(number, megabytes=16):
    return pltpu.CompilerParams(
        collective_id=number, has_side_effects=True, vmem_limit_bytes=megabytes * 2**20
    )


def cost_of(microseconds):
    return pl.CostEstimate(flops=int(microseconds * 1e6), bytes_accessed=1024, transcendentals=0)


def gather_kernel(C, x_ref, out_ref, own_sem, *sems):
    greet(plane_neighbours(C))
    count = x_ref.shape[0]
    own = pltpu.make_async_copy(
        x_ref, out_ref.at[0, pl.ds(lax.axis_index("ctx") * count, count)], own_sem
    )
    gather = rows_gather(C, x_ref, out_ref, sems)
    for index in range(C):
        gather.step(index)
        if index == 0:
            own.start()
    own.wait()
    gather.finish()


def gather_rows(x, C, number):
    return pl.pallas_call(
        functools.partial(gather_kernel, C),
        out_shape=jax.ShapeDtypeStruct((2, C * x.shape[0], x.shape[1]), x.dtype),
        in_specs=[ANY],
        out_specs=ANY,
        scratch_shapes=[pltpu.SemaphoreType.DMA] + gather_sems(C),
        compiler_params=comm_params(number),
        cost_estimate=cost_of(40),
        name="gather_rows",
    )(x)


def plane_peers(C):
    dp, ctx, twin = places_of()
    peers = [(there, flipped(ctx, mask)) for there in (dp, twin) for mask in range(C)]
    return list(enumerate(peers))[1:]


def place_in_plane(C, device):
    return lax.rem(device[0], 2) * C + device[1]


class Deal:
    def __init__(self, C, weights, wide, blocks, out_ref, row_at, sent, came, own_sem):
        self.C, self.out, self.wide, self.sems = C, out_ref, wide, (sent, came, own_sem)
        self.peers, self.row_at = plane_peers(C), row_at
        self.shard = weights[0].shape[0]
        dp, ctx, _ = places_of()
        self.parts = []
        for weight in weights:
            for block in range(blocks):
                self.parts.append((weight, block * 2 * C))
        self.own_device = (dp, ctx)
        self.copies = []

    def spot(self, device, number):
        rows = pl.ds(self.row_at(device), self.shard)
        return self.out.at[rows, pl.ds(number * self.wide, self.wide)]

    def start(self):
        sent, came, own_sem = self.sems
        for number, (weight, first) in enumerate(self.parts):
            for index, device in [(0, self.own_device)] + self.peers:
                at = (first + place_in_plane(self.C, device)) * self.wide
                source = weight.at[:, pl.ds(pl.multiple_of(at, 128), self.wide)]
                target = self.spot(self.own_device, number)
                if index == 0:
                    copy = pltpu.make_async_copy(source, target, own_sem.at[number])
                else:
                    copy = remote(
                        source, target, sent.at[number, index], came.at[number, index], device
                    )
                copy.start()
                self.copies.append((copy, index))

    def landed(self):
        sent, came, _ = self.sems
        for number in range(len(self.parts)):
            for index, device in self.peers:
                spot = self.spot(device, number)
                remote(
                    spot, spot, sent.at[number, index], came.at[number, index], device
                ).wait_recv()
        for copy, index in self.copies:
            if index:
                copy.wait_send()
            else:
                copy.wait()


def deal_sems(C, parts):
    return [
        pltpu.SemaphoreType.DMA((parts, 2 * C)),
        pltpu.SemaphoreType.DMA((parts, 2 * C)),
        pltpu.SemaphoreType.DMA((parts,)),
    ]


def first_kernel(C, Z, dealt, *refs):
    x_ref, wq_ref, wk_ref, wv_ref, wo_ref, gains_ref = refs[:6]
    refs = refs[6:]
    if dealt:
        (wg_ref, wu_ref), refs = refs[:2], refs[2:]
    x_out, w_out, wo_out, gains_line, gains_out = refs[:5]
    refs = refs[5:]
    if dealt:
        gu_out, refs = refs[0], refs[1:]
    own_sem, ring_sent, ring_came, gather_set, refs = refs[0], refs[1], refs[2], refs[3:7], refs[7:]
    gains_set, deal_set, refs = refs[:4], refs[4:7], refs[7:]
    A = 2 * C
    dp, ctx, _ = places_of()
    z, place = lax.div(dp, 2), lax.rem(dp, 2) * C + ctx
    shard = wq_ref.shape[0]
    rings = [
        Ring(Z, lambda at: gains_line.at[at], ring_sent.at[0], ring_came.at[0]),
        Ring(Z, lambda at: wo_out.at[at], ring_sent.at[1], ring_came.at[1]),
    ]
    size = A * shard // 2
    for half, way in enumerate((1, -1)):
        rings.append(
            Ring(
                Z,
                lambda at, half=half: w_out.at[pl.ds(at * (A * shard) + half * size, size)],
                ring_sent.at[2 + half],
                ring_came.at[2 + half],
                way,
            )
        )
    greet([device for _, device in plane_peers(C)] + [rings[0].ahead, rings[0].behind])
    lines = [
        pltpu.make_async_copy(gains_ref, gains_line.at[z], own_sem.at[0]),
        pltpu.make_async_copy(wo_ref, wo_out.at[z], own_sem.at[1]),
    ]
    for line in lines:
        line.start()
    deal = Deal(
        C, (wq_ref, wk_ref, wv_ref), wq_ref.shape[1] // A, 1, w_out,
        lambda device: (device[0] * C + device[1]) * shard, *deal_set,
    )
    deal.start()
    for line, ring in zip(lines, rings):
        line.wait()
        ring.hop(0).start()
    count = x_ref.shape[0]
    own = pltpu.make_async_copy(x_ref, x_out.at[0, pl.ds(ctx * count, count)], own_sem.at[2])
    own.start()
    gather = rows_gather(C, x_ref, x_out, gather_set)
    gather.step(0)
    deal.landed()
    for ring in rings[2:]:
        ring.hop(0).start()
    if dealt:
        columns = Deal(
            C, (wg_ref, wu_ref), wg_ref.shape[1] // (Z * A), Z, gu_out,
            lambda device: place_in_plane(C, device) * shard, *refs,
        )
        columns.start()
    for step in range(Z - 2):
        for ring in rings:
            ring.landed(step)
            ring.hop(step + 1).start()
        if step + 1 < C:
            gather.step(step + 1)
    for ring in rings[:2]:
        ring.landed(Z - 2)
    own_gains = pltpu.make_async_copy(gains_line, gains_out.at[:, place], own_sem.at[3])
    own_gains.start()
    for index in range(Z - 1, C):
        gather.step(index)
    gains = lines_gather(C, gains_line, gains_out, gains_set)
    for index in range(C):
        gains.step(index)
    if dealt:
        columns.landed()
    own.wait()
    own_gains.wait()
    gather.finish()
    gains.finish()
    for ring in rings[2:]:
        ring.landed(Z - 2)
    for ring in rings:
        ring.sent()


def first_gather(x, w_query, w_key, w_value, w_out, gains, w_gate, w_up, dealt, C, Z, number):
    width = x.shape[1]
    A = 2 * C
    shard = w_query.shape[0]

    def shape(*sizes):
        return jax.ShapeDtypeStruct(sizes, x.dtype)

    outs = [
        shape(2, C * x.shape[0], width),
        shape(width, 3 * width // A),
        shape(Z, shard, width),
        shape(Z, *gains.shape),
        shape(Z, A, *gains.shape),
    ]
    operands = [x, w_query, w_key, w_value, w_out, gains]
    scratch = (
        [pltpu.SemaphoreType.DMA((4,))]
        + [pltpu.SemaphoreType.DMA((4, Z))] * 2
        + gather_sems(C) * 2
        + deal_sems(C, 3)
    )
    if dealt:
        operands += [w_gate, w_up]
        outs.append(shape(A * shard, 2 * w_gate.shape[1] // A))
        scratch += deal_sems(C, 2 * Z)
    return pl.pallas_call(
        functools.partial(first_kernel, C, Z, dealt),
        out_shape=tuple(outs),
        in_specs=[ANY] * len(operands),
        out_specs=(ANY,) * len(outs),
        scratch_shapes=scratch,
        compiler_params=comm_params(number, 60),
        cost_estimate=cost_of(100),
        name="first_gather",
    )(*operands)


ROWS = 256


def row_of_sums(values):
    high = values.astype(BF16)
    rest = (values - high.astype(F32)).astype(BF16)
    ones = jnp.ones((8, values.shape[1]), BF16)
    return dot(ones, high, 1, 1) + dot(ones, rest, 1, 1)


def pair_of_rows(first, second):
    return jnp.where(lax.broadcasted_iota(jnp.int32, first.shape, 0) == 0, first, second)


def columns_of(rows):
    eye = (
        lax.broadcasted_iota(jnp.int32, (8, 8), 0) == lax.broadcasted_iota(jnp.int32, (8, 8), 1)
    ).astype(BF16)
    high = rows.astype(BF16)
    rest = rows - high.astype(F32)
    middle = rest.astype(BF16)
    low = (rest - middle.astype(F32)).astype(BF16)
    return dot(high, eye, 0, 0) + dot(middle, eye, 0, 0) + dot(low, eye, 0, 0)


def start_sum(C, stats, landing, sent, came):
    for index, device in plane_peers(C):
        remote(stats, landing.at[index], sent.at[index], came.at[index], device).start()


def finish_sum(C, stats, landing, sent, came, total):
    blocks = stats.shape[0]
    for index, device in plane_peers(C):
        remote(stats, landing.at[index], sent.at[index], came.at[index], device).wait()
    for block in range(blocks):
        value = stats[block]
        for index in range(1, 2 * C):
            value = value + landing[index, block if index < C else (block + blocks // 2) % blocks]
        total[block] = value


def turned(value, cosine, sine):
    return value * cosine + pltpu.roll(value, HD // 2, 1) * sine


def project_kernel(
    C, x_ref, w_ref, gain_ref, cos_ref, sin_ref, line_ref,
    rq_ref, rk_ref, v_ref, q_ref, k_ref, total, out_ref,
    own_sem, ctx_sent, ctx_came, core_sent, core_came, stats, landing, sent, came,
):
    greet([device for _, device in plane_peers(C)])
    dp, ctx, _ = places_of()
    gather = lines_gather(C, line_ref, out_ref, (ctx_sent, ctx_came, core_sent, core_came))
    own = pltpu.make_async_copy(line_ref, out_ref.at[:, lax.rem(dp, 2) * C + ctx], own_sem)
    own.start()
    gather.step(0)
    wide = rq_ref.shape[1]
    width = x_ref.shape[1]
    blocks = stats.shape[0]

    def rows_at(block):
        return pl.ds(pl.multiple_of(block * ROWS, ROWS), ROWS)

    @pl.loop(0, blocks)
    def _(block):
        here = rows_at(block)
        raw = dot(x_ref[here, :], w_ref[...], 1, 0)
        query, key = raw[:, :wide], raw[:, wide : 2 * wide]
        rq_ref[here, :] = query
        rk_ref[here, :] = key
        v_ref[here, :] = raw[:, 2 * wide :].astype(BF16)
        stats[block] = pair_of_rows(row_of_sums(query * query), row_of_sums(key * key))

    start_sum(C, stats, landing, sent, came)
    finish_sum(C, stats, landing, sent, came, total)
    gather.step(1)

    @pl.loop(0, blocks)
    def _(block):
        here = rows_at(block)
        factors = columns_of(lax.rsqrt(total[block] * (1.0 / width) + EPS))
        cosine, sine = cos_ref[here, :], sin_ref[here, :]
        for which, (raw, out) in enumerate(((rq_ref, q_ref), (rk_ref, k_ref))):
            factor = factors[:, which : which + 1]
            for head in range(wide // HD):
                lanes = slice(head * HD, (head + 1) * HD)
                value = raw[here, lanes] * factor * gain_ref[which : which + 1, lanes]
                out[here, lanes] = turned(value, cosine, sine).astype(BF16)

    for index in range(2, C):
        gather.step(index)
    own.wait()
    gather.finish()


def plane_sum_scratch(C, blocks):
    return [
        pltpu.VMEM((blocks, 8, ROWS), F32),
        pltpu.VMEM((2 * C, blocks, 8, ROWS), F32),
        pltpu.SemaphoreType.DMA((2 * C,)),
        pltpu.SemaphoreType.DMA((2 * C,)),
    ]


VM = pl.BlockSpec(memory_space=pltpu.VMEM)


def project(x, w, gains, cosine, sine, lines, C, number):
    total, width = x.shape
    wide = w.shape[1] // 3
    blocks = total // ROWS
    raw = jax.ShapeDtypeStruct((total, wide), F32)
    low = jax.ShapeDtypeStruct((total, wide), BF16)
    return pl.pallas_call(
        functools.partial(project_kernel, C),
        out_shape=(
            raw, raw, low, low, low,
            jax.ShapeDtypeStruct((blocks, 8, ROWS), F32),
            jax.ShapeDtypeStruct((lines.shape[0], 2 * C) + lines.shape[1:], BF16),
        ),
        in_specs=[VM] * 5 + [ANY],
        out_specs=(VM,) * 6 + (ANY,),
        scratch_shapes=[pltpu.SemaphoreType.DMA] + gather_sems(C) + plane_sum_scratch(C, blocks),
        compiler_params=comm_params(number, 48),
        cost_estimate=cost_of(18),
        name="project",
    )(x, w, gains, cosine, sine, lines)


def project_back_kernel(
    C, dq_ref, dk_ref, dv_ref, rq_ref, rk_ref, total, gain_ref, cos_ref, sin_ref, known_ref, deal_ref,
    out_ref, sum_ref, dealt_ref, deal_sent, deal_came, deal_own, term_ref, own_terms, all_terms, terms_sent, terms_came,
    eq, ek, inner, stats, landing, sent, came,
):
    greet([device for _, device in plane_peers(C)])
    wide = rq_ref.shape[1]
    width = wide * 2 * C
    blocks = stats.shape[0]

    def rows_at(block):
        return pl.ds(pl.multiple_of(block * ROWS, ROWS), ROWS)

    Z, shard, _ = dealt_ref.shape
    dp, ctx, _ = places_of()
    line = dp - lax.rem(dp, 2)
    seat = place_in_plane(C, (dp, ctx))

    def deal(number):
        at = seat * Z + number
        to = lax.rem(at, 2 * C)
        source, target = deal_ref.at[pl.ds(number * shard, shard)], dealt_ref.at[lax.div(at, 2 * C)]
        device = line + lax.div(to, C), lax.rem(to, C)
        away = remote(source, target, deal_sent.at[number], deal_came.at[lax.div(at, 2 * C)], device)
        return to, away, pltpu.make_async_copy(source, target, deal_own.at[number])

    for number in range(Z):
        to, away, stay = deal(number)

        @pl.when(to != seat)
        def _():
            away.start()

        @pl.when(to == seat)
        def _():
            stay.start()

    def factors_of(block):
        return columns_of(lax.rsqrt(total[block] * (1.0 / width) + EPS))

    term_ref[...] = jnp.zeros_like(term_ref)

    @pl.loop(0, blocks)
    def _(block):
        here = rows_at(block)
        factors = factors_of(block)
        cosine, sine = cos_ref[here, :], sin_ref[here, :]
        sums = []
        for which, (grad, raw, kept) in enumerate(((dq_ref, rq_ref, eq), (dk_ref, rk_ref, ek))):
            for head in range(wide // HD):
                lanes = slice(head * HD, (head + 1) * HD)
                kept[here, lanes] = turned(grad[here, lanes], cosine, -sine)
            product = kept[here, :] * raw[here, :] * factors[:, which : which + 1]
            term_ref[which : which + 1, :] += jnp.sum(product, axis=0, keepdims=True)
            sums.append(row_of_sums(product * gain_ref[which : which + 1, :]))
        stats[block] = pair_of_rows(*sums)

    start_sum(C, stats, landing, sent, came)
    lanes = pl.ds(pl.multiple_of(seat * wide, 128), wide)
    own_terms[...] = known_ref[...]
    own_terms[:, lanes] = own_terms[:, lanes] + term_ref[...]
    for index, device in plane_peers(C):
        remote(
            own_terms, all_terms.at[index], terms_sent.at[index], terms_came.at[index], device
        ).start()
    finish_sum(C, stats, landing, sent, came, inner)

    @pl.loop(0, blocks)
    def _(block):
        here = rows_at(block)
        factors = factors_of(block)
        means = columns_of(inner[block] * (1.0 / width))
        for which, (kept, raw) in enumerate(((eq, rq_ref), (ek, rk_ref))):
            factor, mean = factors[:, which : which + 1], means[:, which : which + 1]
            weighted = kept[here, :] * gain_ref[which : which + 1, :]
            value = factor * (weighted - raw[here, :] * factor * mean)
            out_ref[here, which * wide : (which + 1) * wide] = value.astype(BF16)
        out_ref[here, 2 * wide :] = dv_ref[here, :].astype(BF16)

    terms = own_terms[...]
    for index, device in plane_peers(C):
        remote(
            own_terms, all_terms.at[index], terms_sent.at[index], terms_came.at[index], device
        ).wait()
        terms = terms + all_terms[index]
    sum_ref[...] = terms
    for number in range(Z):
        to, away, stay = deal(number)

        @pl.when(to != seat)
        def _():
            away.wait_send()

        @pl.when(to == seat)
        def _():
            stay.wait()

    for number in range(Z):
        origin = lax.div(number * 2 * C + seat, Z)
        spot = dealt_ref.at[number]
        device = line + lax.div(origin, C), lax.rem(origin, C)

        @pl.when(origin != seat)
        def _():
            remote(spot, spot, deal_sent.at[number], deal_came.at[number], device).wait_recv()


def project_back(dq, dk, dv, raw_q, raw_k, sums, gains, cosine, sine, terms, dealt, C, Z, number):
    total, wide = dq.shape
    blocks = total // ROWS
    return pl.pallas_call(
        functools.partial(project_back_kernel, C),
        out_shape=(
            jax.ShapeDtypeStruct((total, 3 * wide), BF16),
            jax.ShapeDtypeStruct(terms.shape, F32),
            jax.ShapeDtypeStruct((Z, dealt.shape[0] // Z, dealt.shape[1]), BF16),
        ),
        in_specs=[VM] * 10 + [ANY],
        out_specs=(VM, VM, ANY),
        scratch_shapes=[
            pltpu.SemaphoreType.DMA((Z,)),
            pltpu.SemaphoreType.DMA((Z,)),
            pltpu.SemaphoreType.DMA((Z,)),
            pltpu.VMEM((8, wide), F32),
            pltpu.VMEM(terms.shape, F32),
            pltpu.VMEM((2 * C,) + terms.shape, F32),
            pltpu.SemaphoreType.DMA((2 * C,)),
            pltpu.SemaphoreType.DMA((2 * C,)),
            pltpu.VMEM((total, wide), F32),
            pltpu.VMEM((total, wide), F32),
            pltpu.VMEM((blocks, 8, ROWS), F32),
        ]
        + plane_sum_scratch(C, blocks),
        compiler_params=comm_params(number, 48),
        cost_estimate=cost_of(15),
        name="project_back",
    )(dq, dk, dv, raw_q, raw_k, sums, gains, cosine, sine, terms, dealt)


def attention_out_kernel(
    C, attended_ref, w_ref, tokens_ref, gain_ref, heads, proj, hidden_ref, h_out,
    low, own_sem, part_sent, part_came, copy_sem, *sems,
):
    count, width = tokens_ref.shape
    wide = width // (2 * C)
    dp, ctx, _ = places_of()
    here = place_in_plane(C, (dp, ctx))
    peers = plane_peers(C)
    greet([device for _, device in peers])

    def columns(at):
        return heads.at[:, pl.ds(pl.multiple_of(at * wide, 128), wide)]

    own = pltpu.make_async_copy(attended_ref.at[pl.ds(ctx * count, count)], columns(here), own_sem)
    own.start()
    copies = []
    for index, device in peers:
        rows = pl.ds(index // C * (C * count) + device[1] * count, count)
        copy = remote(
            attended_ref.at[rows], columns(here), part_sent.at[index], part_came.at[index], device
        )
        copy.start()
        copies.append(copy)
    own.wait()
    for index, device in peers:
        spot = columns(place_in_plane(C, device))
        remote(spot, spot, part_sent.at[index], part_came.at[index], device).wait_recv()
    for copy in copies:
        copy.wait_send()
    outs, size = tiles(width, 512)

    @pl.loop(0, outs)
    def _(number):
        lanes = at_tile(number, size)
        proj[:, lanes] = dot(heads[...], w_ref[:, lanes], 1, 0)

    chunks, chunk = tiles(count, 32)
    gain = gain_ref[0:1, :]

    @pl.loop(0, chunks)
    def _(number):
        rows = at_tile(number, chunk)
        value = proj[rows, :]
        factor = lax.rsqrt(jnp.mean(value * value, axis=-1, keepdims=True) + EPS)
        hidden = tokens_ref[rows, :].astype(F32) + value * factor * gain
        hidden_ref[rows, :] = hidden
        low[rows, :] = hidden.astype(BF16)

    gather = rows_gather(C, low, h_out, sems)
    copy = pltpu.make_async_copy(low, h_out.at[0, pl.ds(ctx * count, count)], copy_sem)
    for index in range(C):
        gather.step(index)
        if index == 0:
            copy.start()
    copy.wait()
    gather.finish()


def attention_out(attended, w, tokens, gain, C, number):
    count, width = tokens.shape
    whole = jax.ShapeDtypeStruct((count, width), F32)
    return pl.pallas_call(
        functools.partial(attention_out_kernel, C),
        out_shape=(
            jax.ShapeDtypeStruct((count, width), BF16),
            whole,
            whole,
            jax.ShapeDtypeStruct((2, C * count, width), BF16),
        ),
        in_specs=[VM] * 4,
        out_specs=(VM, VM, VM, ANY),
        scratch_shapes=[
            pltpu.VMEM((count, width), BF16),
            pltpu.SemaphoreType.DMA,
            pltpu.SemaphoreType.DMA((2 * C,)),
            pltpu.SemaphoreType.DMA((2 * C,)),
            pltpu.SemaphoreType.DMA,
        ]
        + gather_sems(C),
        compiler_params=comm_params(number, 60),
        cost_estimate=cost_of(60),
        name="attention_out",
    )(attended, w, tokens, gain)


def return_kernel(C, groups, blocks, x_ref, *refs):
    out, landing, sent, came, own_sem = refs
    A = 2 * C
    shard = out.shape[0] // groups
    part = out.shape[1] // (blocks * A)
    wide = groups * blocks * part
    dp, ctx, _ = places_of()
    own_at = place_in_plane(C, (dp, ctx))
    peers = plane_peers(C)
    greet([device for _, device in peers])
    own = pltpu.make_async_copy(
        x_ref.at[pl.ds(own_at * shard, shard), pl.ds(0, wide)], landing.at[own_at], own_sem
    )
    own.start()

    def copy_to(index, device):
        rows = pl.ds(place_in_plane(C, device) * shard, shard)
        return remote(
            x_ref.at[rows, pl.ds(0, wide)],
            landing.at[own_at],
            sent.at[index],
            came.at[index],
            device,
        )

    def landed(index, device):
        spot = landing.at[place_in_plane(C, device)]
        remote(spot, spot, sent.at[index], came.at[index], device).wait_recv()

    for index, device in peers:
        copy_to(index, device).start()
    own.wait()
    for index, device in peers:
        landed(index, device)
    for index, device in peers:
        copy_to(index, device).wait_send()
    for group in range(groups):
        for block in range(blocks):
            for at in range(A):
                lanes = (group * blocks + block) * part
                to = (block * A + at) * part
                rows = slice(group * shard, (group + 1) * shard)
                out[rows, to : to + part] = landing[at, :, lanes : lanes + part]


def return_rows(x, wide, C, groups, blocks, number):
    A = 2 * C
    shard = x.shape[0] // A
    return pl.pallas_call(
        functools.partial(return_kernel, C, groups, blocks),
        out_shape=jax.ShapeDtypeStruct((groups * shard, wide * A // groups), x.dtype),
        in_specs=[ANY],
        out_specs=VM,
        scratch_shapes=[
            pltpu.VMEM((A, shard, wide), x.dtype),
            pltpu.SemaphoreType.DMA((A,)),
            pltpu.SemaphoreType.DMA((A,)),
            pltpu.SemaphoreType.DMA,
        ],
        compiler_params=comm_params(number, 24),
        cost_estimate=cost_of(20),
        name="return_rows",
    )(x)


class Scatter:
    def __init__(self, C, count, own, other, twin_part, landing, sems, final):
        self.C, self.count, self.half = C, count, count // 2
        self.own, self.other, self.twin_part, self.landing = own, other, twin_part, landing
        self.core_sent, self.core_came, self.ctx_sent, self.ctx_came = sems
        self.dp, self.ctx, self.twin = places_of()
        self.onward = [{m: (bits, bit) for m, bits, bit in tree(order)} for order in bit_orders(C)]
        self.final = final

    def rows(self, half, mask):
        return pl.ds(flipped(self.ctx, mask) * self.count + half * self.half, self.half)

    def block(self, mask):
        return pl.ds(flipped(self.ctx, mask) * self.count, self.count)

    def across(self, half, mask):
        return remote(
            self.other.at[self.rows(half, mask)],
            self.twin_part.at[self.rows(half, mask)],
            self.core_sent.at[half, mask],
            self.core_came.at[half, mask],
            (self.twin, self.ctx),
        )

    def back(self, half, mask, bit):
        return remote(
            self.own.at[self.rows(half, mask)],
            self.landing.at[half, mask],
            self.ctx_sent.at[half, mask],
            self.ctx_came.at[half, mask],
            (self.dp, flipped(self.ctx, bit)),
        )

    def settle(self, half, mask):
        along, bit = self.onward[half][mask]
        self.across(half, mask).wait_recv()
        here = self.rows(half, mask)
        total = self.own[here, :].astype(F32) + self.twin_part[here, :].astype(F32)
        for came in along:
            self.back(half, mask | came, came).wait_recv()
            total = total + self.landing[half, mask | came].astype(F32)
        if mask:
            self.own[here, :] = total.astype(BF16)
            self.back(half, mask, bit).start()
        else:
            self.final(half, total)

    def order(self):
        return sorted(range(self.C), key=lambda mask: (-bin(mask).count("1"), mask))

    def run(self, compute):
        waiting = []
        for mask in self.order():
            compute(1, mask)
            for half in range(2):
                self.across(half, mask).start()
            compute(0, mask)
            ready = [half for half in range(2) if mask and not self.onward[half][mask][0]]
            for half in ready:
                self.settle(half, mask)
            for half, earlier in waiting:
                self.settle(half, earlier)
            waiting = [(half, mask) for half in range(2) if half not in ready]
        for half, earlier in waiting:
            self.settle(half, earlier)
        for half in range(2):
            for mask in range(self.C):
                self.across(half, mask).wait_send()
                if mask:
                    self.back(half, mask, self.onward[half][mask][1]).wait_send()


def scatter_scratch(C, count, width):
    rows = pltpu.VMEM((C * count, width), BF16)
    return [rows, rows, rows, pltpu.VMEM((2, C, count // 2, width), BF16)] + [
        pltpu.SemaphoreType.DMA((2, C))
    ] * 4


def tiles(total, size):
    size = min(total, size)
    return total // size, size


def at_tile(number, size, base=0):
    return pl.ds(pl.multiple_of(base + number * size, size), size)


def mix_kernel(h_ref, wgu_ref, gu_ref, mixed_ref, turned_ref):
    ffn = mixed_ref.shape[1]
    steps, tile = tiles(ffn, 256)
    for number in range(steps):
        first = slice(number * tile, (number + 1) * tile)
        second = slice(ffn + number * tile, ffn + (number + 1) * tile)
        gate = dot(h_ref[...], wgu_ref[:, first], 1, 0)
        up = dot(h_ref[...], wgu_ref[:, second], 1, 0)
        gu_ref[:, first] = gate.astype(BF16)
        gu_ref[:, second] = up.astype(BF16)
        mixed = gate * jax.nn.sigmoid(gate) * up
        mixed_ref[:, first] = mixed.astype(BF16)
        turned_ref[first, :] = mixed.T.astype(BF16)


def mix(h, w_gate_up):
    total, width = h.shape
    ffn = w_gate_up.shape[1] // 2
    rows = min(256, total)
    return pl.pallas_call(
        mix_kernel,
        out_shape=(
            jax.ShapeDtypeStruct((total, 2 * ffn), BF16),
            jax.ShapeDtypeStruct((total, ffn), BF16),
            jax.ShapeDtypeStruct((ffn, total), BF16),
        ),
        grid=(total // rows,),
        in_specs=[
            pl.BlockSpec((rows, width), lambda i: (i, 0)),
            pl.BlockSpec((width, 2 * ffn), lambda i: (0, 0)),
        ],
        out_specs=(
            pl.BlockSpec((rows, 2 * ffn), lambda i: (i, 0)),
            pl.BlockSpec((rows, ffn), lambda i: (i, 0)),
            pl.BlockSpec((ffn, rows), lambda i: (0, i)),
        ),
        compiler_params=pltpu.CompilerParams(vmem_limit_bytes=60 * 2**20),
        cost_estimate=cost_of(20),
        name="mix",
    )(h, w_gate_up)


def feed_forward_kernel(
    C, mixed_ref, turned_ref, gu_ref, first_wd, second_wd, hidden_in, cot_in, gain_ref,
    out_hbm, b_out, down_hbm, term_ref,
    wd_ref, hidden_ref, cot_ref, out_ref,
    mixed_buf, proj, f_own, f_all, turned_buf, gu_buf, b_buf, total,
    mixed_sem, turned_sem, gu_sem, b_sem, down_sem, load_sem,
    ctx_sent, ctx_came, core_sent, core_came,
    own, other, twin_part, landing, *sems,
):
    split = first_wd.shape[1]
    loads = [
        pltpu.make_async_copy(first_wd, wd_ref.at[:, pl.ds(0, split)], load_sem.at[0]),
        pltpu.make_async_copy(
            second_wd, wd_ref.at[:, pl.ds(split, second_wd.shape[1])], load_sem.at[1]
        ),
        pltpu.make_async_copy(hidden_in, hidden_ref, load_sem.at[2]),
        pltpu.make_async_copy(cot_in, cot_ref, load_sem.at[3]),
    ]
    for load in loads:
        load.start()
    greet(plane_neighbours(C))
    count, width = hidden_ref.shape
    ffn = wd_ref.shape[0]
    seq = C * count
    half_rows = count // 2

    def final(half, value):
        proj[pl.ds(half * half_rows, half_rows), :] = value

    scatter = Scatter(C, count, own, other, twin_part, landing, sems, final)
    sequence = [(side, mask) for mask in scatter.order() for side in (1, 0)]

    def rows_of(side, mask):
        return pl.ds(pl.multiple_of(side * seq + flipped(scatter.ctx, mask) * count, count), count)

    def fetch(index):
        return pltpu.make_async_copy(
            mixed_ref.at[rows_of(*sequence[index])], mixed_buf.at[index % 2], mixed_sem.at[index % 2]
        )

    fetch(0).start()
    steps, tile = tiles(ffn, 256)
    outs, wide = tiles(width, 512)

    def compute(side, mask):
        index = sequence.index((side, mask))
        slot = index % 2
        fetch(index).wait()
        if index + 1 < len(sequence):
            fetch(index + 1).start()
        target, here = (own, other)[side], scatter.block(mask)

        @pl.loop(0, outs)
        def _(number):
            lanes = at_tile(number, wide)
            target[here, lanes] = dot(mixed_buf[slot], wd_ref[:, lanes], 1, 0).astype(BF16)

    for load in loads[:2]:
        load.wait()
    scatter.run(compute)
    for load in loads[2:]:
        load.wait()
    gain = gain_ref[0:1, :]
    term_ref[...] = jnp.zeros_like(term_ref)
    chunks, chunk = tiles(count, 32)

    @pl.loop(0, chunks)
    def _(number):
        here = at_tile(number, chunk)
        value = proj[here, :]
        factor = lax.rsqrt(jnp.mean(value * value, axis=-1, keepdims=True) + EPS)
        unit = value * factor
        out_ref[here, :] = hidden_ref[here, :] + unit * gain
        incoming = cot_ref[here, :].astype(F32)
        weighted = incoming * gain
        inner = jnp.mean(weighted * unit, axis=-1, keepdims=True)
        f_own[here, :] = (factor * (weighted - unit * inner)).astype(BF16)
        term_ref[0:1, :] += jnp.sum(incoming * unit, axis=0, keepdims=True)

    gather = rows_gather(C, f_own, f_all, (ctx_sent, ctx_came, core_sent, core_came))
    output = pltpu.make_async_copy(out_ref, out_hbm, load_sem.at[4])
    blocks = [
        (side, mask, index)
        for index in range(C)
        for mask in gather.complete(index)
        for side in (0, 1)
    ]

    def fetch_kept(number):
        side, mask, _ = blocks[number]
        slot, rows = number % 2, rows_of(side, mask)
        return (
            pltpu.make_async_copy(turned_ref.at[:, rows], turned_buf.at[slot], turned_sem.at[slot]),
            pltpu.make_async_copy(gu_ref.at[rows], gu_buf.at[slot], gu_sem.at[slot]),
        )

    def keep(number):
        side, mask, _ = blocks[number]
        return pltpu.make_async_copy(
            b_buf.at[number % 2], b_out.at[rows_of(side, mask)], b_sem.at[number % 2]
        )

    def sum_out(at):
        lanes = pl.ds(at * wide, wide)
        rows = pl.ds(0, ffn)
        return pltpu.make_async_copy(
            other.at[rows, lanes], down_hbm.at[:, lanes], down_sem.at[at]
        )

    def back(number, grads):
        slot = number % 2
        for arrived in fetch_kept(number):
            arrived.wait()
        if number >= 2:
            keep(number - 2).wait()

        @pl.loop(0, steps)
        def _(at):
            first, second = at_tile(at, tile), at_tile(at, tile, ffn)
            grad = dot(grads[...], wd_ref[first, :], 1, 1)
            gate, up = gu_buf[slot, :, first].astype(F32), gu_buf[slot, :, second].astype(F32)
            sig = jax.nn.sigmoid(gate)
            b_buf[slot, :, first] = (grad * up * sig * (1.0 + gate * (1.0 - sig))).astype(BF16)
            b_buf[slot, :, second] = (grad * (gate * sig)).astype(BF16)

        keep(number).start()

        if number < len(blocks) - 1:

            @pl.loop(0, outs)
            def _(at):
                lanes = at_tile(at, wide)
                value = dot(turned_buf[slot], grads[:, lanes], 1, 0)
                if number == 0:
                    total[:, lanes] = value
                else:
                    total[:, lanes] += value

        else:
            for at in range(outs):
                lanes = slice(at * wide, (at + 1) * wide)
                value = dot(turned_buf[slot], grads[:, lanes], 1, 0)
                other[0:ffn, lanes] = (total[:, lanes] + value).astype(BF16)
                sum_out(at).start()

    for arriving in fetch_kept(0):
        arriving.start()
    done = 0
    for index in range(C):
        gather.step(index)
        if index == 0:
            output.start()
        while done < len(blocks) and blocks[done][2] == index:
            side, mask, _ = blocks[done]
            if done + 1 < len(blocks):
                for arriving in fetch_kept(done + 1):
                    arriving.start()
            if (side, mask) == (0, 0):
                back(done, f_own)
            else:
                if side:
                    for half in range(2):
                        gather.crossed(half, mask)
                back(done, f_all.at[side, scatter.block(mask)])
            done += 1
    for number in (len(blocks) - 2, len(blocks) - 1):
        keep(number).wait()
    for at in range(outs):
        sum_out(at).wait()
    output.wait()
    gather.sent()


def feed_forward(mixed, turned_units, gate_up, w_down, hidden, cotangent, gain, C, number):
    count, width = hidden.shape
    total, ffn = 2 * C * count, w_down[0].shape[0]
    pair = pltpu.SemaphoreType.DMA((2,))
    return pl.pallas_call(
        functools.partial(feed_forward_kernel, C),
        out_shape=(
            jax.ShapeDtypeStruct((count, width), F32),
            jax.ShapeDtypeStruct((total, 2 * ffn), BF16),
            jax.ShapeDtypeStruct((ffn, width), BF16),
            jax.ShapeDtypeStruct((8, width), F32),
        ),
        in_specs=[ANY] * 7 + [VM],
        out_specs=(ANY, ANY, ANY, VM),
        scratch_shapes=[
            pltpu.VMEM((ffn, width), BF16),
            pltpu.VMEM((count, width), F32),
            pltpu.VMEM((count, width), BF16),
            pltpu.VMEM((count, width), F32),
            pltpu.VMEM((2, count, ffn), BF16),
            pltpu.VMEM((count, width), F32),
            pltpu.VMEM((count, width), BF16),
            pltpu.VMEM((2, C * count, width), BF16),
            pltpu.VMEM((2, ffn, count), BF16),
            pltpu.VMEM((2, count, 2 * ffn), BF16),
            pltpu.VMEM((2, count, 2 * ffn), BF16),
            pltpu.VMEM((ffn, width), F32),
            pair,
            pair,
            pair,
            pair,
            pltpu.SemaphoreType.DMA((tiles(width, 512)[0],)),
            pltpu.SemaphoreType.DMA((5,)),
        ]
        + gather_sems(C)
        + scatter_scratch(C, count, width),
        compiler_params=comm_params(number, 60),
        cost_estimate=cost_of(80),
        name="feed_forward",
    )(mixed, turned_units, gate_up, *w_down, hidden, cotangent, gain)


def back_scatter_kernel(C, added, b_ref, w_in, *refs):
    if added:
        add_in, add_ref, refs = refs[0], refs[1], refs[2:]
    out_hbm, out_ref, out_sem, w_ref, load_sem, b_buf, b_sem = refs[:7]
    own, other, twin_part, landing, *sems = refs[7:]
    loads = [pltpu.make_async_copy(w_in, w_ref, load_sem.at[0])]
    if added:
        loads.append(pltpu.make_async_copy(add_in, add_ref, load_sem.at[1]))
    for load in loads:
        load.start()
    greet(plane_neighbours(C))
    count, width = out_ref.shape
    seq = C * count
    half_rows = count // 2

    def final(half, total):
        rows = pl.ds(half * half_rows, half_rows)
        if added:
            total = total + add_ref[rows, :].astype(F32)
        out_ref[rows, :] = total
        leave(half).start()

    def leave(half):
        rows = pl.ds(half * half_rows, half_rows)
        return pltpu.make_async_copy(out_ref.at[rows], out_hbm.at[rows], out_sem.at[half])

    scatter = Scatter(C, count, own, other, twin_part, landing, sems, final)
    sequence = [(side, mask) for mask in scatter.order() for side in (1, 0)]

    def fetch(index):
        side, mask = sequence[index]
        rows = pl.ds(side * seq + flipped(scatter.ctx, mask) * count, count)
        return pltpu.make_async_copy(b_ref.at[rows], b_buf.at[index % 2], b_sem.at[index % 2])

    fetch(0).start()
    outs, wide = tiles(width, 512)

    def compute(side, mask):
        index = sequence.index((side, mask))
        slot = index % 2
        fetch(index).wait()
        if index + 1 < len(sequence):
            fetch(index + 1).start()
        target, here = (own, other)[side], scatter.block(mask)

        @pl.loop(0, outs)
        def _(number):
            lanes = at_tile(number, wide)
            target[here, lanes] = dot(b_buf[slot], w_ref[lanes, :], 1, 1).astype(BF16)

    for load in loads:
        load.wait()
    scatter.run(compute)
    for half in range(2):
        leave(half).wait()


def back_scatter(b, w, add, C, number):
    width = w.shape[0]
    count = b.shape[0] // (2 * C)
    added = add is not None
    scratch = [
        pltpu.VMEM((count, width), F32),
        pltpu.SemaphoreType.DMA((2,)),
        pltpu.VMEM(w.shape, w.dtype),
        pltpu.SemaphoreType.DMA((2,)),
        pltpu.VMEM((2, count, b.shape[1]), BF16),
        pltpu.SemaphoreType.DMA((2,)),
    ] + scatter_scratch(C, count, width)

    def kernel(*refs):
        if added:
            b_ref, w_in, add_in, out_hbm, *rest = refs
            back_scatter_kernel(C, True, b_ref, w_in, add_in, rest[-1], out_hbm, *rest[:-1])
        else:
            back_scatter_kernel(C, False, *refs)

    return pl.pallas_call(
        kernel,
        out_shape=jax.ShapeDtypeStruct((count, width), F32),
        in_specs=[ANY] * (3 if added else 2),
        out_specs=ANY,
        scratch_shapes=scratch + ([pltpu.VMEM(add.shape, add.dtype)] if added else []),
        compiler_params=comm_params(number, 48),
        cost_estimate=cost_of(50),
        name="back_scatter",
    )(*((b, w, add) if added else (b, w)))


def rope_tables(places):
    half = HD // 2
    frequency = THETA ** (-(jnp.arange(half, dtype=F32) * 2.0) / HD)
    angles = places.astype(F32)[:, None] * frequency[None, :]
    cosine, sine = jnp.cos(angles), jnp.sin(angles)
    return jnp.concatenate([cosine, cosine], axis=1), jnp.concatenate([-sine, sine], axis=1)


def row_norm(tensor):
    factor = lax.rsqrt(jnp.mean(tensor * tensor, axis=-1, keepdims=True) + EPS)
    return tensor * factor, factor


def row_norm_back(unit, factor, gain, incoming):
    weighted = incoming * gain
    inner = jnp.mean(weighted * unit, axis=-1, keepdims=True)
    return factor * (weighted - unit * inner), jnp.sum(incoming * unit, axis=0)


def layer(
    ctx_size,
    dp_size,
    tokens,
    w_query,
    w_key,
    w_value,
    w_out,
    gain_query,
    gain_key,
    gain_attn,
    w_gate,
    w_up,
    w_down,
    gain_ffn,
    positions,
    image_starts,
    cotangent,
):
    C, Z = ctx_size, dp_size // 2
    A = 2 * C
    N = Z * A
    ctx, dp = lax.axis_index("ctx"), lax.axis_index("dp")
    core, z = lax.rem(dp, 2), lax.div(dp, 2)
    plane_at = core * C + ctx
    own_at = dp * C + ctx
    rows, width = tokens.shape
    ffn_width = w_gate.shape[1]
    shard = w_query.shape[0]
    down_shard = w_down.shape[0]
    seq_len = rows * C
    slice_width = width // A
    ffn_slice = ffn_width // A
    planes = [[zz * A + p for p in range(A)] for zz in range(Z)]
    columns = [[zz * 2 + k for zz in range(Z)] for k in range(2)]

    def swap(x, bit):
        return lax.ppermute(x, AXES, [(i, i ^ bit) for i in range(N)])

    def rows_of(x, at, count):
        return lax.dynamic_slice_in_dim(x, at, count, 0)

    def gather_z_aside(x):
        return lax.all_gather(x, "dp", axis=0, tiled=True, axis_index_groups=columns)

    def scatter_z_aside(x):
        return lax.psum_scatter(
            x, "dp", scatter_dimension=0, tiled=True, axis_index_groups=columns
        )

    def exchange(x):
        return lax.all_to_all(x, AXES, 0, 0, tiled=True, axis_index_groups=planes)

    split = width * 3 // 4
    first_down = gather_z_aside(w_down[:, :split])
    part = down_shard
    dealt = part % 128 == 0
    gains = jnp.stack([gain_query, gain_key, gain_attn, gain_ffn])
    gains = jnp.pad(gains, ((0, 12), (0, -shard % 128)))
    x_both, full_qkv, out_lines, _, all_gains, *gate_up = first_gather(
        tokens, w_query, w_key, w_value, w_out, gains, w_gate, w_up, dealt, C, Z, 1
    )
    if dealt:
        gate_up = gate_up[0]
    else:
        gate_up = jnp.stack([w.reshape(shard, Z, A, part) for w in (w_gate, w_up)], axis=1)
        gate_up = exchange(gate_up.transpose(3, 0, 1, 2, 4).reshape(A * shard, 2 * ffn_slice))
    full_qkv, gate_up, first_down, w_down = lax.optimization_barrier(
        (full_qkv, gate_up, first_down, w_down)
    )
    second_down = w_down[:, split:]
    full_gate_up = gather_z_aside(gate_up)
    all_gains = all_gains[:, :, :4, :shard].astype(F32).transpose(2, 0, 1, 3).reshape(4, width)
    head_gains = lax.dynamic_slice(all_gains, (0, plane_at * slice_width), (2, slice_width))
    head_gains = jnp.pad(head_gains, ((0, 6), (0, 0)))
    gain_a, gain_f = all_gains[2:3], all_gains[3:4]

    x_all = x_both.reshape(2 * seq_len, width)
    other_dp = dp + 1 - 2 * core
    places = jnp.concatenate(
        [rows_of(positions, dp * seq_len, seq_len), rows_of(positions, other_dp * seq_len, seq_len)]
    )
    starts = jnp.concatenate([rows_of(image_starts, dp, 1), rows_of(image_starts, other_dp, 1)])
    start_rows = jnp.repeat(starts, seq_len, axis=0)
    inside = (places[:, None] >= start_rows) & (places[:, None] < start_rows + IMG)
    limits = jnp.max(jnp.where(inside, start_rows + (IMG - 1), places[:, None]), axis=1)
    limit_column = limits[:, None]
    place_rows = places.reshape(2, 1, seq_len)
    cosine, sine = rope_tables(places)
    raw_q, raw_k, value, query_turned, key_turned, squares, full_out = project(
        x_all, full_qkv, head_gains, cosine, sine, out_lines, C, 8
    )
    full_out = full_out.reshape(width, width)
    attended = attend(query_turned, key_turned, value, limit_column, place_rows, seq_len)
    attended_own, attn_proj, hidden, h_both = attention_out(
        attended, full_out, tokens, jnp.pad(gain_a, ((0, 7), (0, 0))), C, 2
    )

    h_all = h_both.reshape(2 * seq_len, width)
    full_gate_up, second_down, h_all = lax.optimization_barrier((full_gate_up, second_down, h_all))
    second_down = gather_z_aside(second_down)
    gate_up_low, mixed, turned_units = mix(h_all, full_gate_up)
    output, b_all, term_down, term_gain_ffn = feed_forward(
        mixed, turned_units, gate_up_low, (first_down, second_down), hidden, cotangent,
        jnp.pad(gain_f, ((0, 7), (0, 0))), C, 3,
    )

    term_down, b_all = lax.optimization_barrier((term_down, b_all))
    grad_w_down = scatter_z_aside(term_down)
    grad_hidden = back_scatter(b_all, full_gate_up, cotangent, C, 5)
    term_gate_up = dot(h_all, b_all, 0, 0, BF16)
    term_gate_up, grad_hidden, grad_w_down = lax.optimization_barrier(
        (term_gate_up, grad_hidden, grad_w_down)
    )
    grad_gate_up = scatter_z_aside(term_gate_up)

    attn_unit, attn_factor = row_norm(attn_proj)
    grad_attn, term_gain_attn = row_norm_back(attn_unit, attn_factor, gain_a, grad_hidden)
    a_all = gather_rows(grad_attn.astype(BF16), C, 7).reshape(2 * seq_len, width)
    grad_attended = dot(
        a_all, rows_of(full_out, plane_at * slice_width, slice_width), 1, 1, BF16
    )
    term_out = dot(attended, a_all, 0, 0, BF16)
    grad_q, grad_k, grad_v = attend_back(
        query_turned, key_turned, value, grad_attended, limit_column, place_rows, seq_len
    )
    known = jnp.concatenate(
        [jnp.zeros((2, width), F32), term_gain_attn[None], term_gain_ffn[:1], jnp.zeros((4, width), F32)]
    )
    grad_raw, gain_terms, term_out = project_back(
        grad_q, grad_k, grad_v, raw_q, raw_k, squares, head_gains, cosine, sine, known, term_out,
        C, Z, 9,
    )
    term_qkv = dot(x_all, grad_raw, 0, 0, BF16)
    last = jnp.concatenate([term_qkv, term_out.reshape(width, slice_width)], axis=1)
    last, grad_raw, grad_gate_up, gain_terms, output, grad_w_down = lax.optimization_barrier(
        (last, grad_raw, grad_gate_up, gain_terms, output.astype(BF16), grad_w_down.astype(F32))
    )
    last = scatter_z_aside(last)
    if dealt:
        grad_gate_up = return_rows(grad_gate_up, 2 * ffn_slice, C, 2, Z, 10)
        grad_gate_up = grad_gate_up.reshape(2, shard, ffn_width)
    else:
        grad_gate_up = (
            exchange(grad_gate_up)
            .reshape(A, shard, 2, Z, part)
            .transpose(2, 1, 3, 0, 4)
            .reshape(2, shard, ffn_width)
        )
    gain_terms = gain_terms[:4]
    gain_terms = gain_terms + swap(gain_terms, A)
    *grad_gate_up, gain_terms, grad_raw = lax.optimization_barrier(
        (grad_gate_up[0].astype(F32), grad_gate_up[1].astype(F32), gain_terms, grad_raw)
    )
    for power in range(1, Z.bit_length() - 1):
        gain_terms = gain_terms + swap(gain_terms, A << power)
    grad_input = back_scatter(grad_raw, full_qkv, None, C, 6) + grad_hidden
    last, grad_input = lax.optimization_barrier((last, grad_input))
    grad_qkv = return_rows(last, 3 * slice_width, C, 3, 1, 11).reshape(3, shard, width)
    grad_w_out = last[:, 3 * slice_width :]
    gain_sums = lax.dynamic_slice(gain_terms, (0, own_at * shard), (4, shard))

    return (
        output,
        grad_input,
        grad_qkv[0].astype(F32),
        grad_qkv[1].astype(F32),
        grad_qkv[2].astype(F32),
        grad_w_out.reshape(shard, width).astype(F32),
        gain_sums[0],
        gain_sums[1],
        gain_sums[2],
        grad_gate_up[0],
        grad_gate_up[1],
        grad_w_down,
        gain_sums[3],
    )


def solution(mesh):
    split, line, copied = P(AXES, None), P(AXES), P()
    return jax.shard_map(
        functools.partial(layer, mesh.shape["ctx"], mesh.shape["dp"]),
        mesh=mesh,
        in_specs=(split,) * 5 + (line,) * 3 + (split,) * 3 + (line, copied, copied, split),
        out_specs=(split,) * 6 + (line,) * 3 + (split,) * 3 + (line,),
        check_vma=False,
    )
```

```python
import functools
import math

import jax
import jax.numpy as jnp
from jax import lax
from jax.experimental import pallas as pl
from jax.experimental.pallas import tpu as pltpu
from jax.sharding import PartitionSpec as P

HD = 128
IMG = 256
EPS = 1e-06
THETA = 500000.0
NEG = -1e30
AXES = ("dp", "ctx")
F32 = jnp.float32
BF16 = jnp.bfloat16
SCALE = 1.0 / math.sqrt(HD)
LOG2E = math.log2(math.e)


def dot(left, right, left_dim, right_dim, kind=F32):
    return lax.dot_general(
        left, right, (((left_dim,), (right_dim,)), ((), ())), preferred_element_type=kind
    )


def probs_of(q, k, limit, places):
    scores = dot(q, k, 1, 1)
    scores = jnp.where(places <= limit, scores, NEG)
    peak = jnp.max(scores, axis=-1, keepdims=True)
    weights = jnp.exp2((scores - peak) * (SCALE * LOG2E))
    return weights * (1.0 / jnp.sum(weights, axis=-1, keepdims=True))


def attend_kernel(q_ref, k_ref, v_ref, limit_ref, place_ref, out_ref):
    probs = probs_of(q_ref[...], k_ref[...], limit_ref[...], place_ref[0])
    out_ref[...] = dot(probs.astype(BF16), v_ref[...], 1, 0).astype(BF16)


def attend_back_kernel(
    q_ref, k_ref, v_ref, g_ref, limit_ref, place_ref, dq_ref, dk_ref, dv_ref
):
    step = pl.program_id(2)

    @pl.when(step == 0)
    def _():
        dk_ref[...] = jnp.zeros_like(dk_ref)
        dv_ref[...] = jnp.zeros_like(dv_ref)

    q, k, v, g = q_ref[...], k_ref[...], v_ref[...], g_ref[...]
    probs = probs_of(q, k, limit_ref[...], place_ref[0])
    grad_probs = dot(g, v, 1, 1)
    inner = jnp.sum(probs * grad_probs, axis=-1, keepdims=True)
    grad_scores = (probs * (grad_probs - inner)).astype(BF16)
    dq_ref[...] = dot(grad_scores, k, 1, 0) * SCALE
    dk_ref[...] += dot(grad_scores, q, 0, 0) * SCALE
    dv_ref[...] += dot(probs.astype(BF16), g, 0, 0)


def attention_specs(seq_len, rows):
    steps = seq_len // rows
    query = pl.BlockSpec((rows, HD), lambda s, h, i: (s * steps + i, h))
    keys = pl.BlockSpec((seq_len, HD), lambda s, h, i: (s, h))
    limit = pl.BlockSpec((rows, 1), lambda s, h, i: (s * steps + i, 0))
    places = pl.BlockSpec((1, 1, seq_len), lambda s, h, i: (s, 0, 0))
    return query, keys, limit, places


def attend(q, k, v, limits, places, seq_len):
    rows = min(256, seq_len)
    total, width = q.shape
    query, keys, limit, place = attention_specs(seq_len, rows)
    return pl.pallas_call(
        attend_kernel,
        out_shape=jax.ShapeDtypeStruct((total, width), BF16),
        grid=(total // seq_len, width // HD, seq_len // rows),
        in_specs=[query, keys, keys, limit, place],
        out_specs=query,
        compiler_params=pltpu.CompilerParams(vmem_limit_bytes=48 * 2**20),
        cost_estimate=pl.CostEstimate(
            flops=4 * total * seq_len * width,
            bytes_accessed=8 * total * width,
            transcendentals=total * seq_len * (width // HD),
        ),
        name="attend",
    )(q, k, v, limits, places)


def attend_back(q, k, v, g, limits, places, seq_len):
    rows = min(256, seq_len)
    total, width = q.shape
    query, keys, limit, place = attention_specs(seq_len, rows)
    shape = jax.ShapeDtypeStruct((total, width), F32)
    return pl.pallas_call(
        attend_back_kernel,
        out_shape=(shape, shape, shape),
        grid=(total // seq_len, width // HD, seq_len // rows),
        in_specs=[query, keys, keys, query, limit, place],
        out_specs=(query, keys, keys),
        compiler_params=pltpu.CompilerParams(vmem_limit_bytes=48 * 2**20),
        cost_estimate=pl.CostEstimate(
            flops=10 * total * seq_len * width,
            bytes_accessed=20 * total * width,
            transcendentals=total * seq_len * (width // HD),
        ),
        name="attend_back",
    )(q, k, v, g, limits, places)


MESH = pl.DeviceIdType.MESH
ANY = pl.BlockSpec(memory_space=pl.ANY)


def flipped(at, mask):
    bit = 1
    while bit <= mask:
        if mask & bit:
            at = at + bit - 2 * bit * lax.rem(lax.div(at, bit), 2)
        bit *= 2
    return at


def bit_orders(C):
    bits = [1 << b for b in range(C.bit_length() - 1)]
    return bits, bits[::-1]


def tree(order):
    found = [(0, order, 0)]
    for place, bit in enumerate(order):
        found += [(mask | bit, order[place + 1 :], bit) for mask, _, _ in list(found)]
    return found


def signal_barrier(peers):
    barrier = pltpu.get_barrier_semaphore()
    for peer in peers:
        pl.semaphore_signal(barrier, inc=1, device_id=peer, device_id_type=MESH)
    return barrier


def greet(peers):
    pl.semaphore_wait(signal_barrier(peers), len(peers))


def remote(src, dst, sent, arrived, device):
    return pltpu.make_async_remote_copy(
        src_ref=src, dst_ref=dst, send_sem=sent, recv_sem=arrived, device_id=device, device_id_type=MESH
    )


def places_of():
    dp, ctx = lax.axis_index("dp"), lax.axis_index("ctx")
    return dp, ctx, dp + 1 - 2 * lax.rem(dp, 2)


class Gather:
    def __init__(self, C, source, slot, over, from_over, sems):
        self.C = C
        self.source, self.slot, self.over, self.from_over = source, slot, over, from_over
        self.ctx_sent, self.ctx_came, self.core_sent, self.core_came = sems
        self.dp, self.ctx, self.twin = places_of()
        self.trees = [tree(order) for order in bit_orders(C)]
        self.sends = []

    def held(self, half, mask):
        return self.slot(flipped(self.ctx, mask), half) if mask else self.source(half)

    def by_ctx(self, half, mask, bit):
        return remote(
            self.held(half, mask),
            self.slot(flipped(self.ctx, mask), half),
            self.ctx_sent.at[half, mask | bit],
            self.ctx_came.at[half, mask | bit],
            (self.dp, flipped(self.ctx, bit)),
        )

    def by_core(self, half, mask):
        return remote(
            self.held(half, mask),
            self.over(flipped(self.ctx, mask), half),
            self.core_sent.at[half, mask],
            self.core_came.at[half, mask],
            (self.twin, self.ctx),
        )

    def landed(self, half, mask, bit):
        slot = self.slot(flipped(self.ctx, mask), half)
        remote(
            slot,
            slot,
            self.ctx_sent.at[half, mask],
            self.ctx_came.at[half, mask],
            (self.dp, flipped(self.ctx, bit)),
        ).wait_recv()

    def start(self, copy):
        copy.start()
        self.sends.append(copy)

    def step(self, index):
        for half in range(2):
            mask, onward, bit = self.trees[half][index]
            if mask:
                self.landed(half, mask, bit)
            for further in onward:
                self.start(self.by_ctx(half, mask, further))
            if mask:
                self.start(self.by_core(half, mask))
        if index == 0:
            for half in range(2):
                self.start(self.by_core(half, 0))

    def crossed(self, half, mask):
        slot = self.from_over(flipped(self.ctx, mask), half)
        remote(
            slot,
            slot,
            self.core_sent.at[half, mask],
            self.core_came.at[half, mask],
            (self.twin, self.ctx),
        ).wait_recv()

    def sent(self):
        for copy in self.sends:
            copy.wait_send()

    def finish(self):
        self.sent()
        for half in range(2):
            for mask in range(self.C):
                self.crossed(half, mask)

    def complete(self, index):
        place = [{m: at for at, (m, _, _) in enumerate(tree)} for tree in self.trees]
        return [m for m in range(self.C) if max(place[0][m], place[1][m]) == index]


def rows_gather(C, x_ref, out_ref, sems):
    count = x_ref.shape[0]
    size = count // 2

    def rows(seat, half):
        return pl.ds(seat * count + half * size, size)

    return Gather(
        C,
        lambda half: x_ref.at[pl.ds(half * size, size)],
        lambda seat, half: out_ref.at[0, rows(seat, half)],
        lambda seat, half: out_ref.at[1, rows(seat, half)],
        lambda seat, half: out_ref.at[1, rows(seat, half)],
        sems,
    )


class Ring:
    def __init__(self, Z, block, sent, came, way=1):
        dp, ctx, _ = places_of()
        self.Z, self.z, self.block, self.sems, self.way = Z, lax.div(dp, 2), block, (sent, came), way
        self.ahead = lax.rem(dp + 2 * Z + 2 * way, 2 * Z), ctx
        self.behind = lax.rem(dp + 2 * Z - 2 * way, 2 * Z), ctx

    def hop(self, step):
        spot = self.block(lax.rem(self.z + self.Z - self.way * step, self.Z))
        return remote(spot, spot, self.sems[0].at[step], self.sems[1].at[step], self.ahead)

    def landed(self, step):
        spot = self.block(lax.rem(self.z + 2 * self.Z - self.way * (1 + step), self.Z))
        remote(spot, spot, self.sems[0].at[step], self.sems[1].at[step], self.behind).wait_recv()

    def sent(self):
        for step in range(self.Z - 1):
            self.hop(step).wait_send()


def lines_gather(C, line_ref, out_ref, sems):
    dp, ctx, _ = places_of()
    core = lax.rem(dp, 2)
    size = line_ref.shape[0] // 2

    def slot(side, seat, half):
        return out_ref.at[pl.ds(half * size, size), side * C + seat]

    return Gather(
        C,
        lambda half: line_ref.at[pl.ds(half * size, size)],
        lambda seat, half: slot(core, seat, half),
        lambda seat, half: slot(core, seat, half),
        lambda seat, half: slot(1 - core, seat, half),
        sems,
    )


def gather_sems(C):
    return [pltpu.SemaphoreType.DMA((2, C))] * 4


def plane_neighbours(C):
    dp, ctx, twin = places_of()
    return [(dp, flipped(ctx, bit)) for bit in bit_orders(C)[0]] + [(twin, ctx)]


def comm_params(number, megabytes=16):
    return pltpu.CompilerParams(
        collective_id=number, has_side_effects=True, vmem_limit_bytes=megabytes * 2**20
    )


def cost_of(microseconds):
    return pl.CostEstimate(flops=int(microseconds * 1e6), bytes_accessed=1024, transcendentals=0)


def gather_kernel(C, x_ref, out_ref, own_sem, *sems):
    greet(plane_neighbours(C))
    count = x_ref.shape[0]
    own = pltpu.make_async_copy(
        x_ref, out_ref.at[0, pl.ds(lax.axis_index("ctx") * count, count)], own_sem
    )
    gather = rows_gather(C, x_ref, out_ref, sems)
    for index in range(C):
        gather.step(index)
        if index == 0:
            own.start()
    own.wait()
    gather.finish()


def gather_rows(x, C, number):
    return pl.pallas_call(
        functools.partial(gather_kernel, C),
        out_shape=jax.ShapeDtypeStruct((2, C * x.shape[0], x.shape[1]), x.dtype),
        in_specs=[ANY],
        out_specs=ANY,
        scratch_shapes=[pltpu.SemaphoreType.DMA] + gather_sems(C),
        compiler_params=comm_params(number),
        cost_estimate=cost_of(40),
        name="gather_rows",
    )(x)


def plane_peers(C):
    dp, ctx, twin = places_of()
    peers = [(there, flipped(ctx, mask)) for there in (dp, twin) for mask in range(C)]
    return list(enumerate(peers))[1:]


def place_in_plane(C, device):
    return lax.rem(device[0], 2) * C + device[1]


class Deal:
    def __init__(self, C, weights, wide, blocks, out_ref, row_at, sent, came, own_sem):
        self.C, self.out, self.wide, self.sems = C, out_ref, wide, (sent, came, own_sem)
        self.peers, self.row_at = plane_peers(C), row_at
        self.shard = weights[0].shape[0]
        dp, ctx, _ = places_of()
        self.parts = []
        for weight in weights:
            for block in range(blocks):
                self.parts.append((weight, block * 2 * C))
        self.own_device = (dp, ctx)
        self.copies = []

    def spot(self, device, number):
        rows = pl.ds(self.row_at(device), self.shard)
        return self.out.at[rows, pl.ds(number * self.wide, self.wide)]

    def start(self):
        sent, came, own_sem = self.sems
        for number, (weight, first) in enumerate(self.parts):
            for index, device in [(0, self.own_device)] + self.peers:
                at = (first + place_in_plane(self.C, device)) * self.wide
                source = weight.at[:, pl.ds(pl.multiple_of(at, 128), self.wide)]
                target = self.spot(self.own_device, number)
                if index == 0:
                    copy = pltpu.make_async_copy(source, target, own_sem.at[number])
                else:
                    copy = remote(
                        source, target, sent.at[number, index], came.at[number, index], device
                    )
                copy.start()
                self.copies.append((copy, index))

    def landed(self):
        sent, came, _ = self.sems
        for number in range(len(self.parts)):
            for index, device in self.peers:
                spot = self.spot(device, number)
                remote(
                    spot, spot, sent.at[number, index], came.at[number, index], device
                ).wait_recv()
        for copy, index in self.copies:
            if index:
                copy.wait_send()
            else:
                copy.wait()


def deal_sems(C, parts):
    return [
        pltpu.SemaphoreType.DMA((parts, 2 * C)),
        pltpu.SemaphoreType.DMA((parts, 2 * C)),
        pltpu.SemaphoreType.DMA((parts,)),
    ]


def first_kernel(C, Z, dealt, *refs):
    x_ref, wq_ref, wk_ref, wv_ref, wo_ref, gains_ref = refs[:6]
    refs = refs[6:]
    if dealt:
        (wg_ref, wu_ref), refs = refs[:2], refs[2:]
    x_out, w_out, wo_out, gains_line, gains_out = refs[:5]
    refs = refs[5:]
    if dealt:
        gu_out, refs = refs[0], refs[1:]
    own_sem, ring_sent, ring_came, gather_set, refs = refs[0], refs[1], refs[2], refs[3:7], refs[7:]
    gains_set, deal_set, refs = refs[:4], refs[4:7], refs[7:]
    A = 2 * C
    dp, ctx, _ = places_of()
    z, place = lax.div(dp, 2), lax.rem(dp, 2) * C + ctx
    shard = wq_ref.shape[0]
    rings = [
        Ring(Z, lambda at: gains_line.at[at], ring_sent.at[0], ring_came.at[0]),
        Ring(Z, lambda at: wo_out.at[at], ring_sent.at[1], ring_came.at[1]),
    ]
    size = A * shard // 2
    for half, way in enumerate((1, -1)):
        rings.append(
            Ring(
                Z,
                lambda at, half=half: w_out.at[pl.ds(at * (A * shard) + half * size, size)],
                ring_sent.at[2 + half],
                ring_came.at[2 + half],
                way,
            )
        )
    greet([device for _, device in plane_peers(C)] + [rings[0].ahead, rings[0].behind])
    lines = [
        pltpu.make_async_copy(gains_ref, gains_line.at[z], own_sem.at[0]),
        pltpu.make_async_copy(wo_ref, wo_out.at[z], own_sem.at[1]),
    ]
    for line in lines:
        line.start()
    deal = Deal(
        C, (wq_ref, wk_ref, wv_ref), wq_ref.shape[1] // A, 1, w_out,
        lambda device: (device[0] * C + device[1]) * shard, *deal_set,
    )
    deal.start()
    for line, ring in zip(lines, rings):
        line.wait()
        ring.hop(0).start()
    count = x_ref.shape[0]
    own = pltpu.make_async_copy(x_ref, x_out.at[0, pl.ds(ctx * count, count)], own_sem.at[2])
    own.start()
    gather = rows_gather(C, x_ref, x_out, gather_set)
    gather.step(0)
    deal.landed()
    for ring in rings[2:]:
        ring.hop(0).start()
    if dealt:
        columns = Deal(
            C, (wg_ref, wu_ref), wg_ref.shape[1] // (Z * A), Z, gu_out,
            lambda device: place_in_plane(C, device) * shard, *refs,
        )
        columns.start()
    for step in range(Z - 2):
        for ring in rings:
            ring.landed(step)
            ring.hop(step + 1).start()
        if step + 1 < C:
            gather.step(step + 1)
    for ring in rings[:2]:
        ring.landed(Z - 2)
    own_gains = pltpu.make_async_copy(gains_line, gains_out.at[:, place], own_sem.at[3])
    own_gains.start()
    for index in range(Z - 1, C):
        gather.step(index)
    gains = lines_gather(C, gains_line, gains_out, gains_set)
    for index in range(C):
        gains.step(index)
    if dealt:
        columns.landed()
    own.wait()
    own_gains.wait()
    gather.finish()
    gains.finish()
    for ring in rings[2:]:
        ring.landed(Z - 2)
    for ring in rings:
        ring.sent()


def first_gather(x, w_query, w_key, w_value, w_out, gains, w_gate, w_up, dealt, C, Z, number):
    width = x.shape[1]
    A = 2 * C
    shard = w_query.shape[0]

    def shape(*sizes):
        return jax.ShapeDtypeStruct(sizes, x.dtype)

    outs = [
        shape(2, C * x.shape[0], width),
        shape(width, 3 * width // A),
        shape(Z, shard, width),
        shape(Z, *gains.shape),
        shape(Z, A, *gains.shape),
    ]
    operands = [x, w_query, w_key, w_value, w_out, gains]
    scratch = (
        [pltpu.SemaphoreType.DMA((4,))]
        + [pltpu.SemaphoreType.DMA((4, Z))] * 2
        + gather_sems(C) * 2
        + deal_sems(C, 3)
    )
    if dealt:
        operands += [w_gate, w_up]
        outs.append(shape(A * shard, 2 * w_gate.shape[1] // A))
        scratch += deal_sems(C, 2 * Z)
    return pl.pallas_call(
        functools.partial(first_kernel, C, Z, dealt),
        out_shape=tuple(outs),
        in_specs=[ANY] * len(operands),
        out_specs=(ANY,) * len(outs),
        scratch_shapes=scratch,
        compiler_params=comm_params(number, 60),
        cost_estimate=cost_of(100),
        name="first_gather",
    )(*operands)


ROWS = 256


def row_of_sums(values):
    high = values.astype(BF16)
    rest = (values - high.astype(F32)).astype(BF16)
    ones = jnp.ones((8, values.shape[1]), BF16)
    return dot(ones, high, 1, 1) + dot(ones, rest, 1, 1)


def pair_of_rows(first, second):
    return jnp.where(lax.broadcasted_iota(jnp.int32, first.shape, 0) == 0, first, second)


def columns_of(rows):
    eye = (
        lax.broadcasted_iota(jnp.int32, (8, 8), 0) == lax.broadcasted_iota(jnp.int32, (8, 8), 1)
    ).astype(BF16)
    high = rows.astype(BF16)
    rest = rows - high.astype(F32)
    middle = rest.astype(BF16)
    low = (rest - middle.astype(F32)).astype(BF16)
    return dot(high, eye, 0, 0) + dot(middle, eye, 0, 0) + dot(low, eye, 0, 0)


def start_sum(C, stats, landing, sent, came):
    for index, device in plane_peers(C):
        remote(stats, landing.at[index], sent.at[index], came.at[index], device).start()


def finish_sum(C, stats, landing, sent, came, total):
    blocks = stats.shape[0]
    for index, device in plane_peers(C):
        remote(stats, landing.at[index], sent.at[index], came.at[index], device).wait()
    for block in range(blocks):
        value = stats[block]
        for index in range(1, 2 * C):
            value = value + landing[index, block if index < C else (block + blocks // 2) % blocks]
        total[block] = value


def turned(value, cosine, sine):
    return value * cosine + pltpu.roll(value, HD // 2, 1) * sine


def project_kernel(
    C, x_ref, w_ref, gain_ref, cos_ref, sin_ref, line_ref,
    rq_ref, rk_ref, v_ref, q_ref, k_ref, total, out_ref,
    own_sem, ctx_sent, ctx_came, core_sent, core_came, stats, landing, sent, came,
):
    greet([device for _, device in plane_peers(C)])
    dp, ctx, _ = places_of()
    gather = lines_gather(C, line_ref, out_ref, (ctx_sent, ctx_came, core_sent, core_came))
    own = pltpu.make_async_copy(line_ref, out_ref.at[:, lax.rem(dp, 2) * C + ctx], own_sem)
    own.start()
    gather.step(0)
    wide = rq_ref.shape[1]
    width = x_ref.shape[1]
    blocks = stats.shape[0]

    def rows_at(block):
        return pl.ds(pl.multiple_of(block * ROWS, ROWS), ROWS)

    @pl.loop(0, blocks)
    def _(block):
        here = rows_at(block)
        raw = dot(x_ref[here, :], w_ref[...], 1, 0)
        query, key = raw[:, :wide], raw[:, wide : 2 * wide]
        rq_ref[here, :] = query
        rk_ref[here, :] = key
        v_ref[here, :] = raw[:, 2 * wide :].astype(BF16)
        stats[block] = pair_of_rows(row_of_sums(query * query), row_of_sums(key * key))

    start_sum(C, stats, landing, sent, came)
    finish_sum(C, stats, landing, sent, came, total)
    gather.step(1)

    @pl.loop(0, blocks)
    def _(block):
        here = rows_at(block)
        factors = columns_of(lax.rsqrt(total[block] * (1.0 / width) + EPS))
        cosine, sine = cos_ref[here, :], sin_ref[here, :]
        for which, (raw, out) in enumerate(((rq_ref, q_ref), (rk_ref, k_ref))):
            factor = factors[:, which : which + 1]
            for head in range(wide // HD):
                lanes = slice(head * HD, (head + 1) * HD)
                value = raw[here, lanes] * factor * gain_ref[which : which + 1, lanes]
                out[here, lanes] = turned(value, cosine, sine).astype(BF16)

    for index in range(2, C):
        gather.step(index)
    own.wait()
    gather.finish()


def plane_sum_scratch(C, blocks):
    return [
        pltpu.VMEM((blocks, 8, ROWS), F32),
        pltpu.VMEM((2 * C, blocks, 8, ROWS), F32),
        pltpu.SemaphoreType.DMA((2 * C,)),
        pltpu.SemaphoreType.DMA((2 * C,)),
    ]


VM = pl.BlockSpec(memory_space=pltpu.VMEM)


def project(x, w, gains, cosine, sine, lines, C, number):
    total, width = x.shape
    wide = w.shape[1] // 3
    blocks = total // ROWS
    raw = jax.ShapeDtypeStruct((total, wide), F32)
    low = jax.ShapeDtypeStruct((total, wide), BF16)
    return pl.pallas_call(
        functools.partial(project_kernel, C),
        out_shape=(
            raw, raw, low, low, low,
            jax.ShapeDtypeStruct((blocks, 8, ROWS), F32),
            jax.ShapeDtypeStruct((lines.shape[0], 2 * C) + lines.shape[1:], BF16),
        ),
        in_specs=[VM] * 5 + [ANY],
        out_specs=(VM,) * 6 + (ANY,),
        scratch_shapes=[pltpu.SemaphoreType.DMA] + gather_sems(C) + plane_sum_scratch(C, blocks),
        compiler_params=comm_params(number, 48),
        cost_estimate=cost_of(18),
        name="project",
    )(x, w, gains, cosine, sine, lines)


def project_back_kernel(
    C, dq_ref, dk_ref, dv_ref, rq_ref, rk_ref, total, gain_ref, cos_ref, sin_ref, known_ref, deal_ref,
    out_ref, sum_ref, dealt_ref, deal_sent, deal_came, deal_own, term_ref, own_terms, all_terms, terms_sent, terms_came,
    eq, ek, inner, stats, landing, sent, came,
):
    greet([device for _, device in plane_peers(C)])
    wide = rq_ref.shape[1]
    width = wide * 2 * C
    blocks = stats.shape[0]

    def rows_at(block):
        return pl.ds(pl.multiple_of(block * ROWS, ROWS), ROWS)

    Z, shard, _ = dealt_ref.shape
    dp, ctx, _ = places_of()
    line = dp - lax.rem(dp, 2)
    seat = place_in_plane(C, (dp, ctx))

    def deal(number):
        at = seat * Z + number
        to = lax.rem(at, 2 * C)
        source, target = deal_ref.at[pl.ds(number * shard, shard)], dealt_ref.at[lax.div(at, 2 * C)]
        device = line + lax.div(to, C), lax.rem(to, C)
        away = remote(source, target, deal_sent.at[number], deal_came.at[lax.div(at, 2 * C)], device)
        return to, away, pltpu.make_async_copy(source, target, deal_own.at[number])

    for number in range(Z):
        to, away, stay = deal(number)

        @pl.when(to != seat)
        def _():
            away.start()

        @pl.when(to == seat)
        def _():
            stay.start()

    def factors_of(block):
        return columns_of(lax.rsqrt(total[block] * (1.0 / width) + EPS))

    term_ref[...] = jnp.zeros_like(term_ref)

    @pl.loop(0, blocks)
    def _(block):
        here = rows_at(block)
        factors = factors_of(block)
        cosine, sine = cos_ref[here, :], sin_ref[here, :]
        sums = []
        for which, (grad, raw, kept) in enumerate(((dq_ref, rq_ref, eq), (dk_ref, rk_ref, ek))):
            for head in range(wide // HD):
                lanes = slice(head * HD, (head + 1) * HD)
                kept[here, lanes] = turned(grad[here, lanes], cosine, -sine)
            product = kept[here, :] * raw[here, :] * factors[:, which : which + 1]
            term_ref[which : which + 1, :] += jnp.sum(product, axis=0, keepdims=True)
            sums.append(row_of_sums(product * gain_ref[which : which + 1, :]))
        stats[block] = pair_of_rows(*sums)

    start_sum(C, stats, landing, sent, came)
    lanes = pl.ds(pl.multiple_of(seat * wide, 128), wide)
    own_terms[...] = known_ref[...]
    own_terms[:, lanes] = own_terms[:, lanes] + term_ref[...]
    for index, device in plane_peers(C):
        remote(
            own_terms, all_terms.at[index], terms_sent.at[index], terms_came.at[index], device
        ).start()
    finish_sum(C, stats, landing, sent, came, inner)

    @pl.loop(0, blocks)
    def _(block):
        here = rows_at(block)
        factors = factors_of(block)
        means = columns_of(inner[block] * (1.0 / width))
        for which, (kept, raw) in enumerate(((eq, rq_ref), (ek, rk_ref))):
            factor, mean = factors[:, which : which + 1], means[:, which : which + 1]
            weighted = kept[here, :] * gain_ref[which : which + 1, :]
            value = factor * (weighted - raw[here, :] * factor * mean)
            out_ref[here, which * wide : (which + 1) * wide] = value.astype(BF16)
        out_ref[here, 2 * wide :] = dv_ref[here, :].astype(BF16)

    terms = own_terms[...]
    for index, device in plane_peers(C):
        remote(
            own_terms, all_terms.at[index], terms_sent.at[index], terms_came.at[index], device
        ).wait()
        terms = terms + all_terms[index]
    sum_ref[...] = terms
    for number in range(Z):
        to, away, stay = deal(number)

        @pl.when(to != seat)
        def _():
            away.wait_send()

        @pl.when(to == seat)
        def _():
            stay.wait()

    for number in range(Z):
        origin = lax.div(number * 2 * C + seat, Z)
        spot = dealt_ref.at[number]
        device = line + lax.div(origin, C), lax.rem(origin, C)

        @pl.when(origin != seat)
        def _():
            remote(spot, spot, deal_sent.at[number], deal_came.at[number], device).wait_recv()


def project_back(dq, dk, dv, raw_q, raw_k, sums, gains, cosine, sine, terms, dealt, C, Z, number):
    total, wide = dq.shape
    blocks = total // ROWS
    return pl.pallas_call(
        functools.partial(project_back_kernel, C),
        out_shape=(
            jax.ShapeDtypeStruct((total, 3 * wide), BF16),
            jax.ShapeDtypeStruct(terms.shape, F32),
            jax.ShapeDtypeStruct((Z, dealt.shape[0] // Z, dealt.shape[1]), BF16),
        ),
        in_specs=[VM] * 10 + [ANY],
        out_specs=(VM, VM, ANY),
        scratch_shapes=[
            pltpu.SemaphoreType.DMA((Z,)),
            pltpu.SemaphoreType.DMA((Z,)),
            pltpu.SemaphoreType.DMA((Z,)),
            pltpu.VMEM((8, wide), F32),
            pltpu.VMEM(terms.shape, F32),
            pltpu.VMEM((2 * C,) + terms.shape, F32),
            pltpu.SemaphoreType.DMA((2 * C,)),
            pltpu.SemaphoreType.DMA((2 * C,)),
            pltpu.VMEM((total, wide), F32),
            pltpu.VMEM((total, wide), F32),
            pltpu.VMEM((blocks, 8, ROWS), F32),
        ]
        + plane_sum_scratch(C, blocks),
        compiler_params=comm_params(number, 48),
        cost_estimate=cost_of(15),
        name="project_back",
    )(dq, dk, dv, raw_q, raw_k, sums, gains, cosine, sine, terms, dealt)


def attention_out_kernel(
    C, attended_ref, w_ref, tokens_ref, gain_ref, heads, proj, hidden_ref, h_out,
    low, own_sem, part_sent, part_came, copy_sem, *sems,
):
    count, width = tokens_ref.shape
    wide = width // (2 * C)
    dp, ctx, _ = places_of()
    here = place_in_plane(C, (dp, ctx))
    peers = plane_peers(C)
    greet([device for _, device in peers])

    def columns(at):
        return heads.at[:, pl.ds(pl.multiple_of(at * wide, 128), wide)]

    own = pltpu.make_async_copy(attended_ref.at[pl.ds(ctx * count, count)], columns(here), own_sem)
    own.start()
    copies = []
    for index, device in peers:
        rows = pl.ds(index // C * (C * count) + device[1] * count, count)
        copy = remote(
            attended_ref.at[rows], columns(here), part_sent.at[index], part_came.at[index], device
        )
        copy.start()
        copies.append(copy)
    own.wait()
    for index, device in peers:
        spot = columns(place_in_plane(C, device))
        remote(spot, spot, part_sent.at[index], part_came.at[index], device).wait_recv()
    for copy in copies:
        copy.wait_send()
    outs, size = tiles(width, 512)

    @pl.loop(0, outs)
    def _(number):
        lanes = at_tile(number, size)
        proj[:, lanes] = dot(heads[...], w_ref[:, lanes], 1, 0)

    chunks, chunk = tiles(count, 32)
    gain = gain_ref[0:1, :]

    @pl.loop(0, chunks)
    def _(number):
        rows = at_tile(number, chunk)
        value = proj[rows, :]
        factor = lax.rsqrt(jnp.mean(value * value, axis=-1, keepdims=True) + EPS)
        hidden = tokens_ref[rows, :].astype(F32) + value * factor * gain
        hidden_ref[rows, :] = hidden
        low[rows, :] = hidden.astype(BF16)

    gather = rows_gather(C, low, h_out, sems)
    copy = pltpu.make_async_copy(low, h_out.at[0, pl.ds(ctx * count, count)], copy_sem)
    for index in range(C):
        gather.step(index)
        if index == 0:
            copy.start()
    copy.wait()
    gather.finish()


def attention_out(attended, w, tokens, gain, C, number):
    count, width = tokens.shape
    whole = jax.ShapeDtypeStruct((count, width), F32)
    return pl.pallas_call(
        functools.partial(attention_out_kernel, C),
        out_shape=(
            jax.ShapeDtypeStruct((count, width), BF16),
            whole,
            whole,
            jax.ShapeDtypeStruct((2, C * count, width), BF16),
        ),
        in_specs=[VM] * 4,
        out_specs=(VM, VM, VM, ANY),
        scratch_shapes=[
            pltpu.VMEM((count, width), BF16),
            pltpu.SemaphoreType.DMA,
            pltpu.SemaphoreType.DMA((2 * C,)),
            pltpu.SemaphoreType.DMA((2 * C,)),
            pltpu.SemaphoreType.DMA,
        ]
        + gather_sems(C),
        compiler_params=comm_params(number, 60),
        cost_estimate=cost_of(60),
        name="attention_out",
    )(attended, w, tokens, gain)


def return_kernel(C, groups, blocks, x_ref, *refs):
    out, landing, sent, came, own_sem, *refs = refs
    A = 2 * C
    shard = landing.shape[1]
    part = out.shape[1] // (blocks * A)
    wide = groups * blocks * part
    dp, ctx, _ = places_of()
    own_at = place_in_plane(C, (dp, ctx))
    peers = plane_peers(C)
    greet([device for _, device in peers])
    own = pltpu.make_async_copy(
        x_ref.at[pl.ds(own_at * shard, shard), pl.ds(0, wide)], landing.at[own_at], own_sem
    )
    own.start()
    if refs:
        kept, kept_sem = refs
        stay = pltpu.make_async_copy(x_ref.at[:, pl.ds(wide, kept.shape[1])], kept, kept_sem)
        stay.start()

    def copy_to(index, device):
        rows = pl.ds(place_in_plane(C, device) * shard, shard)
        return remote(
            x_ref.at[rows, pl.ds(0, wide)],
            landing.at[own_at],
            sent.at[index],
            came.at[index],
            device,
        )

    def landed(index, device):
        spot = landing.at[place_in_plane(C, device)]
        remote(spot, spot, sent.at[index], came.at[index], device).wait_recv()

    for index, device in peers:
        copy_to(index, device).start()
    own.wait()
    for index, device in peers:
        landed(index, device)
    for index, device in peers:
        copy_to(index, device).wait_send()
    for group in range(groups):
        for block in range(blocks):
            for at in range(A):
                lanes = (group * blocks + block) * part
                to = (block * A + at) * part
                rows = slice(group * shard, (group + 1) * shard)
                out[rows, to : to + part] = landing[at, :, lanes : lanes + part]
    if refs:
        stay.wait()
        size = kept.shape[1]
        for at in range(A):
            rows, lanes = slice(at * shard, (at + 1) * shard), slice(at * size, (at + 1) * size)
            out[groups * shard : (groups + 1) * shard, lanes] = kept[rows, :]


def return_rows(x, wide, C, groups, blocks, number):
    A = 2 * C
    shard = x.shape[0] // A
    more = x.shape[1] - wide
    scratch = [
        pltpu.VMEM((A, shard, wide), x.dtype),
        pltpu.SemaphoreType.DMA((A,)),
        pltpu.SemaphoreType.DMA((A,)),
        pltpu.SemaphoreType.DMA,
    ]
    if more:
        scratch += [pltpu.VMEM((x.shape[0], more), x.dtype), pltpu.SemaphoreType.DMA]
    return pl.pallas_call(
        functools.partial(return_kernel, C, groups, blocks),
        out_shape=jax.ShapeDtypeStruct(
            ((groups + (more > 0)) * shard, wide * A // groups), x.dtype
        ),
        in_specs=[ANY],
        out_specs=VM,
        scratch_shapes=scratch,
        compiler_params=comm_params(number, 24),
        cost_estimate=cost_of(20),
        name="return_rows",
    )(x)


class Scatter:
    def __init__(self, C, count, own, other, twin_part, landing, sems, final):
        self.C, self.count, self.half = C, count, count // 2
        self.own, self.other, self.twin_part, self.landing = own, other, twin_part, landing
        self.core_sent, self.core_came, self.ctx_sent, self.ctx_came = sems
        self.dp, self.ctx, self.twin = places_of()
        self.onward = [{m: (bits, bit) for m, bits, bit in tree(order)} for order in bit_orders(C)]
        self.final = final

    def rows(self, half, mask):
        return pl.ds(flipped(self.ctx, mask) * self.count + half * self.half, self.half)

    def block(self, mask):
        return pl.ds(flipped(self.ctx, mask) * self.count, self.count)

    def across(self, half, mask):
        return remote(
            self.other.at[self.rows(half, mask)],
            self.twin_part.at[self.rows(half, mask)],
            self.core_sent.at[half, mask],
            self.core_came.at[half, mask],
            (self.twin, self.ctx),
        )

    def back(self, half, mask, bit):
        return remote(
            self.own.at[self.rows(half, mask)],
            self.landing.at[half, mask],
            self.ctx_sent.at[half, mask],
            self.ctx_came.at[half, mask],
            (self.dp, flipped(self.ctx, bit)),
        )

    def settle(self, half, mask):
        along, bit = self.onward[half][mask]
        self.across(half, mask).wait_recv()
        here = self.rows(half, mask)
        total = self.own[here, :].astype(F32) + self.twin_part[here, :].astype(F32)
        for came in along:
            self.back(half, mask | came, came).wait_recv()
            total = total + self.landing[half, mask | came].astype(F32)
        if mask:
            self.own[here, :] = total.astype(BF16)
            self.back(half, mask, bit).start()
        else:
            self.final(half, total)

    def order(self):
        return sorted(range(self.C), key=lambda mask: (-bin(mask).count("1"), mask))

    def run(self, compute):
        waiting = []
        for mask in self.order():
            compute(1, mask)
            for half in range(2):
                self.across(half, mask).start()
            compute(0, mask)
            ready = [half for half in range(2) if mask and not self.onward[half][mask][0]]
            for half in ready:
                self.settle(half, mask)
            for half, earlier in waiting:
                self.settle(half, earlier)
            waiting = [(half, mask) for half in range(2) if half not in ready]
        for half, earlier in waiting:
            self.settle(half, earlier)
        for half in range(2):
            for mask in range(self.C):
                self.across(half, mask).wait_send()
                if mask:
                    self.back(half, mask, self.onward[half][mask][1]).wait_send()


def scatter_scratch(C, count, width):
    rows = pltpu.VMEM((C * count, width), BF16)
    return [rows, rows, rows, pltpu.VMEM((2, C, count // 2, width), BF16)] + [
        pltpu.SemaphoreType.DMA((2, C))
    ] * 4


def tiles(total, size):
    size = min(total, size)
    return total // size, size


def at_tile(number, size, base=0):
    return pl.ds(pl.multiple_of(base + number * size, size), size)


def mix_kernel(h_ref, wgu_ref, gu_ref, mixed_ref, turned_ref):
    ffn = mixed_ref.shape[1]
    steps, tile = tiles(ffn, 256)
    for number in range(steps):
        first = slice(number * tile, (number + 1) * tile)
        second = slice(ffn + number * tile, ffn + (number + 1) * tile)
        gate = dot(h_ref[...], wgu_ref[:, first], 1, 0)
        up = dot(h_ref[...], wgu_ref[:, second], 1, 0)
        gu_ref[:, first] = gate.astype(BF16)
        gu_ref[:, second] = up.astype(BF16)
        mixed = gate * jax.nn.sigmoid(gate) * up
        mixed_ref[:, first] = mixed.astype(BF16)
        turned_ref[first, :] = mixed.T.astype(BF16)


def mix(h, w_gate_up):
    total, width = h.shape
    ffn = w_gate_up.shape[1] // 2
    rows = min(256, total)
    return pl.pallas_call(
        mix_kernel,
        out_shape=(
            jax.ShapeDtypeStruct((total, 2 * ffn), BF16),
            jax.ShapeDtypeStruct((total, ffn), BF16),
            jax.ShapeDtypeStruct((ffn, total), BF16),
        ),
        grid=(total // rows,),
        in_specs=[
            pl.BlockSpec((rows, width), lambda i: (i, 0)),
            pl.BlockSpec((width, 2 * ffn), lambda i: (0, 0)),
        ],
        out_specs=(
            pl.BlockSpec((rows, 2 * ffn), lambda i: (i, 0)),
            pl.BlockSpec((rows, ffn), lambda i: (i, 0)),
            pl.BlockSpec((ffn, rows), lambda i: (0, i)),
        ),
        compiler_params=pltpu.CompilerParams(vmem_limit_bytes=60 * 2**20),
        cost_estimate=cost_of(20),
        name="mix",
    )(h, w_gate_up)


def feed_forward_kernel(
    C, mixed_ref, turned_ref, gu_ref, first_wd, second_wd, hidden_in, cot_in, gain_ref,
    out_hbm, b_out, down_hbm, term_ref,
    wd_ref, hidden_ref, cot_ref, out_ref,
    mixed_buf, proj, f_own, f_all, turned_buf, gu_buf, b_buf, total,
    mixed_sem, turned_sem, gu_sem, b_sem, down_sem, load_sem,
    ctx_sent, ctx_came, core_sent, core_came,
    own, other, twin_part, landing, *sems,
):
    split = first_wd.shape[1]
    loads = [
        pltpu.make_async_copy(first_wd, wd_ref.at[:, pl.ds(0, split)], load_sem.at[0]),
        pltpu.make_async_copy(
            second_wd, wd_ref.at[:, pl.ds(split, second_wd.shape[1])], load_sem.at[1]
        ),
        pltpu.make_async_copy(hidden_in, hidden_ref, load_sem.at[2]),
        pltpu.make_async_copy(cot_in, cot_ref, load_sem.at[3]),
    ]
    for load in loads:
        load.start()
    greet(plane_neighbours(C))
    count, width = hidden_ref.shape
    ffn = wd_ref.shape[0]
    seq = C * count
    half_rows = count // 2

    def final(half, value):
        proj[pl.ds(half * half_rows, half_rows), :] = value

    scatter = Scatter(C, count, own, other, twin_part, landing, sems, final)
    sequence = [(side, mask) for mask in scatter.order() for side in (1, 0)]

    def rows_of(side, mask):
        return pl.ds(pl.multiple_of(side * seq + flipped(scatter.ctx, mask) * count, count), count)

    def fetch(index):
        return pltpu.make_async_copy(
            mixed_ref.at[rows_of(*sequence[index])], mixed_buf.at[index % 2], mixed_sem.at[index % 2]
        )

    fetch(0).start()
    steps, tile = tiles(ffn, 256)
    outs, wide = tiles(width, 512)

    def compute(side, mask):
        index = sequence.index((side, mask))
        slot = index % 2
        fetch(index).wait()
        if index + 1 < len(sequence):
            fetch(index + 1).start()
        target, here = (own, other)[side], scatter.block(mask)

        @pl.loop(0, outs)
        def _(number):
            lanes = at_tile(number, wide)
            target[here, lanes] = dot(mixed_buf[slot], wd_ref[:, lanes], 1, 0).astype(BF16)

    for load in loads[:2]:
        load.wait()
    scatter.run(compute)
    for load in loads[2:]:
        load.wait()
    gain = gain_ref[0:1, :]
    term_ref[...] = jnp.zeros_like(term_ref)
    chunks, chunk = tiles(count, 32)

    @pl.loop(0, chunks)
    def _(number):
        here = at_tile(number, chunk)
        value = proj[here, :]
        factor = lax.rsqrt(jnp.mean(value * value, axis=-1, keepdims=True) + EPS)
        unit = value * factor
        out_ref[here, :] = hidden_ref[here, :] + unit * gain
        incoming = cot_ref[here, :].astype(F32)
        weighted = incoming * gain
        inner = jnp.mean(weighted * unit, axis=-1, keepdims=True)
        f_own[here, :] = (factor * (weighted - unit * inner)).astype(BF16)
        term_ref[0:1, :] += jnp.sum(incoming * unit, axis=0, keepdims=True)

    gather = rows_gather(C, f_own, f_all, (ctx_sent, ctx_came, core_sent, core_came))
    output = pltpu.make_async_copy(out_ref, out_hbm, load_sem.at[4])
    blocks = [
        (side, mask, index)
        for index in range(C)
        for mask in gather.complete(index)
        for side in (0, 1)
    ]

    def fetch_kept(number):
        side, mask, _ = blocks[number]
        slot, rows = number % 2, rows_of(side, mask)
        return (
            pltpu.make_async_copy(turned_ref.at[:, rows], turned_buf.at[slot], turned_sem.at[slot]),
            pltpu.make_async_copy(gu_ref.at[rows], gu_buf.at[slot], gu_sem.at[slot]),
        )

    def keep(number):
        side, mask, _ = blocks[number]
        return pltpu.make_async_copy(
            b_buf.at[number % 2], b_out.at[rows_of(side, mask)], b_sem.at[number % 2]
        )

    def sum_out(at):
        lanes = pl.ds(at * wide, wide)
        rows = pl.ds(0, ffn)
        return pltpu.make_async_copy(
            other.at[rows, lanes], down_hbm.at[:, lanes], down_sem.at[at]
        )

    def back(number, grads):
        slot = number % 2
        for arrived in fetch_kept(number):
            arrived.wait()
        if number >= 2:
            keep(number - 2).wait()

        @pl.loop(0, steps)
        def _(at):
            first, second = at_tile(at, tile), at_tile(at, tile, ffn)
            grad = dot(grads[...], wd_ref[first, :], 1, 1)
            gate, up = gu_buf[slot, :, first].astype(F32), gu_buf[slot, :, second].astype(F32)
            sig = jax.nn.sigmoid(gate)
            b_buf[slot, :, first] = (grad * up * sig * (1.0 + gate * (1.0 - sig))).astype(BF16)
            b_buf[slot, :, second] = (grad * (gate * sig)).astype(BF16)

        keep(number).start()

        if number < len(blocks) - 1:

            @pl.loop(0, outs)
            def _(at):
                lanes = at_tile(at, wide)
                value = dot(turned_buf[slot], grads[:, lanes], 1, 0)
                if number == 0:
                    total[:, lanes] = value
                else:
                    total[:, lanes] += value

        else:
            for at in range(outs):
                lanes = slice(at * wide, (at + 1) * wide)
                value = dot(turned_buf[slot], grads[:, lanes], 1, 0)
                other[0:ffn, lanes] = (total[:, lanes] + value).astype(BF16)
                sum_out(at).start()

    for arriving in fetch_kept(0):
        arriving.start()
    done = 0
    for index in range(C):
        gather.step(index)
        if index == 0:
            output.start()
        while done < len(blocks) and blocks[done][2] == index:
            side, mask, _ = blocks[done]
            if done + 1 < len(blocks):
                for arriving in fetch_kept(done + 1):
                    arriving.start()
            if (side, mask) == (0, 0):
                back(done, f_own)
            else:
                if side:
                    for half in range(2):
                        gather.crossed(half, mask)
                back(done, f_all.at[side, scatter.block(mask)])
            done += 1
    for number in (len(blocks) - 2, len(blocks) - 1):
        keep(number).wait()
    for at in range(outs):
        sum_out(at).wait()
    output.wait()
    gather.sent()


def feed_forward(mixed, turned_units, gate_up, w_down, hidden, cotangent, gain, C, number):
    count, width = hidden.shape
    total, ffn = 2 * C * count, w_down[0].shape[0]
    pair = pltpu.SemaphoreType.DMA((2,))
    return pl.pallas_call(
        functools.partial(feed_forward_kernel, C),
        out_shape=(
            jax.ShapeDtypeStruct((count, width), F32),
            jax.ShapeDtypeStruct((total, 2 * ffn), BF16),
            jax.ShapeDtypeStruct((ffn, width), BF16),
            jax.ShapeDtypeStruct((8, width), F32),
        ),
        in_specs=[ANY] * 7 + [VM],
        out_specs=(ANY, ANY, ANY, VM),
        scratch_shapes=[
            pltpu.VMEM((ffn, width), BF16),
            pltpu.VMEM((count, width), F32),
            pltpu.VMEM((count, width), BF16),
            pltpu.VMEM((count, width), F32),
            pltpu.VMEM((2, count, ffn), BF16),
            pltpu.VMEM((count, width), F32),
            pltpu.VMEM((count, width), BF16),
            pltpu.VMEM((2, C * count, width), BF16),
            pltpu.VMEM((2, ffn, count), BF16),
            pltpu.VMEM((2, count, 2 * ffn), BF16),
            pltpu.VMEM((2, count, 2 * ffn), BF16),
            pltpu.VMEM((ffn, width), F32),
            pair,
            pair,
            pair,
            pair,
            pltpu.SemaphoreType.DMA((tiles(width, 512)[0],)),
            pltpu.SemaphoreType.DMA((5,)),
        ]
        + gather_sems(C)
        + scatter_scratch(C, count, width),
        compiler_params=comm_params(number, 60),
        cost_estimate=cost_of(80),
        name="feed_forward",
    )(mixed, turned_units, gate_up, *w_down, hidden, cotangent, gain)


def back_scatter_kernel(C, added, b_ref, w_in, *refs):
    if added:
        add_in, add_ref, refs = refs[0], refs[1], refs[2:]
    out_hbm, out_ref, out_sem, w_ref, load_sem, b_buf, b_sem = refs[:7]
    own, other, twin_part, landing, *sems = refs[7:]
    loads = [pltpu.make_async_copy(w_in, w_ref, load_sem.at[0])]
    if added:
        loads.append(pltpu.make_async_copy(add_in, add_ref, load_sem.at[1]))
    for load in loads:
        load.start()
    greet(plane_neighbours(C))
    count, width = out_ref.shape
    seq = C * count
    half_rows = count // 2

    def final(half, total):
        rows = pl.ds(half * half_rows, half_rows)
        if added:
            total = total + add_ref[rows, :].astype(F32)
        out_ref[rows, :] = total
        leave(half).start()

    def leave(half):
        rows = pl.ds(half * half_rows, half_rows)
        return pltpu.make_async_copy(out_ref.at[rows], out_hbm.at[rows], out_sem.at[half])

    scatter = Scatter(C, count, own, other, twin_part, landing, sems, final)
    sequence = [(side, mask) for mask in scatter.order() for side in (1, 0)]

    def fetch(index):
        side, mask = sequence[index]
        rows = pl.ds(side * seq + flipped(scatter.ctx, mask) * count, count)
        return pltpu.make_async_copy(b_ref.at[rows], b_buf.at[index % 2], b_sem.at[index % 2])

    fetch(0).start()
    outs, wide = tiles(width, 512)

    def compute(side, mask):
        index = sequence.index((side, mask))
        slot = index % 2
        fetch(index).wait()
        if index + 1 < len(sequence):
            fetch(index + 1).start()
        target, here = (own, other)[side], scatter.block(mask)

        @pl.loop(0, outs)
        def _(number):
            lanes = at_tile(number, wide)
            target[here, lanes] = dot(b_buf[slot], w_ref[lanes, :], 1, 1).astype(BF16)

    for load in loads:
        load.wait()
    scatter.run(compute)
    for half in range(2):
        leave(half).wait()


def back_scatter(b, w, add, C, number):
    width = w.shape[0]
    count = b.shape[0] // (2 * C)
    added = add is not None
    scratch = [
        pltpu.VMEM((count, width), F32),
        pltpu.SemaphoreType.DMA((2,)),
        pltpu.VMEM(w.shape, w.dtype),
        pltpu.SemaphoreType.DMA((2,)),
        pltpu.VMEM((2, count, b.shape[1]), BF16),
        pltpu.SemaphoreType.DMA((2,)),
    ] + scatter_scratch(C, count, width)

    def kernel(*refs):
        if added:
            b_ref, w_in, add_in, out_hbm, *rest = refs
            back_scatter_kernel(C, True, b_ref, w_in, add_in, rest[-1], out_hbm, *rest[:-1])
        else:
            back_scatter_kernel(C, False, *refs)

    return pl.pallas_call(
        kernel,
        out_shape=jax.ShapeDtypeStruct((count, width), F32),
        in_specs=[ANY] * (3 if added else 2),
        out_specs=ANY,
        scratch_shapes=scratch + ([pltpu.VMEM(add.shape, add.dtype)] if added else []),
        compiler_params=comm_params(number, 48),
        cost_estimate=cost_of(50),
        name="back_scatter",
    )(*((b, w, add) if added else (b, w)))


def rope_tables(places):
    half = HD // 2
    frequency = THETA ** (-(jnp.arange(half, dtype=F32) * 2.0) / HD)
    angles = places.astype(F32)[:, None] * frequency[None, :]
    cosine, sine = jnp.cos(angles), jnp.sin(angles)
    return jnp.concatenate([cosine, cosine], axis=1), jnp.concatenate([-sine, sine], axis=1)


def row_norm(tensor):
    factor = lax.rsqrt(jnp.mean(tensor * tensor, axis=-1, keepdims=True) + EPS)
    return tensor * factor, factor


def row_norm_back(unit, factor, gain, incoming):
    weighted = incoming * gain
    inner = jnp.mean(weighted * unit, axis=-1, keepdims=True)
    return factor * (weighted - unit * inner), jnp.sum(incoming * unit, axis=0)


def layer(
    ctx_size,
    dp_size,
    tokens,
    w_query,
    w_key,
    w_value,
    w_out,
    gain_query,
    gain_key,
    gain_attn,
    w_gate,
    w_up,
    w_down,
    gain_ffn,
    positions,
    image_starts,
    cotangent,
):
    C, Z = ctx_size, dp_size // 2
    A = 2 * C
    N = Z * A
    ctx, dp = lax.axis_index("ctx"), lax.axis_index("dp")
    core, z = lax.rem(dp, 2), lax.div(dp, 2)
    plane_at = core * C + ctx
    own_at = dp * C + ctx
    rows, width = tokens.shape
    ffn_width = w_gate.shape[1]
    shard = w_query.shape[0]
    down_shard = w_down.shape[0]
    seq_len = rows * C
    slice_width = width // A
    ffn_slice = ffn_width // A
    planes = [[zz * A + p for p in range(A)] for zz in range(Z)]
    columns = [[zz * 2 + k for zz in range(Z)] for k in range(2)]

    def swap(x, bit):
        return lax.ppermute(x, AXES, [(i, i ^ bit) for i in range(N)])

    def rows_of(x, at, count):
        return lax.dynamic_slice_in_dim(x, at, count, 0)

    def gather_z_aside(x):
        return lax.all_gather(x, "dp", axis=0, tiled=True, axis_index_groups=columns)

    def scatter_z_aside(x):
        return lax.psum_scatter(
            x, "dp", scatter_dimension=0, tiled=True, axis_index_groups=columns
        )

    def exchange(x):
        return lax.all_to_all(x, AXES, 0, 0, tiled=True, axis_index_groups=planes)

    split = width * 3 // 4
    first_down = gather_z_aside(w_down[:, :split])
    part = down_shard
    dealt = part % 128 == 0
    gains = jnp.stack([gain_query, gain_key, gain_attn, gain_ffn])
    gains = jnp.pad(gains, ((0, 12), (0, -shard % 128)))
    x_both, full_qkv, out_lines, _, all_gains, *gate_up = first_gather(
        tokens, w_query, w_key, w_value, w_out, gains, w_gate, w_up, dealt, C, Z, 1
    )
    if dealt:
        gate_up = gate_up[0]
    else:
        gate_up = jnp.stack([w.reshape(shard, Z, A, part) for w in (w_gate, w_up)], axis=1)
        gate_up = exchange(gate_up.transpose(3, 0, 1, 2, 4).reshape(A * shard, 2 * ffn_slice))
    full_qkv, gate_up, first_down, w_down = lax.optimization_barrier(
        (full_qkv, gate_up, first_down, w_down)
    )
    second_down = w_down[:, split:]
    full_gate_up = gather_z_aside(gate_up)
    all_gains = all_gains[:, :, :4, :shard].astype(F32).transpose(2, 0, 1, 3).reshape(4, width)
    head_gains = lax.dynamic_slice(all_gains, (0, plane_at * slice_width), (2, slice_width))
    head_gains = jnp.pad(head_gains, ((0, 6), (0, 0)))
    gain_a, gain_f = all_gains[2:3], all_gains[3:4]

    x_all = x_both.reshape(2 * seq_len, width)
    other_dp = dp + 1 - 2 * core
    places = jnp.concatenate(
        [rows_of(positions, dp * seq_len, seq_len), rows_of(positions, other_dp * seq_len, seq_len)]
    )
    starts = jnp.concatenate([rows_of(image_starts, dp, 1), rows_of(image_starts, other_dp, 1)])
    start_rows = jnp.repeat(starts, seq_len, axis=0)
    inside = (places[:, None] >= start_rows) & (places[:, None] < start_rows + IMG)
    limits = jnp.max(jnp.where(inside, start_rows + (IMG - 1), places[:, None]), axis=1)
    limit_column = limits[:, None]
    place_rows = places.reshape(2, 1, seq_len)
    cosine, sine = rope_tables(places)
    raw_q, raw_k, value, query_turned, key_turned, squares, full_out = project(
        x_all, full_qkv, head_gains, cosine, sine, out_lines, C, 8
    )
    full_out = full_out.reshape(width, width)
    attended = attend(query_turned, key_turned, value, limit_column, place_rows, seq_len)
    attended_own, attn_proj, hidden, h_both = attention_out(
        attended, full_out, tokens, jnp.pad(gain_a, ((0, 7), (0, 0))), C, 2
    )

    h_all = h_both.reshape(2 * seq_len, width)
    full_gate_up, second_down, h_all = lax.optimization_barrier((full_gate_up, second_down, h_all))
    second_down = gather_z_aside(second_down)
    gate_up_low, mixed, turned_units = mix(h_all, full_gate_up)
    output, b_all, term_down, term_gain_ffn = feed_forward(
        mixed, turned_units, gate_up_low, (first_down, second_down), hidden, cotangent,
        jnp.pad(gain_f, ((0, 7), (0, 0))), C, 3,
    )

    term_down, b_all = lax.optimization_barrier((term_down, b_all))
    grad_w_down = scatter_z_aside(term_down)
    grad_hidden = back_scatter(b_all, full_gate_up, cotangent, C, 5)
    term_gate_up = dot(h_all, b_all, 0, 0, BF16)
    term_gate_up, grad_hidden, grad_w_down = lax.optimization_barrier(
        (term_gate_up, grad_hidden, grad_w_down)
    )
    grad_gate_up = scatter_z_aside(term_gate_up)

    attn_unit, attn_factor = row_norm(attn_proj)
    grad_attn, term_gain_attn = row_norm_back(attn_unit, attn_factor, gain_a, grad_hidden)
    a_all = gather_rows(grad_attn.astype(BF16), C, 7).reshape(2 * seq_len, width)
    grad_attended = dot(
        a_all, rows_of(full_out, plane_at * slice_width, slice_width), 1, 1, BF16
    )
    term_out = dot(attended, a_all, 0, 0, BF16)
    grad_q, grad_k, grad_v = attend_back(
        query_turned, key_turned, value, grad_attended, limit_column, place_rows, seq_len
    )
    known = jnp.concatenate(
        [jnp.zeros((2, width), F32), term_gain_attn[None], term_gain_ffn[:1], jnp.zeros((4, width), F32)]
    )
    grad_raw, gain_terms, term_out = project_back(
        grad_q, grad_k, grad_v, raw_q, raw_k, squares, head_gains, cosine, sine, known, term_out,
        C, Z, 9,
    )
    term_qkv = dot(x_all, grad_raw, 0, 0, BF16)
    by_blocks = term_out.reshape(Z, shard, A, slice_width).transpose(0, 2, 1, 3)
    by_blocks = by_blocks.reshape(width, slice_width)
    last = jnp.concatenate([term_qkv, by_blocks], axis=1)
    last, grad_raw, grad_gate_up, gain_terms, output, grad_w_down = lax.optimization_barrier(
        (last, grad_raw, grad_gate_up, gain_terms, output.astype(BF16), grad_w_down.astype(F32))
    )
    last = scatter_z_aside(last)
    if dealt:
        grad_gate_up = return_rows(grad_gate_up, 2 * ffn_slice, C, 2, Z, 10)
        grad_gate_up = grad_gate_up.reshape(2, shard, ffn_width)
    else:
        grad_gate_up = (
            exchange(grad_gate_up)
            .reshape(A, shard, 2, Z, part)
            .transpose(2, 1, 3, 0, 4)
            .reshape(2, shard, ffn_width)
        )
    gain_terms = gain_terms[:4]
    gain_terms = gain_terms + swap(gain_terms, A)
    *grad_gate_up, gain_terms, grad_raw = lax.optimization_barrier(
        (grad_gate_up[0].astype(F32), grad_gate_up[1].astype(F32), gain_terms, grad_raw)
    )
    for power in range(1, Z.bit_length() - 1):
        gain_terms = gain_terms + swap(gain_terms, A << power)
    grad_input = back_scatter(grad_raw, full_qkv, None, C, 6) + grad_hidden
    last, grad_input = lax.optimization_barrier((last, grad_input))
    grad_qkv = return_rows(last, 3 * slice_width, C, 3, 1, 11).reshape(4, shard, width)
    gain_sums = lax.dynamic_slice(gain_terms, (0, own_at * shard), (4, shard))

    return (
        output,
        grad_input,
        grad_qkv[0].astype(F32),
        grad_qkv[1].astype(F32),
        grad_qkv[2].astype(F32),
        grad_qkv[3].astype(F32),
        gain_sums[0],
        gain_sums[1],
        gain_sums[2],
        grad_gate_up[0],
        grad_gate_up[1],
        grad_w_down,
        gain_sums[3],
    )


def solution(mesh):
    split, line, copied = P(AXES, None), P(AXES), P()
    return jax.shard_map(
        functools.partial(layer, mesh.shape["ctx"], mesh.shape["dp"]),
        mesh=mesh,
        in_specs=(split,) * 5 + (line,) * 3 + (split,) * 3 + (line, copied, copied, split),
        out_specs=(split,) * 6 + (line,) * 3 + (split,) * 3 + (line,),
        check_vma=False,
    )
```
